32 devices in a mesh: dp: 2 (over x), seq: 16 (over z, y, core).
Axes of the slice: x: 2, y: 2, z: 4, core: 2. Of those that a mesh axis runs over, the one named last changes fastest.
Arguments:
- tokens: bfloat16 [2, 16, 256, 1024], P('dp', 'seq'), may hold values from -24 to 24
- cotangent: bfloat16 [2, 16, 256, 1024], P('dp', 'seq'), may hold values from -6 to 6
- row_mask: int32 [4, 16, 2, 2], P(None, 'seq'), may hold values from 0 to 1, as said below
- column_mask: int32 [4, 256, 2, 2], P(None, 'seq'), may hold values from 0 to 1, as said below
- w_query: bfloat16 [1024, 512], P('dp'), may hold values from -0.25 to 0.25
- w_key: bfloat16 [1024, 512], P('dp'), may hold values from -0.25 to 0.25
- w_value: bfloat16 [1024, 512], P('dp'), may hold values from -0.1875 to 0.1875
- w_out: bfloat16 [512, 1024], P('dp'), may hold values from -0.25 to 0.25
Outputs:
- mixed: bfloat16 [2, 16, 256, 1024], P('dp', 'seq')
- grad_tokens: bfloat16 [2, 16, 256, 1024], P('dp', 'seq')
- grad_value: float32 [1024, 512], P(('dp', 'seq'))
- grad_output: float32 [512, 1024], P(None, ('dp', 'seq'))
The draws below stay inside these ranges and needn't reach their ends.
Inputs may be any that keep to these rules, and one draw needn't show every extreme that they name: `row_mask`: each block mask is lower triangular with ones on its diagonal. `column_mask`: each block mask is lower triangular with ones on its diagonal.
All inputs are finite; a program needn't handle non-finite values.
Results may differ from the reference program's by a relative error of at most 0.015.
Values may be sent and summed in bfloat16 or wider, within the bound.
A program may use at most 64 MiB of HBM per device.

```python
import math
import jax
import jax.numpy as jnp
from jax import lax

D = 1024
HEADS = 8
HEAD_DIM = 64
GC = 256
ROWBLK = 128
COLBLK = 8
HALF_HEADS = 4
HD = 512
GR = 16
SEQS = 2
NBR = 2
NBC = 2


def shared_projection(key):
    return jax.random.normal(key, (D, HD))


def draw_w_query(key, part):
    common = shared_projection(key)
    return jnp.clip(common * D ** (-0.5), -0.25, 0.25).astype(jnp.bfloat16)


def draw_w_key(key, part):
    key = jax.random.fold_in(key, 22)
    own_part = jax.random.normal(key, (D, HD))
    mixture = own_part
    return jnp.clip(mixture * D ** (-0.5), -0.25, 0.25).astype(jnp.bfloat16)


def random_blocks(key, heads, lines, blocks):
    bits = jax.random.randint(key, (heads, lines, blocks, blocks), 0, 2)
    lower = jnp.arange(blocks)[:, None] > jnp.arange(blocks)[None, :]
    diagonal = jnp.arange(blocks)[:, None] == jnp.arange(blocks)[None, :]
    return jnp.where(lower, bits, 0) + diagonal.astype(jnp.int32)


def draw_row_mask(key, part):
    key = jax.random.fold_in(key, 31)
    return random_blocks(key, HALF_HEADS, GR, NBR).astype(jnp.int32)


def draw_column_mask(key, part):
    key = jax.random.fold_in(key, 32)
    return random_blocks(key, HALF_HEADS, GC, NBC).astype(jnp.int32)


def draw_tokens(key, part):
    key = jax.random.fold_in(key, 11)
    keys = jax.random.split(key, 1)
    shape = (SEQS, GR, GC, D)
    base = jax.random.normal(keys[0], shape)
    return jnp.clip(base, -6.0, 6.0).astype(jnp.bfloat16)


def with_spikes(values, rng, source, target, blocks, factor):
    def block_of(position):
        return (jnp.arange(values.shape[position]) // (values.shape[position] // blocks)).reshape((-1,) + (1,) * (values.ndim - 1 - position))

    near = jax.random.permutation(rng, blocks)[block_of(target)]
    other_side = (block_of(target) + blocks // 2) % blocks
    return jnp.where((block_of(source) == near) | (block_of(source) == other_side), factor * values, values)


def levels(stream_key, shape, shards, least, largest):
    gain = 1.0
    for dim, blocks in shards:
        steps = jax.random.uniform(jax.random.fold_in(jax.random.fold_in(stream_key, 6), dim), (blocks,), jnp.float32, least / len(shards), largest / len(shards))
        gain = gain * jnp.repeat(jnp.exp(steps), shape[dim] // blocks).reshape((-1,) + (1,) * (len(shape) - 1 - dim))
    return gain


def bell_draw(stream_key, dims, deviation, most, shards=(), held_as=jnp.bfloat16):
    drawn = jax.random.normal(stream_key, dims, jnp.float32) * deviation
    if len(shards) > 0:
        drawn = levels(stream_key, dims, shards, -0.22, 0.18) * drawn
    return jnp.clip(drawn, min=-most, max=most).astype(held_as)


def bell_draw_with(stream_key, extent, deviation, reach, cuts, heavy, kind=jnp.bfloat16):
    values = deviation * jax.random.normal(stream_key, extent, jnp.float32)
    if cuts:
        values = values * levels(stream_key, extent, cuts, -0.22, 0.18)
    return jnp.clip(with_spikes(values, jax.random.fold_in(stream_key, 3), *heavy), -reach, reach).astype(kind)


def setup_inputs(seed: int = 0) -> dict:
    arg_keys = jax.random.split(jax.random.key(seed), 9)
    return {
        "tokens": draw_tokens(jax.random.fold_in(arg_keys[8], 71), 0),
        "cotangent": bell_draw_with(arg_keys[1], (SEQS, GR, GC, D), 1.0, 6.0, ((0, 2), (1, 16)), (1, 3, 16, 2.0)),
        "row_mask": draw_row_mask(jax.random.fold_in(arg_keys[8], 71), 0),
        "column_mask": draw_column_mask(jax.random.fold_in(arg_keys[8], 71), 0),
        "w_query": draw_w_query(jax.random.fold_in(arg_keys[8], 71), 0),
        "w_key": draw_w_key(jax.random.fold_in(arg_keys[8], 71), 0),
        "w_value": bell_draw(arg_keys[6], (D, HD), D ** -0.5, 0.1875, ((0, 2),)),
        "w_out": bell_draw(arg_keys[7], (HD, D), HD ** -0.5, 0.25, ((0, 2),)),
    }


row_forms = ('blhe,bmhe->bhlm', 'bhlm,bmhe->blhe')
column_forms = ('lbhe,mbhe->bhlm', 'bhlm,mbhe->lbhe')
contract_last = (((1,), (1,)), ((), ()))
contract_first = (((0,), (0,)), ((), ()))

def allowed_cells(mask_blocks, block_size):
    expanded = jnp.repeat(jnp.repeat(mask_blocks, block_size, axis=-2), block_size, axis=-1)
    length = expanded.shape[-1]
    causal = jnp.arange(length)[:, None] >= jnp.arange(length)[None, :]
    return (expanded == 1) & causal

def attend(queries, key_part, value_part, allowed, forms):
    scale_factor = 1.0 / math.sqrt(queries.shape[-1])
    scores = jnp.einsum(forms[0], queries.astype(jnp.float32), key_part.astype(jnp.float32)) * scale_factor
    scores = jnp.where(allowed, scores, -1e+30)
    highest = lax.stop_gradient(lax.optimization_barrier(jnp.max(scores, axis=-1, keepdims=True)))
    weights = jnp.exp(scores - highest)
    weights = weights / lax.optimization_barrier(jnp.sum(weights, axis=-1, keepdims=True))
    rounded = lax.optimization_barrier(weights.astype(jnp.bfloat16)).astype(jnp.float32)
    result = jnp.einsum(forms[1], rounded, value_part.astype(jnp.float32))
    return result.astype(jnp.bfloat16)

def layer(sequence, cot_seq, row_mask, column_mask, w_query, w_key, w_value, w_out):
    grid_rows, grid_cols, width = sequence.shape
    flat = sequence.reshape(-1, width)
    cot_flat = cot_seq.reshape(-1, width)
    half = HEADS // 2

    def project(weight):
        product = jnp.dot(flat, weight, preferred_element_type=jnp.float32).astype(jnp.bfloat16)
        return product.reshape(grid_rows, grid_cols, HEADS, HEAD_DIM)
    row_allowed = allowed_cells(jnp.transpose(row_mask, (1, 0, 2, 3)), ROWBLK)
    column_allowed = allowed_cells(jnp.transpose(column_mask, (1, 0, 2, 3)), COLBLK)

    def core(query_all, key_all, value_all):
        row_out = attend(query_all[:, :, :half], key_all[:, :, :half], value_all[:, :, :half], row_allowed, row_forms)
        column_out = attend(query_all[:, :, half:], key_all[:, :, half:], value_all[:, :, half:], column_allowed, column_forms)
        return jnp.concatenate([row_out, column_out], axis=2)
    heads_out, core_back = jax.vjp(core, project(w_query), project(w_key), project(w_value))
    attended = heads_out.reshape(-1, HD)
    mixed = jnp.dot(attended, w_out, preferred_element_type=jnp.float32).astype(jnp.bfloat16)
    grad_heads = lax.dot_general(cot_flat, w_out, contract_last, preferred_element_type=jnp.float32).astype(jnp.bfloat16)
    grads = core_back(grad_heads.reshape(grid_rows, grid_cols, HEADS, HEAD_DIM))

    def back(grad, weight):
        return lax.dot_general(grad.reshape(-1, HD), weight, contract_last, preferred_element_type=jnp.float32)
    grad_tokens = (back(grads[0], w_query) + back(grads[1], w_key) + back(grads[2], w_value)).astype(jnp.bfloat16)
    value_term = lax.dot_general(flat, grads[2].reshape(-1, HD), contract_first, preferred_element_type=jnp.float32)
    out_term = lax.dot_general(attended, cot_flat, contract_first, preferred_element_type=jnp.float32)
    return (mixed.reshape(sequence.shape), grad_tokens.reshape(sequence.shape), value_term, out_term)

def reference(tokens, cotangent, row_mask, column_mask, w_query, w_key, w_value, w_out):

    def step(carry, pair):
        mixed, grad_tokens, value_term, out_term = layer(pair[0], pair[1], row_mask, column_mask, w_query, w_key, w_value, w_out)
        return ((carry[0] + value_term, carry[1] + out_term), (mixed, grad_tokens))
    start = (jnp.zeros((D, HD), jnp.float32), jnp.zeros((HD, D), jnp.float32))
    totals, stacked = lax.scan(step, start, (tokens, cotangent))
    return (stacked[0], stacked[1], totals[0], totals[1])
```

```python
import math

import jax
import jax.numpy as jnp
from jax import lax
from jax.experimental import pallas as pl
from jax.experimental.pallas import tpu as pltpu
from jax.sharding import PartitionSpec as P

HEAD_DIM = 64
ROWBLK = 128
COLBLK = 8


row_forms = ("blhe,bmhe->bhlm", "bhlm,bmhe->blhe")
column_forms = ("lbhe,mbhe->bhlm", "bhlm,mbhe->lbhe")
contract_last = (((1,), (1,)), ((), ()))
contract_first = (((0,), (0,)), ((), ()))


def allowed_cells(mask_blocks, block_size):
    expanded = jnp.repeat(jnp.repeat(mask_blocks, block_size, axis=-2), block_size, axis=-1)
    length = expanded.shape[-1]
    causal = jnp.arange(length)[:, None] >= jnp.arange(length)[None, :]
    return (expanded == 1) & causal


def attend(queries, key_part, value_part, allowed, forms):
    scale_factor = 1.0 / math.sqrt(queries.shape[-1])
    scores = (
        jnp.einsum(forms[0], queries.astype(jnp.float32), key_part.astype(jnp.float32))
        * scale_factor
    )
    scores = jnp.where(allowed, scores, -1e30)
    highest = lax.stop_gradient(jnp.max(scores, axis=-1, keepdims=True))
    weights = jnp.exp(scores - highest)
    weights = weights / jnp.sum(weights, axis=-1, keepdims=True)
    rounded = lax.optimization_barrier(weights.astype(jnp.bfloat16)).astype(jnp.float32)
    result = jnp.einsum(forms[1], rounded, value_part.astype(jnp.float32))
    return result.astype(jnp.bfloat16)


def body(tokens, cotangent, row_mask, column_mask, w_query, w_key, w_value, w_out):
    rows_here = tokens.shape[1]
    grid_cols = tokens.shape[2]
    width = tokens.shape[3]
    heads_width = w_query.shape[1]
    half = heads_width // HEAD_DIM // 2
    split = half * HEAD_DIM
    flat = tokens.reshape(-1, width)
    cot_flat = cotangent.reshape(-1, width)
    token_count = flat.shape[0]
    seq_count = lax.axis_size("seq")
    grid_rows = rows_here * seq_count
    cols_here = grid_cols // seq_count
    full_query, full_key, full_value, full_out = (
        lax.all_gather(w_query, "dp", axis=0, tiled=True),
        lax.all_gather(w_key, "dp", axis=0, tiled=True),
        lax.all_gather(w_value, "dp", axis=0, tiled=True),
        lax.all_gather(w_out, "dp", axis=0, tiled=True),
    )
    proj_query = jnp.dot(flat, full_query, preferred_element_type=jnp.float32)
    proj_key = jnp.dot(flat, full_key, preferred_element_type=jnp.float32)
    proj_value = jnp.dot(flat, full_value, preferred_element_type=jnp.float32)
    query_flat = proj_query.astype(jnp.bfloat16)
    key_flat = proj_key.astype(jnp.bfloat16)
    value_flat = proj_value.astype(jnp.bfloat16)
    row_allowed = allowed_cells(jnp.transpose(row_mask, (1, 0, 2, 3)), ROWBLK)
    column_allowed = allowed_cells(jnp.transpose(column_mask, (1, 0, 2, 3)), COLBLK)

    def row_core(first, second, third):
        return attend(first, second, third, row_allowed, row_forms)

    def column_core(first, second, third):
        return attend(first, second, third, column_allowed, column_forms)

    def row_heads(matrix):
        return matrix[:, :split].reshape(rows_here, grid_cols, half, HEAD_DIM)

    def column_heads(matrix):
        return matrix[:, split:].reshape(rows_here, grid_cols, split)

    def as_columns(block):
        return block.reshape(grid_rows, cols_here, half, HEAD_DIM)

    def joined(row_part, col_part):
        return jnp.concatenate(
            [row_part.reshape(token_count, split), col_part.reshape(token_count, split)], axis=1
        )

    col_query, col_key, col_value = (
        lax.all_to_all(column_heads(query_flat), "seq", split_axis=1, concat_axis=0, tiled=True),
        lax.all_to_all(column_heads(key_flat), "seq", split_axis=1, concat_axis=0, tiled=True),
        lax.all_to_all(column_heads(value_flat), "seq", split_axis=1, concat_axis=0, tiled=True),
    )
    row_out, row_back = jax.vjp(
        row_core, row_heads(query_flat), row_heads(key_flat), row_heads(value_flat)
    )
    column_out, column_back = jax.vjp(
        column_core, as_columns(col_query), as_columns(col_key), as_columns(col_value)
    )
    returned = lax.all_to_all(
        column_out.reshape(grid_rows, cols_here, split),
        "seq",
        split_axis=0,
        concat_axis=1,
        tiled=True,
    )
    attended = joined(row_out, returned)
    mixed = jnp.dot(attended, full_out, preferred_element_type=jnp.float32)
    grad_heads = lax.dot_general(
        cot_flat, full_out, contract_last, preferred_element_type=jnp.float32
    )
    mixed = mixed.astype(jnp.bfloat16).reshape(tokens.shape)
    grad_heads = grad_heads.astype(jnp.bfloat16)
    row_grads = row_back(grad_heads[:, :split].reshape(rows_here, grid_cols, half, HEAD_DIM))
    grad_columns = lax.all_to_all(
        grad_heads[:, split:].reshape(rows_here, grid_cols, split),
        "seq",
        split_axis=1,
        concat_axis=0,
        tiled=True,
    )
    col_grads = column_back(as_columns(grad_columns))
    back_grads = (
        lax.all_to_all(
            col_grads[0].reshape(grid_rows, cols_here, split),
            "seq",
            split_axis=0,
            concat_axis=1,
            tiled=True,
        ),
        lax.all_to_all(
            col_grads[1].reshape(grid_rows, cols_here, split),
            "seq",
            split_axis=0,
            concat_axis=1,
            tiled=True,
        ),
        lax.all_to_all(
            col_grads[2].reshape(grid_rows, cols_here, split),
            "seq",
            split_axis=0,
            concat_axis=1,
            tiled=True,
        ),
    )
    grad_query = joined(row_grads[0], back_grads[0])
    grad_key = joined(row_grads[1], back_grads[1])
    grad_val = joined(row_grads[2], back_grads[2])
    grad_tokens = (
        lax.dot_general(grad_query, full_query, contract_last, preferred_element_type=jnp.float32)
        + lax.dot_general(grad_key, full_key, contract_last, preferred_element_type=jnp.float32)
        + lax.dot_general(grad_val, full_value, contract_last, preferred_element_type=jnp.float32)
    )
    grad_tokens = grad_tokens.astype(jnp.bfloat16).reshape(tokens.shape)
    summed = lax.psum_scatter(
        jnp.concatenate(
            [
                lax.dot_general(flat, grad_val, contract_first, preferred_element_type=jnp.float32),
                lax.dot_general(
                    cot_flat, attended, contract_first, preferred_element_type=jnp.float32
                ),
            ],
            axis=1,
        ),
        ("dp", "seq"),
        scatter_dimension=0,
        tiled=True,
    )
    grad_value = summed[:, :heads_width]
    grad_output = jnp.transpose(summed[:, heads_width:])
    return (mixed, grad_tokens, grad_value, grad_output)


MESH = pl.DeviceIdType.MESH
F32 = jnp.float32
BF16 = jnp.bfloat16


def dot_nn(a, b):
    return jnp.dot(a, b, preferred_element_type=F32)


def dot_nt(a, b):
    return lax.dot_general(a, b, contract_last, preferred_element_type=F32)


def dot_tn(a, b):
    return lax.dot_general(a, b, contract_first, preferred_element_type=F32)


def fused_kernel(
    dp_count,
    seq_count,
    tokens_ref,
    cot_ref,
    bits_ref,
    wq_ref,
    wk_ref,
    wv_ref,
    wo_ref,
    mixed_ref,
    gtok_ref,
    gval_ref,
    gout_ref,
    w_full,
    wo_full,
    qkv_send,
    qkv_recv,
    g_rows,
    g_send,
    g_recv,
    out_send,
    out_recv,
    grad_send,
    grad_recv,
    row_grads,
    probs,
    attended,
    part,
    part_recv1,
    acc1,
    part_recv2,
    acc2,
    part_recv3,
    acc3,
    part_recv4,
    w_send_sem,
    w_recv_sem,
    a_send_sem,
    a_recv_sem,
    r_send_sem,
    r_recv_sem,
):
    dp = lax.axis_index("dp")
    seq = lax.axis_index("seq")
    core = lax.rem(seq, 2)
    y = lax.rem(seq // 2, 2)
    z = seq // 4
    z_count = seq_count // 4
    positions = tokens_ref.shape[0]
    cols = positions // seq_count
    shard = wq_ref.shape[0]
    out_shard = wo_ref.shape[0]
    split = qkv_send.shape[2]
    other = 1 - dp
    x_peer = (other, seq)
    core_peer = (dp, seq + 1 - 2 * core)
    y_peer = (dp, seq + 2 - 4 * y)

    barrier = pltpu.get_barrier_semaphore()
    pl.semaphore_signal(barrier, inc=1, device_id=x_peer, device_id_type=MESH)

    @pl.loop(1, seq_count)
    def _(step):
        pl.semaphore_signal(
            barrier,
            inc=1,
            device_id=(dp, lax.rem(seq + step, seq_count)),
            device_id_type=MESH,
        )

    own_rows = pl.ds(pl.multiple_of(dp * shard, shard), shard)
    w_full[0, own_rows, :] = wq_ref[...]
    w_full[1, own_rows, :] = wk_ref[...]
    w_full[2, own_rows, :] = wv_ref[...]
    own_out = pl.ds(pl.multiple_of(dp * out_shard, out_shard), out_shard)
    wo_full[own_out, :] = wo_ref[...]
    pl.semaphore_wait(barrier, seq_count)

    def region(group, owner, qy, qc):
        if group == 1:
            quarter = out_shard // 4
            start = pl.multiple_of(owner * out_shard + (qy * 2 + qc) * quarter, quarter)
            return wo_full.at[pl.ds(start, quarter), :]
        quarter = shard // 4
        start = pl.multiple_of(owner * shard + (qy * 2 + qc) * quarter, quarter)
        lanes = pl.ds(split if group == 0 else 0, split)
        return w_full.at[:, pl.ds(start, quarter), lanes]

    def weight_copy(group, hop):
        if hop == 0:
            ref, peer = region(group, dp, y, core), x_peer
        elif hop == 1:
            ref, peer = region(group, other, y, core), y_peer
        elif hop == 2:
            ref, peer = region(group, other, y, core), core_peer
        else:
            ref, peer = region(group, other, 1 - y, core), core_peer
        return pltpu.make_async_remote_copy(
            src_ref=ref,
            dst_ref=ref,
            send_sem=w_send_sem.at[group, hop],
            recv_sem=w_recv_sem.at[group, hop],
            device_id=peer,
            device_id_type=MESH,
        )

    def share_weights(group):
        weight_copy(group, 0).wait_recv()
        if group < 2:
            weight_copy(group + 1, 0).start()
        weight_copy(group, 1).start()
        weight_copy(group, 2).start()
        weight_copy(group, 1).wait_recv()
        weight_copy(group, 3).start()
        weight_copy(group, 2).wait_recv()
        weight_copy(group, 3).wait_recv()

    def column_copy(src, dst, phase, step):
        target = lax.rem(seq + step, seq_count)
        there = pl.ds(pl.multiple_of(target * cols, cols), cols)
        here = pl.ds(pl.multiple_of(seq * cols, cols), cols)
        return pltpu.make_async_remote_copy(
            src_ref=src.at[:, there, :],
            dst_ref=dst.at[:, here, :],
            send_sem=a_send_sem.at[phase, step],
            recv_sem=a_recv_sem.at[phase, step],
            device_id=(dp, target),
            device_id_type=MESH,
        )

    def exchange(src, dst, phase):
        @pl.loop(1, seq_count)
        def _(step):
            column_copy(src, dst, phase, step).start()

        here = pl.ds(pl.multiple_of(seq * cols, cols), cols)
        dst[:, here, :] = src[:, here, :]

    def arrived(src, dst, phase):
        @pl.loop(1, seq_count)
        def _(step):
            column_copy(src, dst, phase, step).wait_recv()

    def sent(src, dst, phase):
        @pl.loop(1, seq_count)
        def _(step):
            column_copy(src, dst, phase, step).wait_send()

    weight_copy(0, 0).start()

    query_pos = lax.broadcasted_iota(jnp.int32, (positions, positions), 0)
    key_pos = lax.broadcasted_iota(jnp.int32, (positions, positions), 1)
    lane = lax.broadcasted_iota(jnp.int32, (1, 2 * HEAD_DIM), 1)
    first_lanes = lane < HEAD_DIM
    keep = (first_lanes.astype(F32).astype(BF16), (lane >= HEAD_DIM).astype(F32).astype(BF16))

    def row_sight():
        same = (query_pos // ROWBLK) == (key_pos // ROWBLK)
        return same, key_pos <= query_pos

    def column_sight():
        row, row2 = query_pos // cols, key_pos // cols
        same = (row // COLBLK) == (row2 // COLBLK)
        matching = lax.rem(query_pos, cols) == lax.rem(key_pos, cols)
        return same, matching & (row2 <= row)

    def softmax(head, query, key, sight):
        bit = bits_ref[head : head + 1, :]
        same, causal = sight
        visible = causal & (same | (bit > 0))
        scores = dot_nt(query, key) * (1.0 / math.sqrt(HEAD_DIM))
        scores = jnp.where(visible, scores, -1e30)
        weights = jnp.exp(scores - jnp.max(scores, axis=-1, keepdims=True))
        return weights / jnp.sum(weights, axis=-1, keepdims=True)

    def pair_of(pair):
        return pl.ds(pair * 2 * HEAD_DIM, 2 * HEAD_DIM)

    def merge(halves):
        return jnp.where(first_lanes, halves[0], halves[1]).astype(BF16)

    def forward(base, query, key, value, sight, slot):
        outs = []
        for side in range(2):
            weights = softmax(base + side, query * keep[side], key, sight)
            probs[slot + side] = weights
            outs.append(dot_nn(weights.astype(BF16), value))
        return merge(outs)

    def backward(query, key, value, grad, slot):
        grads = ([], [], [])
        for side in range(2):
            weights = probs[slot + side]
            grad_side = grad * keep[side]
            grad_probs = dot_nt(grad_side, value)
            grad_scores = weights * (
                grad_probs - jnp.sum(weights * grad_probs, axis=-1, keepdims=True)
            )
            grad_scores = (grad_scores * (1.0 / math.sqrt(HEAD_DIM))).astype(BF16)
            grads[0].append(dot_nn(grad_scores, key))
            grads[1].append(dot_tn(grad_scores, query))
            grads[2].append(dot_tn(weights.astype(BF16), grad))
        return [merge(grad_pair) for grad_pair in grads]

    def rs_copy(which, hop):
        if hop == 0:
            src, dst, peer = part.at[which, :, :, 1 - core], part_recv1.at[which], core_peer
        elif hop == 1:
            src, dst, peer = acc1.at[which, other], part_recv2.at[which], x_peer
        elif hop == 2:
            src, dst, peer = acc2.at[which, :, 1 - y], part_recv3.at[which], y_peer
        else:
            z_there = lax.rem(z + hop - 2, z_count)
            src, dst = acc3.at[which, z_there], part_recv4.at[which, hop - 3]
            peer = (dp, z_there * 4 + y * 2 + core)
        return pltpu.make_async_remote_copy(
            src_ref=src,
            dst_ref=dst,
            send_sem=r_send_sem.at[which, hop],
            recv_sem=r_recv_sem.at[which, hop],
            device_id=peer,
            device_id_type=MESH,
        )

    def rs_start(which, full):
        part[which] = full.astype(BF16).reshape(part.shape[1:])
        rs_copy(which, 0).start()

    def rs_next(which, hop):
        rs_copy(which, hop).wait_recv()
        if hop == 0:
            acc1[which] = (
                part[which, :, :, core].astype(F32) + part_recv1[which].astype(F32)
            ).astype(BF16)
            rs_copy(which, 1).start()
        elif hop == 1:
            total = acc1[which, dp].astype(F32) + part_recv2[which].astype(F32)
            acc2[which] = total.astype(BF16).reshape(acc2.shape[1:])
            rs_copy(which, 2).start()
        else:
            acc3[which] = (
                acc2[which, :, y].astype(F32) + part_recv3[which].astype(F32)
            ).astype(BF16)
            for step in range(1, z_count):
                rs_copy(which, 2 + step).start()

    def rs_end(which):
        total = acc3[which, z].astype(F32)
        for step in range(1, z_count):
            rs_copy(which, 2 + step).wait_recv()
            total = total + part_recv4[which, step - 1].astype(F32)
        return total

    share_weights(0)
    for index in range(3):
        qkv_send[index] = dot_nn(tokens_ref[...], w_full[index, :, split:]).astype(BF16)
    exchange(qkv_send, qkv_recv, 0)

    share_weights(1)
    g_send[0] = dot_nt(cot_ref[...], wo_full[split:, :]).astype(BF16)
    exchange(g_send, g_recv, 1)
    g_rows[...] = dot_nt(cot_ref[...], wo_full[:split, :]).astype(BF16)

    share_weights(2)
    row_qkv = [dot_nn(tokens_ref[...], w_full[index, :, :split]).astype(BF16) for index in range(3)]
    sight = row_sight()
    for pair in range(split // (2 * HEAD_DIM)):
        lanes = slice(pair * 2 * HEAD_DIM, (pair + 1) * 2 * HEAD_DIM)
        query, key, value = (item[:, lanes] for item in row_qkv)
        attended[:, pair_of(pair)] = forward(2 * pair, query, key, value, sight, 0)
        grads = backward(query, key, value, g_rows[:, pair_of(pair)], 0)
        for index in range(3):
            row_grads[index, :, pair_of(pair)] = grads[index]

    arrived(qkv_send, qkv_recv, 0)
    half = split // HEAD_DIM
    sight = column_sight()
    for pair in range(split // (2 * HEAD_DIM)):
        query, key, value = (qkv_recv[index, :, pair_of(pair)] for index in range(3))
        out_send[0, :, pair_of(pair)] = forward(
            half + 2 * pair, query, key, value, sight, 2 * pair
        )
    exchange(out_send, out_recv, 2)

    arrived(g_send, g_recv, 1)
    for pair in range(split // (2 * HEAD_DIM)):
        query, key, value = (qkv_recv[index, :, pair_of(pair)] for index in range(3))
        grads = backward(query, key, value, g_recv[0, :, pair_of(pair)], 2 * pair)
        for index in range(3):
            grad_send[index, :, pair_of(pair)] = grads[index]
    exchange(grad_send, grad_recv, 3)

    arrived(out_send, out_recv, 2)
    attended[:, pl.ds(split, split)] = out_recv[0]
    rs_start(0, dot_tn(cot_ref[...], attended[...]))
    mixed_ref[...] = dot_nn(attended[...], wo_full[...]).astype(BF16)
    rs_next(0, 0)
    row_part = (
        dot_nt(row_grads[0], w_full[0, :, :split])
        + dot_nt(row_grads[1], w_full[1, :, :split])
        + dot_nt(row_grads[2], w_full[2, :, :split])
    )
    part_value_rows = dot_tn(tokens_ref[...], row_grads[2])
    rs_next(0, 1)

    arrived(grad_send, grad_recv, 3)
    part_value_cols = dot_tn(tokens_ref[...], grad_recv[2])
    rs_start(1, jnp.concatenate([part_value_rows, part_value_cols], axis=1))
    rs_next(0, 2)
    rs_next(1, 0)
    gtok_ref[...] = (
        row_part
        + dot_nt(grad_recv[0], w_full[0, :, split:])
        + dot_nt(grad_recv[1], w_full[1, :, split:])
        + dot_nt(grad_recv[2], w_full[2, :, split:])
    ).astype(BF16)
    gout_ref[...] = rs_end(0).T
    rs_next(1, 1)
    rs_next(1, 2)
    gval_ref[...] = rs_end(1)

    for group in range(3):
        for hop in range(4):
            weight_copy(group, hop).wait_send()
    sent(qkv_send, qkv_recv, 0)
    sent(g_send, g_recv, 1)
    sent(out_send, out_recv, 2)
    sent(grad_send, grad_recv, 3)
    for which in range(2):
        for hop in range(2 + z_count):
            rs_copy(which, hop).wait_send()


def fused_fits(dp_count, seq_count, tokens, row_mask, column_mask, w_query, w_out):
    positions = tokens.shape[1] * tokens.shape[2]
    return (
        tokens.shape[0] == 1
        and tokens.shape[1] == 1
        and dp_count == 2
        and seq_count % 4 == 0
        and positions % (16 * seq_count) == 0
        and w_query.shape[0] % 64 == 0
        and w_out.shape[0] % 64 == 0
        and tokens.shape[3] % (16 * dp_count * seq_count) == 0
        and row_mask.shape[2] == 2
        and column_mask.shape[2] == 2
    )


def fused_body(tokens, cotangent, row_mask, column_mask, w_query, w_key, w_value, w_out):
    dp_count, seq_count = lax.axis_size("dp"), lax.axis_size("seq")
    if not fused_fits(dp_count, seq_count, tokens, row_mask, column_mask, w_query, w_out):
        return body(
            tokens, cotangent, row_mask, column_mask, w_query, w_key, w_value, w_out
        )
    positions, width = tokens.shape[1] * tokens.shape[2], tokens.shape[3]
    heads_width = w_query.shape[1]
    split = heads_width // 2
    rows = width // (dp_count * seq_count)
    z_count = seq_count // 4
    bits = jnp.concatenate(
        [
            jnp.broadcast_to(row_mask[:, 0, 1, 0][:, None], (row_mask.shape[0], positions)),
            jnp.tile(column_mask[:, :, 1, 0], (1, seq_count)),
        ],
        axis=0,
    ).astype(F32)
    lead = (2, dp_count, seq_count // 2)
    call = pl.pallas_call(
        lambda *refs: fused_kernel(dp_count, seq_count, *refs),
        out_shape=(
            jax.ShapeDtypeStruct((positions, width), BF16),
            jax.ShapeDtypeStruct((positions, width), BF16),
            jax.ShapeDtypeStruct((rows, heads_width), F32),
            jax.ShapeDtypeStruct((heads_width, rows), F32),
        ),
        in_specs=[pl.BlockSpec(memory_space=pltpu.VMEM)] * 7,
        out_specs=[pl.BlockSpec(memory_space=pltpu.VMEM)] * 4,
        scratch_shapes=[
            pltpu.VMEM((3, width, heads_width), BF16),
            pltpu.VMEM((heads_width, width), BF16),
            pltpu.VMEM((3, positions, split), BF16),
            pltpu.VMEM((3, positions, split), BF16),
            pltpu.VMEM((positions, split), BF16),
            pltpu.VMEM((1, positions, split), BF16),
            pltpu.VMEM((1, positions, split), BF16),
            pltpu.VMEM((1, positions, split), BF16),
            pltpu.VMEM((1, positions, split), BF16),
            pltpu.VMEM((3, positions, split), BF16),
            pltpu.VMEM((3, positions, split), BF16),
            pltpu.VMEM((3, positions, split), BF16),
            pltpu.VMEM((split // HEAD_DIM, positions, positions), F32),
            pltpu.VMEM((positions, heads_width), BF16),
            pltpu.VMEM(lead + (2, rows, heads_width), BF16),
            pltpu.VMEM(lead + (rows, heads_width), BF16),
            pltpu.VMEM(lead + (rows, heads_width), BF16),
            pltpu.VMEM((2, seq_count // 2, rows, heads_width), BF16),
            pltpu.VMEM((2, z_count, 2, rows, heads_width), BF16),
            pltpu.VMEM((2, z_count, rows, heads_width), BF16),
            pltpu.VMEM((2, z_count, rows, heads_width), BF16),
            pltpu.VMEM((2, z_count - 1, rows, heads_width), BF16),
            pltpu.SemaphoreType.DMA((3, 4)),
            pltpu.SemaphoreType.DMA((3, 4)),
            pltpu.SemaphoreType.DMA((4, seq_count)),
            pltpu.SemaphoreType.DMA((4, seq_count)),
            pltpu.SemaphoreType.DMA((2, 2 + z_count)),
            pltpu.SemaphoreType.DMA((2, 2 + z_count)),
        ],
        compiler_params=pltpu.CompilerParams(
            collective_id=0, has_side_effects=True, vmem_limit_bytes=48 * 1024 * 1024
        ),
        cost_estimate=pl.CostEstimate(
            flops=3_400_000_000, bytes_accessed=8_000_000, transcendentals=524288
        ),
    )
    mixed, grad_tokens, grad_value, grad_output = call(
        tokens.reshape(positions, width),
        cotangent.reshape(positions, width),
        bits,
        w_query,
        w_key,
        w_value,
        w_out,
    )
    return (
        mixed.reshape(tokens.shape),
        grad_tokens.reshape(tokens.shape),
        grad_value,
        grad_output,
    )


def solution(mesh):
    return jax.shard_map(
        fused_body,
        mesh=mesh,
        in_specs=(
            P("dp", "seq", None, None),
            P("dp", "seq", None, None),
            P(None, "seq", None, None),
            P(None, "seq", None, None),
            P("dp", None),
            P("dp", None),
            P("dp", None),
            P("dp", None),
        ),
        out_specs=(
            P("dp", "seq", None, None),
            P("dp", "seq", None, None),
            P(("dp", "seq"), None),
            P(None, ("dp", "seq")),
        ),
        check_vma=False,
    )
```

```python
import math

import jax
import jax.numpy as jnp
from jax import lax
from jax.experimental import pallas as pl
from jax.experimental.pallas import tpu as pltpu
from jax.sharding import PartitionSpec as P

HEAD_DIM = 64
ROWBLK = 128
COLBLK = 8


row_forms = ("blhe,bmhe->bhlm", "bhlm,bmhe->blhe")
column_forms = ("lbhe,mbhe->bhlm", "bhlm,mbhe->lbhe")
contract_last = (((1,), (1,)), ((), ()))
contract_first = (((0,), (0,)), ((), ()))


def allowed_cells(mask_blocks, block_size):
    expanded = jnp.repeat(jnp.repeat(mask_blocks, block_size, axis=-2), block_size, axis=-1)
    length = expanded.shape[-1]
    causal = jnp.arange(length)[:, None] >= jnp.arange(length)[None, :]
    return (expanded == 1) & causal


def attend(queries, key_part, value_part, allowed, forms):
    scale_factor = 1.0 / math.sqrt(queries.shape[-1])
    scores = (
        jnp.einsum(forms[0], queries.astype(jnp.float32), key_part.astype(jnp.float32))
        * scale_factor
    )
    scores = jnp.where(allowed, scores, -1e30)
    highest = lax.stop_gradient(jnp.max(scores, axis=-1, keepdims=True))
    weights = jnp.exp(scores - highest)
    weights = weights / jnp.sum(weights, axis=-1, keepdims=True)
    rounded = lax.optimization_barrier(weights.astype(jnp.bfloat16)).astype(jnp.float32)
    result = jnp.einsum(forms[1], rounded, value_part.astype(jnp.float32))
    return result.astype(jnp.bfloat16)


def body(tokens, cotangent, row_mask, column_mask, w_query, w_key, w_value, w_out):
    rows_here = tokens.shape[1]
    grid_cols = tokens.shape[2]
    width = tokens.shape[3]
    heads_width = w_query.shape[1]
    half = heads_width // HEAD_DIM // 2
    split = half * HEAD_DIM
    flat = tokens.reshape(-1, width)
    cot_flat = cotangent.reshape(-1, width)
    token_count = flat.shape[0]
    seq_count = lax.axis_size("seq")
    grid_rows = rows_here * seq_count
    cols_here = grid_cols // seq_count
    full_query, full_key, full_value, full_out = (
        lax.all_gather(w_query, "dp", axis=0, tiled=True),
        lax.all_gather(w_key, "dp", axis=0, tiled=True),
        lax.all_gather(w_value, "dp", axis=0, tiled=True),
        lax.all_gather(w_out, "dp", axis=0, tiled=True),
    )
    proj_query = jnp.dot(flat, full_query, preferred_element_type=jnp.float32)
    proj_key = jnp.dot(flat, full_key, preferred_element_type=jnp.float32)
    proj_value = jnp.dot(flat, full_value, preferred_element_type=jnp.float32)
    query_flat = proj_query.astype(jnp.bfloat16)
    key_flat = proj_key.astype(jnp.bfloat16)
    value_flat = proj_value.astype(jnp.bfloat16)
    row_allowed = allowed_cells(jnp.transpose(row_mask, (1, 0, 2, 3)), ROWBLK)
    column_allowed = allowed_cells(jnp.transpose(column_mask, (1, 0, 2, 3)), COLBLK)

    def row_core(first, second, third):
        return attend(first, second, third, row_allowed, row_forms)

    def column_core(first, second, third):
        return attend(first, second, third, column_allowed, column_forms)

    def row_heads(matrix):
        return matrix[:, :split].reshape(rows_here, grid_cols, half, HEAD_DIM)

    def column_heads(matrix):
        return matrix[:, split:].reshape(rows_here, grid_cols, split)

    def as_columns(block):
        return block.reshape(grid_rows, cols_here, half, HEAD_DIM)

    def joined(row_part, col_part):
        return jnp.concatenate(
            [row_part.reshape(token_count, split), col_part.reshape(token_count, split)], axis=1
        )

    col_query, col_key, col_value = (
        lax.all_to_all(column_heads(query_flat), "seq", split_axis=1, concat_axis=0, tiled=True),
        lax.all_to_all(column_heads(key_flat), "seq", split_axis=1, concat_axis=0, tiled=True),
        lax.all_to_all(column_heads(value_flat), "seq", split_axis=1, concat_axis=0, tiled=True),
    )
    row_out, row_back = jax.vjp(
        row_core, row_heads(query_flat), row_heads(key_flat), row_heads(value_flat)
    )
    column_out, column_back = jax.vjp(
        column_core, as_columns(col_query), as_columns(col_key), as_columns(col_value)
    )
    returned = lax.all_to_all(
        column_out.reshape(grid_rows, cols_here, split),
        "seq",
        split_axis=0,
        concat_axis=1,
        tiled=True,
    )
    attended = joined(row_out, returned)
    mixed = jnp.dot(attended, full_out, preferred_element_type=jnp.float32)
    grad_heads = lax.dot_general(
        cot_flat, full_out, contract_last, preferred_element_type=jnp.float32
    )
    mixed = mixed.astype(jnp.bfloat16).reshape(tokens.shape)
    grad_heads = grad_heads.astype(jnp.bfloat16)
    row_grads = row_back(grad_heads[:, :split].reshape(rows_here, grid_cols, half, HEAD_DIM))
    grad_columns = lax.all_to_all(
        grad_heads[:, split:].reshape(rows_here, grid_cols, split),
        "seq",
        split_axis=1,
        concat_axis=0,
        tiled=True,
    )
    col_grads = column_back(as_columns(grad_columns))
    back_grads = (
        lax.all_to_all(
            col_grads[0].reshape(grid_rows, cols_here, split),
            "seq",
            split_axis=0,
            concat_axis=1,
            tiled=True,
        ),
        lax.all_to_all(
            col_grads[1].reshape(grid_rows, cols_here, split),
            "seq",
            split_axis=0,
            concat_axis=1,
            tiled=True,
        ),
        lax.all_to_all(
            col_grads[2].reshape(grid_rows, cols_here, split),
            "seq",
            split_axis=0,
            concat_axis=1,
            tiled=True,
        ),
    )
    grad_query = joined(row_grads[0], back_grads[0])
    grad_key = joined(row_grads[1], back_grads[1])
    grad_val = joined(row_grads[2], back_grads[2])
    grad_tokens = (
        lax.dot_general(grad_query, full_query, contract_last, preferred_element_type=jnp.float32)
        + lax.dot_general(grad_key, full_key, contract_last, preferred_element_type=jnp.float32)
        + lax.dot_general(grad_val, full_value, contract_last, preferred_element_type=jnp.float32)
    )
    grad_tokens = grad_tokens.astype(jnp.bfloat16).reshape(tokens.shape)
    summed = lax.psum_scatter(
        jnp.concatenate(
            [
                lax.dot_general(flat, grad_val, contract_first, preferred_element_type=jnp.float32),
                lax.dot_general(
                    cot_flat, attended, contract_first, preferred_element_type=jnp.float32
                ),
            ],
            axis=1,
        ),
        ("dp", "seq"),
        scatter_dimension=0,
        tiled=True,
    )
    grad_value = summed[:, :heads_width]
    grad_output = jnp.transpose(summed[:, heads_width:])
    return (mixed, grad_tokens, grad_value, grad_output)


MESH = pl.DeviceIdType.MESH
F32 = jnp.float32
BF16 = jnp.bfloat16


def dot_nn(a, b):
    return jnp.dot(a, b, preferred_element_type=F32)


def dot_nt(a, b):
    return lax.dot_general(a, b, contract_last, preferred_element_type=F32)


def dot_tn(a, b):
    return lax.dot_general(a, b, contract_first, preferred_element_type=F32)


def fused_kernel(
    dp_count,
    seq_count,
    tokens_hbm,
    cot_hbm,
    row_mask_hbm,
    column_mask_hbm,
    wq_hbm,
    wk_hbm,
    wv_hbm,
    wo_hbm,
    mixed_hbm,
    gtok_hbm,
    gval_hbm,
    gout_hbm,
    tokens_ref,
    cot_ref,
    tokens_t,
    cot_t,
    row_mask_ref,
    column_mask_ref,
    bias,
    mixed_ref,
    gtok_ref,
    gval_ref,
    gout_ref,
    gtok_part,
    w_full,
    wo_full,
    qkv_send,
    qkv_recv,
    g_rows,
    g_send,
    g_recv,
    out_send,
    out_recv,
    grad_send,
    grad_recv,
    row_grads,
    probs,
    attended,
    part,
    part_recv1,
    acc1,
    part_recv2,
    acc2,
    part_recv3,
    acc3,
    part_recv4,
    w_send_sem,
    w_recv_sem,
    a_send_sem,
    a_recv_sem,
    r_send_sem,
    r_recv_sem,
    local_sem,
):
    dp = lax.axis_index("dp")
    seq = lax.axis_index("seq")
    core = lax.rem(seq, 2)
    y = lax.rem(seq // 2, 2)
    z = seq // 4
    z_count = seq_count // 4
    positions = tokens_ref.shape[0]
    cols = positions // seq_count
    shard = wq_hbm.shape[0]
    out_shard = wo_hbm.shape[0]
    split = qkv_send.shape[2]
    half = split // HEAD_DIM
    other = 1 - dp
    x_peer = (other, seq)
    core_peer = (dp, seq + 1 - 2 * core)
    y_peer = (dp, seq + 2 - 4 * y)

    own_rows = pl.ds(pl.multiple_of(dp * shard, shard), shard)
    own_out = pl.ds(pl.multiple_of(dp * out_shard, out_shard), out_shard)
    weights_in = [
        pltpu.make_async_copy(wq_hbm, w_full.at[0, own_rows, :], local_sem.at[0]),
        pltpu.make_async_copy(wk_hbm, w_full.at[1, own_rows, :], local_sem.at[1]),
        pltpu.make_async_copy(wv_hbm, w_full.at[2, own_rows, :], local_sem.at[2]),
        pltpu.make_async_copy(wo_hbm, wo_full.at[own_out, :], local_sem.at[3]),
    ]
    others_in = [
        pltpu.make_async_copy(tokens_hbm, tokens_ref, local_sem.at[4]),
        pltpu.make_async_copy(cot_hbm, cot_ref, local_sem.at[5]),
        pltpu.make_async_copy(row_mask_hbm, row_mask_ref, local_sem.at[6]),
        pltpu.make_async_copy(column_mask_hbm, column_mask_ref, local_sem.at[7]),
    ]
    outs = [
        pltpu.make_async_copy(mixed_ref, mixed_hbm, local_sem.at[8]),
        pltpu.make_async_copy(gtok_ref, gtok_hbm, local_sem.at[9]),
        pltpu.make_async_copy(gval_ref, gval_hbm, local_sem.at[10]),
        pltpu.make_async_copy(gout_ref, gout_hbm, local_sem.at[11]),
    ]
    for copy in weights_in + others_in:
        copy.start()

    barrier = pltpu.get_barrier_semaphore()
    pl.semaphore_signal(barrier, inc=1, device_id=x_peer, device_id_type=MESH)

    @pl.loop(1, seq_count)
    def _(step):
        pl.semaphore_signal(
            barrier,
            inc=1,
            device_id=(dp, lax.rem(seq + step, seq_count)),
            device_id_type=MESH,
        )

    for copy in weights_in:
        copy.wait()
    pl.semaphore_wait(barrier, seq_count)

    def region(group, owner, qy, qc):
        if group == 3:
            quarter = out_shard // 4
            start = pl.multiple_of(owner * out_shard + (qy * 2 + qc) * quarter, quarter)
            return wo_full.at[pl.ds(start, quarter), :]
        quarter = shard // 4
        start = pl.multiple_of(owner * shard + (qy * 2 + qc) * quarter, quarter)
        if group == 4:
            return w_full.at[:, pl.ds(start, quarter), pl.ds(0, split)]
        return w_full.at[group, pl.ds(start, quarter), pl.ds(split, split)]

    def weight_copy(group, hop):
        if hop == 0:
            ref, peer = region(group, dp, y, core), x_peer
        elif hop == 1:
            ref, peer = region(group, other, y, core), y_peer
        elif hop == 2:
            ref, peer = region(group, other, y, core), core_peer
        else:
            ref, peer = region(group, other, 1 - y, core), core_peer
        return pltpu.make_async_remote_copy(
            src_ref=ref,
            dst_ref=ref,
            send_sem=w_send_sem.at[group, hop],
            recv_sem=w_recv_sem.at[group, hop],
            device_id=peer,
            device_id_type=MESH,
        )

    def pass_on(group):
        weight_copy(group, 0).wait_recv()
        if group + 2 < 5:
            weight_copy(group + 2, 0).start()
        weight_copy(group, 1).start()
        weight_copy(group, 2).start()

    def pass_core(group):
        weight_copy(group, 1).wait_recv()
        weight_copy(group, 3).start()

    def weights_here(group):
        weight_copy(group, 2).wait_recv()
        weight_copy(group, 3).wait_recv()

    def column_copy(src, dst, phase, step):
        target = lax.rem(seq + step, seq_count)
        there = pl.ds(pl.multiple_of(target * cols, cols), cols)
        here = pl.ds(pl.multiple_of(seq * cols, cols), cols)
        return pltpu.make_async_remote_copy(
            src_ref=src.at[:, there, :],
            dst_ref=dst.at[:, here, :],
            send_sem=a_send_sem.at[phase, step],
            recv_sem=a_recv_sem.at[phase, step],
            device_id=(dp, target),
            device_id_type=MESH,
        )

    def one(ref, index):
        return ref.at[pl.ds(index, 1)]

    def exchange(src, dst, phase):
        @pl.loop(1, seq_count)
        def _(step):
            column_copy(src, dst, phase, step).start()

        here = pl.ds(pl.multiple_of(seq * cols, cols), cols)
        dst[:, here, :] = src[:, here, :]

    def arrived(src, dst, phase):
        @pl.loop(1, seq_count)
        def _(step):
            column_copy(src, dst, phase, step).wait_recv()

    def sent(src, dst, phase):
        @pl.loop(1, seq_count)
        def _(step):
            column_copy(src, dst, phase, step).wait_send()

    weight_copy(0, 0).start()
    weight_copy(1, 0).start()

    query_pos = lax.broadcasted_iota(jnp.int32, (positions, positions), 0)
    key_pos = lax.broadcasted_iota(jnp.int32, (positions, positions), 1)
    lane = lax.broadcasted_iota(jnp.int32, (1, 2 * HEAD_DIM), 1)
    first_lanes = lane < HEAD_DIM
    keep = (first_lanes.astype(F32).astype(BF16), (lane >= HEAD_DIM).astype(F32).astype(BF16))

    def store_bias(index, seen):
        bias[index] = jnp.where(seen, 0.0, -1e30)

    row, row2 = query_pos // cols, key_pos // cols
    matching = (lax.rem(query_pos, cols) == lax.rem(key_pos, cols)) & (row2 <= row)
    store_bias(0, key_pos <= query_pos)
    store_bias(1, (key_pos <= query_pos) & ((query_pos // ROWBLK) == (key_pos // ROWBLK)))
    store_bias(2, matching)
    store_bias(3, matching & ((row // COLBLK) == (row2 // COLBLK)))

    for copy in others_in:
        copy.wait()
    tokens_t[...] = tokens_ref[...].T
    cot_t[...] = cot_ref[...].T

    def head_bias(head):
        if head < half:
            bit = row_mask_ref[head, 0, 1, 0]
            return jnp.where(bit == 1, bias[0], bias[1])
        column = lax.rem(lax.broadcasted_iota(jnp.int32, (1, positions), 1), cols)
        bits = jnp.zeros((1, positions), jnp.int32)
        for index in range(cols):
            bits = jnp.where(column == index, column_mask_ref[head - half, index, 1, 0], bits)
        return jnp.where(bits == 1, bias[2], bias[3])

    def softmax(head, query, key):
        scores = dot_nt(query, key) * (1.0 / math.sqrt(HEAD_DIM)) + head_bias(head)
        weights = jnp.exp(scores - jnp.max(scores, axis=-1, keepdims=True))
        return weights * (1.0 / jnp.sum(weights, axis=-1, keepdims=True))

    def pair_of(pair):
        return pl.ds(pair * 2 * HEAD_DIM, 2 * HEAD_DIM)

    def merge(halves):
        return jnp.where(first_lanes, halves[0], halves[1]).astype(BF16)

    def forward(base, query, key, value, slot):
        outs = []
        for side in range(2):
            weights = softmax(base + side, query * keep[side], key)
            probs[slot + side] = weights
            outs.append(dot_nn(weights.astype(BF16), value))
        return merge(outs)

    def backward(query, key, value, grad, slot):
        grads = ([], [], [])
        for side in range(2):
            weights = probs[slot + side]
            grad_side = grad * keep[side]
            grad_probs = dot_nt(grad_side, value)
            grad_scores = weights * (
                grad_probs - jnp.sum(weights * grad_probs, axis=-1, keepdims=True)
            )
            grad_scores = (grad_scores * (1.0 / math.sqrt(HEAD_DIM))).astype(BF16)
            grads[0].append(dot_nn(grad_scores, key))
            grads[1].append(dot_tn(grad_scores, query))
            grads[2].append(dot_tn(weights.astype(BF16), grad))
        return [merge(grad_pair) for grad_pair in grads]

    def rs_copy(which, hop):
        if hop == 0:
            src, dst, peer = part.at[which, :, :, 1 - core], part_recv1.at[which], core_peer
        elif hop == 1:
            src, dst, peer = acc1.at[which, other], part_recv2.at[which], x_peer
        elif hop == 2:
            src, dst, peer = acc2.at[which, :, 1 - y], part_recv3.at[which], y_peer
        else:
            z_there = lax.rem(z + hop - 2, z_count)
            src, dst = acc3.at[which, z_there], part_recv4.at[which, hop - 3]
            peer = (dp, z_there * 4 + y * 2 + core)
        return pltpu.make_async_remote_copy(
            src_ref=src,
            dst_ref=dst,
            send_sem=r_send_sem.at[which, hop],
            recv_sem=r_recv_sem.at[which, hop],
            device_id=peer,
            device_id_type=MESH,
        )

    def rs_start(which, full):
        part[which] = full.astype(BF16).reshape(part.shape[1:])
        rs_copy(which, 0).start()

    def rs_next(which, hop):
        rs_copy(which, hop).wait_recv()
        if hop == 0:
            acc1[which] = (
                part[which, :, :, core].astype(F32) + part_recv1[which].astype(F32)
            ).astype(BF16)
            rs_copy(which, 1).start()
        elif hop == 1:
            total = acc1[which, dp].astype(F32) + part_recv2[which].astype(F32)
            acc2[which] = total.astype(BF16).reshape(acc2.shape[1:])
            rs_copy(which, 2).start()
        else:
            acc3[which] = (
                acc2[which, :, y].astype(F32) + part_recv3[which].astype(F32)
            ).astype(BF16)
            for step in range(1, z_count):
                rs_copy(which, 2 + step).start()

    def rs_end(which):
        total = acc3[which, z].astype(F32)
        for step in range(1, z_count):
            rs_copy(which, 2 + step).wait_recv()
            total = total + part_recv4[which, step - 1].astype(F32)
        return total

    def project_columns(index):
        weights_here(index)
        qkv_send[index] = dot_nn(tokens_ref[...], w_full[index, :, split:]).astype(BF16)
        exchange(one(qkv_send, index), one(qkv_recv, index), index)

    for group in range(3):
        pass_on(group)
    for group in range(3):
        pass_core(group)
    project_columns(0)
    project_columns(1)
    pass_on(3)
    project_columns(2)
    pass_core(3)
    pass_on(4)
    weights_here(3)
    g_send[0] = dot_nt(cot_ref[...], wo_full[split:, :]).astype(BF16)
    exchange(g_send, g_recv, 3)
    g_rows[...] = dot_nt(cot_ref[...], wo_full[:split, :]).astype(BF16)

    pass_core(4)
    weights_here(4)
    row_qkv = [dot_nn(tokens_ref[...], w_full[index, :, :split]).astype(BF16) for index in range(3)]
    for pair in range(split // (2 * HEAD_DIM)):
        lanes = slice(pair * 2 * HEAD_DIM, (pair + 1) * 2 * HEAD_DIM)
        query, key, value = (item[:, lanes] for item in row_qkv)
        attended[:, pair_of(pair)] = forward(2 * pair, query, key, value, 0)
        grads = backward(query, key, value, g_rows[:, pair_of(pair)], 0)
        for index in range(3):
            row_grads[index, :, pair_of(pair)] = grads[index]
    rs_start(0, dot_nn(cot_t[...], attended[:, :split]))
    rs_start(1, dot_nn(tokens_t[...], row_grads[2]))

    for index in range(3):
        arrived(one(qkv_send, index), one(qkv_recv, index), index)
    for pair in range(split // (2 * HEAD_DIM)):
        query, key, value = (qkv_recv[index, :, pair_of(pair)] for index in range(3))
        out_send[0, :, pair_of(pair)] = forward(half + 2 * pair, query, key, value, 2 * pair)
    exchange(out_send, out_recv, 4)
    rs_next(0, 0)
    rs_next(1, 0)

    arrived(g_send, g_recv, 3)
    for pair in range(split // (2 * HEAD_DIM)):
        query, key, value = (qkv_recv[index, :, pair_of(pair)] for index in range(3))
        grads = backward(query, key, value, g_recv[0, :, pair_of(pair)], 2 * pair)
        for index in range(3):
            grad_send[index, :, pair_of(pair)] = grads[index]
    exchange(grad_send, grad_recv, 5)
    rs_next(0, 1)
    rs_next(1, 1)

    arrived(out_send, out_recv, 4)
    attended[:, pl.ds(split, split)] = out_recv[0]
    rs_start(2, dot_nn(cot_t[...], out_recv[0]))
    mixed_ref[...] = dot_nn(attended[...], wo_full[...]).astype(BF16)
    outs[0].start()
    rs_next(2, 0)
    gtok_part[...] = (
        dot_nt(row_grads[0], w_full[0, :, :split])
        + dot_nt(row_grads[1], w_full[1, :, :split])
        + dot_nt(row_grads[2], w_full[2, :, :split])
    )
    rs_next(0, 2)
    rs_next(1, 2)

    arrived(grad_send, grad_recv, 5)
    rs_start(3, dot_nn(tokens_t[...], grad_recv[2]))
    rs_next(2, 1)
    rs_next(3, 0)
    gtok_ref[...] = (
        gtok_part[...]
        + dot_nt(grad_recv[0], w_full[0, :, split:])
        + dot_nt(grad_recv[1], w_full[1, :, split:])
        + dot_nt(grad_recv[2], w_full[2, :, split:])
    ).astype(BF16)
    outs[1].start()
    rs_next(3, 1)
    rs_next(2, 2)
    gout_ref[:split, :] = rs_end(0).T
    gval_ref[:, :split] = rs_end(1)
    rs_next(3, 2)
    gout_ref[split:, :] = rs_end(2).T
    outs[3].start()
    gval_ref[:, split:] = rs_end(3)
    outs[2].start()

    for group in range(5):
        for hop in range(4):
            weight_copy(group, hop).wait_send()
    for index in range(3):
        sent(one(qkv_send, index), one(qkv_recv, index), index)
    sent(g_send, g_recv, 3)
    sent(out_send, out_recv, 4)
    sent(grad_send, grad_recv, 5)
    for which in range(4):
        for hop in range(2 + z_count):
            rs_copy(which, hop).wait_send()
    for copy in outs:
        copy.wait()


def fused_fits(dp_count, seq_count, tokens, row_mask, column_mask, w_query, w_out):
    positions = tokens.shape[1] * tokens.shape[2]
    return (
        tokens.shape[0] == 1
        and tokens.shape[1] == 1
        and dp_count == 2
        and seq_count % 4 == 0
        and positions % (16 * seq_count) == 0
        and w_query.shape[0] % 64 == 0
        and w_out.shape[0] % 64 == 0
        and tokens.shape[3] % (16 * dp_count * seq_count) == 0
        and row_mask.shape[2] == 2
        and column_mask.shape[2] == 2
    )


def fused_body(tokens, cotangent, row_mask, column_mask, w_query, w_key, w_value, w_out):
    dp_count, seq_count = lax.axis_size("dp"), lax.axis_size("seq")
    if not fused_fits(dp_count, seq_count, tokens, row_mask, column_mask, w_query, w_out):
        return body(
            tokens, cotangent, row_mask, column_mask, w_query, w_key, w_value, w_out
        )
    positions, width = tokens.shape[1] * tokens.shape[2], tokens.shape[3]
    heads_width = w_query.shape[1]
    split = heads_width // 2
    rows = width // (dp_count * seq_count)
    z_count = seq_count // 4
    lead = (4, dp_count, seq_count // 2)
    call = pl.pallas_call(
        lambda *refs: fused_kernel(dp_count, seq_count, *refs),
        out_shape=(
            jax.ShapeDtypeStruct((positions, width), BF16),
            jax.ShapeDtypeStruct((positions, width), BF16),
            jax.ShapeDtypeStruct((rows, heads_width), F32),
            jax.ShapeDtypeStruct((heads_width, rows), F32),
        ),
        in_specs=[pl.BlockSpec(memory_space=pl.ANY)] * 8,
        out_specs=[pl.BlockSpec(memory_space=pl.ANY)] * 4,
        scratch_shapes=[
            pltpu.VMEM((positions, width), BF16),
            pltpu.VMEM((positions, width), BF16),
            pltpu.VMEM((width, positions), BF16),
            pltpu.VMEM((width, positions), BF16),
            pltpu.SMEM(row_mask.shape, jnp.int32),
            pltpu.SMEM(column_mask.shape, jnp.int32),
            pltpu.VMEM((4, positions, positions), F32),
            pltpu.VMEM((positions, width), BF16),
            pltpu.VMEM((positions, width), BF16),
            pltpu.VMEM((rows, heads_width), F32),
            pltpu.VMEM((heads_width, rows), F32),
            pltpu.VMEM((positions, width), F32),
            pltpu.VMEM((3, width, heads_width), BF16),
            pltpu.VMEM((heads_width, width), BF16),
            pltpu.VMEM((3, positions, split), BF16),
            pltpu.VMEM((3, positions, split), BF16),
            pltpu.VMEM((positions, split), BF16),
            pltpu.VMEM((1, positions, split), BF16),
            pltpu.VMEM((1, positions, split), BF16),
            pltpu.VMEM((1, positions, split), BF16),
            pltpu.VMEM((1, positions, split), BF16),
            pltpu.VMEM((3, positions, split), BF16),
            pltpu.VMEM((3, positions, split), BF16),
            pltpu.VMEM((3, positions, split), BF16),
            pltpu.VMEM((split // HEAD_DIM, positions, positions), F32),
            pltpu.VMEM((positions, heads_width), BF16),
            pltpu.VMEM(lead + (2, rows, split), BF16),
            pltpu.VMEM(lead + (rows, split), BF16),
            pltpu.VMEM(lead + (rows, split), BF16),
            pltpu.VMEM((4, seq_count // 2, rows, split), BF16),
            pltpu.VMEM((4, z_count, 2, rows, split), BF16),
            pltpu.VMEM((4, z_count, rows, split), BF16),
            pltpu.VMEM((4, z_count, rows, split), BF16),
            pltpu.VMEM((4, z_count - 1, rows, split), BF16),
            pltpu.SemaphoreType.DMA((5, 4)),
            pltpu.SemaphoreType.DMA((5, 4)),
            pltpu.SemaphoreType.DMA((6, seq_count)),
            pltpu.SemaphoreType.DMA((6, seq_count)),
            pltpu.SemaphoreType.DMA((4, 2 + z_count)),
            pltpu.SemaphoreType.DMA((4, 2 + z_count)),
            pltpu.SemaphoreType.DMA((12,)),
        ],
        compiler_params=pltpu.CompilerParams(
            collective_id=0, has_side_effects=True, vmem_limit_bytes=48 * 1024 * 1024
        ),
        cost_estimate=pl.CostEstimate(
            flops=3_400_000_000, bytes_accessed=8_000_000, transcendentals=524288
        ),
    )
    mixed, grad_tokens, grad_value, grad_output = call(
        tokens.reshape(positions, width),
        cotangent.reshape(positions, width),
        row_mask,
        column_mask,
        w_query,
        w_key,
        w_value,
        w_out,
    )
    return (
        mixed.reshape(tokens.shape),
        grad_tokens.reshape(tokens.shape),
        grad_value,
        grad_output,
    )


def solution(mesh):
    return jax.shard_map(
        fused_body,
        mesh=mesh,
        in_specs=(
            P("dp", "seq", None, None),
            P("dp", "seq", None, None),
            P(None, "seq", None, None),
            P(None, "seq", None, None),
            P("dp", None),
            P("dp", None),
            P("dp", None),
            P("dp", None),
        ),
        out_specs=(
            P("dp", "seq", None, None),
            P("dp", "seq", None, None),
            P(("dp", "seq"), None),
            P(None, ("dp", "seq")),
        ),
        check_vma=False,
    )
```

```python
import math

import jax
import jax.numpy as jnp
from jax import lax
from jax.experimental import pallas as pl
from jax.experimental.pallas import tpu as pltpu
from jax.sharding import PartitionSpec as P

HEAD_DIM = 64
ROWBLK = 128
COLBLK = 8


row_forms = ("blhe,bmhe->bhlm", "bhlm,bmhe->blhe")
column_forms = ("lbhe,mbhe->bhlm", "bhlm,mbhe->lbhe")
contract_last = (((1,), (1,)), ((), ()))
contract_first = (((0,), (0,)), ((), ()))


def allowed_cells(mask_blocks, block_size):
    expanded = jnp.repeat(jnp.repeat(mask_blocks, block_size, axis=-2), block_size, axis=-1)
    length = expanded.shape[-1]
    causal = jnp.arange(length)[:, None] >= jnp.arange(length)[None, :]
    return (expanded == 1) & causal


def attend(queries, key_part, value_part, allowed, forms):
    scale_factor = 1.0 / math.sqrt(queries.shape[-1])
    scores = (
        jnp.einsum(forms[0], queries.astype(jnp.float32), key_part.astype(jnp.float32))
        * scale_factor
    )
    scores = jnp.where(allowed, scores, -1e30)
    highest = lax.stop_gradient(jnp.max(scores, axis=-1, keepdims=True))
    weights = jnp.exp(scores - highest)
    weights = weights / jnp.sum(weights, axis=-1, keepdims=True)
    rounded = lax.optimization_barrier(weights.astype(jnp.bfloat16)).astype(jnp.float32)
    result = jnp.einsum(forms[1], rounded, value_part.astype(jnp.float32))
    return result.astype(jnp.bfloat16)


def body(tokens, cotangent, row_mask, column_mask, w_query, w_key, w_value, w_out):
    rows_here = tokens.shape[1]
    grid_cols = tokens.shape[2]
    width = tokens.shape[3]
    heads_width = w_query.shape[1]
    half = heads_width // HEAD_DIM // 2
    split = half * HEAD_DIM
    flat = tokens.reshape(-1, width)
    cot_flat = cotangent.reshape(-1, width)
    token_count = flat.shape[0]
    seq_count = lax.axis_size("seq")
    grid_rows = rows_here * seq_count
    cols_here = grid_cols // seq_count
    full_query, full_key, full_value, full_out = (
        lax.all_gather(w_query, "dp", axis=0, tiled=True),
        lax.all_gather(w_key, "dp", axis=0, tiled=True),
        lax.all_gather(w_value, "dp", axis=0, tiled=True),
        lax.all_gather(w_out, "dp", axis=0, tiled=True),
    )
    proj_query = jnp.dot(flat, full_query, preferred_element_type=jnp.float32)
    proj_key = jnp.dot(flat, full_key, preferred_element_type=jnp.float32)
    proj_value = jnp.dot(flat, full_value, preferred_element_type=jnp.float32)
    query_flat = proj_query.astype(jnp.bfloat16)
    key_flat = proj_key.astype(jnp.bfloat16)
    value_flat = proj_value.astype(jnp.bfloat16)
    row_allowed = allowed_cells(jnp.transpose(row_mask, (1, 0, 2, 3)), ROWBLK)
    column_allowed = allowed_cells(jnp.transpose(column_mask, (1, 0, 2, 3)), COLBLK)

    def row_core(first, second, third):
        return attend(first, second, third, row_allowed, row_forms)

    def column_core(first, second, third):
        return attend(first, second, third, column_allowed, column_forms)

    def row_heads(matrix):
        return matrix[:, :split].reshape(rows_here, grid_cols, half, HEAD_DIM)

    def column_heads(matrix):
        return matrix[:, split:].reshape(rows_here, grid_cols, split)

    def as_columns(block):
        return block.reshape(grid_rows, cols_here, half, HEAD_DIM)

    def joined(row_part, col_part):
        return jnp.concatenate(
            [row_part.reshape(token_count, split), col_part.reshape(token_count, split)], axis=1
        )

    col_query, col_key, col_value = (
        lax.all_to_all(column_heads(query_flat), "seq", split_axis=1, concat_axis=0, tiled=True),
        lax.all_to_all(column_heads(key_flat), "seq", split_axis=1, concat_axis=0, tiled=True),
        lax.all_to_all(column_heads(value_flat), "seq", split_axis=1, concat_axis=0, tiled=True),
    )
    row_out, row_back = jax.vjp(
        row_core, row_heads(query_flat), row_heads(key_flat), row_heads(value_flat)
    )
    column_out, column_back = jax.vjp(
        column_core, as_columns(col_query), as_columns(col_key), as_columns(col_value)
    )
    returned = lax.all_to_all(
        column_out.reshape(grid_rows, cols_here, split),
        "seq",
        split_axis=0,
        concat_axis=1,
        tiled=True,
    )
    attended = joined(row_out, returned)
    mixed = jnp.dot(attended, full_out, preferred_element_type=jnp.float32)
    grad_heads = lax.dot_general(
        cot_flat, full_out, contract_last, preferred_element_type=jnp.float32
    )
    mixed = mixed.astype(jnp.bfloat16).reshape(tokens.shape)
    grad_heads = grad_heads.astype(jnp.bfloat16)
    row_grads = row_back(grad_heads[:, :split].reshape(rows_here, grid_cols, half, HEAD_DIM))
    grad_columns = lax.all_to_all(
        grad_heads[:, split:].reshape(rows_here, grid_cols, split),
        "seq",
        split_axis=1,
        concat_axis=0,
        tiled=True,
    )
    col_grads = column_back(as_columns(grad_columns))
    back_grads = (
        lax.all_to_all(
            col_grads[0].reshape(grid_rows, cols_here, split),
            "seq",
            split_axis=0,
            concat_axis=1,
            tiled=True,
        ),
        lax.all_to_all(
            col_grads[1].reshape(grid_rows, cols_here, split),
            "seq",
            split_axis=0,
            concat_axis=1,
            tiled=True,
        ),
        lax.all_to_all(
            col_grads[2].reshape(grid_rows, cols_here, split),
            "seq",
            split_axis=0,
            concat_axis=1,
            tiled=True,
        ),
    )
    grad_query = joined(row_grads[0], back_grads[0])
    grad_key = joined(row_grads[1], back_grads[1])
    grad_val = joined(row_grads[2], back_grads[2])
    grad_tokens = (
        lax.dot_general(grad_query, full_query, contract_last, preferred_element_type=jnp.float32)
        + lax.dot_general(grad_key, full_key, contract_last, preferred_element_type=jnp.float32)
        + lax.dot_general(grad_val, full_value, contract_last, preferred_element_type=jnp.float32)
    )
    grad_tokens = grad_tokens.astype(jnp.bfloat16).reshape(tokens.shape)
    summed = lax.psum_scatter(
        jnp.concatenate(
            [
                lax.dot_general(flat, grad_val, contract_first, preferred_element_type=jnp.float32),
                lax.dot_general(
                    cot_flat, attended, contract_first, preferred_element_type=jnp.float32
                ),
            ],
            axis=1,
        ),
        ("dp", "seq"),
        scatter_dimension=0,
        tiled=True,
    )
    grad_value = summed[:, :heads_width]
    grad_output = jnp.transpose(summed[:, heads_width:])
    return (mixed, grad_tokens, grad_value, grad_output)


MESH = pl.DeviceIdType.MESH
F32 = jnp.float32
BF16 = jnp.bfloat16


def dot_nn(a, b):
    return jnp.dot(a, b, preferred_element_type=F32)


def dot_nt(a, b):
    return lax.dot_general(a, b, contract_last, preferred_element_type=F32)


def dot_tn(a, b):
    return lax.dot_general(a, b, contract_first, preferred_element_type=F32)


def fused_kernel(
    dp_count,
    seq_count,
    tokens_hbm,
    cot_hbm,
    row_mask_hbm,
    column_mask_hbm,
    wq_hbm,
    wk_hbm,
    wv_hbm,
    wo_hbm,
    mixed_hbm,
    gtok_hbm,
    gval_hbm,
    gout_hbm,
    tokens_ref,
    cot_ref,
    tokens_t,
    cot_t,
    row_mask_ref,
    column_mask_ref,
    bias,
    mixed_ref,
    gtok_ref,
    gval_ref,
    gout_ref,
    gtok_part,
    w_full,
    wo_full,
    qkv_send,
    qkv_recv,
    g_rows,
    g_send,
    g_recv,
    out_send,
    out_recv,
    grad_send,
    grad_recv,
    row_grads,
    probs,
    attended,
    part,
    part_recv1,
    acc1,
    part_recv2,
    acc2,
    part_recv3,
    acc3,
    part_recv4,
    w_send_sem,
    w_recv_sem,
    a_send_sem,
    a_recv_sem,
    r_send_sem,
    r_recv_sem,
    local_sem,
):
    dp = lax.axis_index("dp")
    seq = lax.axis_index("seq")
    core = lax.rem(seq, 2)
    y = lax.rem(seq // 2, 2)
    z = seq // 4
    z_count = seq_count // 4
    positions = tokens_ref.shape[0]
    cols = positions // seq_count
    shard = wq_hbm.shape[0]
    out_shard = wo_hbm.shape[0]
    split = qkv_send.shape[2]
    half = split // HEAD_DIM
    other = 1 - dp
    x_peer = (other, seq)
    core_peer = (dp, seq + 1 - 2 * core)
    y_peer = (dp, seq + 2 - 4 * y)

    own_rows = pl.ds(pl.multiple_of(dp * shard, shard), shard)
    own_out = pl.ds(pl.multiple_of(dp * out_shard, out_shard), out_shard)
    weights_in = [
        pltpu.make_async_copy(wq_hbm, w_full.at[0, own_rows, :], local_sem.at[0]),
        pltpu.make_async_copy(wk_hbm, w_full.at[1, own_rows, :], local_sem.at[1]),
        pltpu.make_async_copy(wv_hbm, w_full.at[2, own_rows, :], local_sem.at[2]),
        pltpu.make_async_copy(wo_hbm, wo_full.at[own_out, :], local_sem.at[3]),
    ]
    others_in = [
        pltpu.make_async_copy(tokens_hbm, tokens_ref, local_sem.at[4]),
        pltpu.make_async_copy(cot_hbm, cot_ref, local_sem.at[5]),
        pltpu.make_async_copy(row_mask_hbm, row_mask_ref, local_sem.at[6]),
        pltpu.make_async_copy(column_mask_hbm, column_mask_ref, local_sem.at[7]),
    ]
    outs = [
        pltpu.make_async_copy(mixed_ref, mixed_hbm, local_sem.at[8]),
        pltpu.make_async_copy(gtok_ref, gtok_hbm, local_sem.at[9]),
        pltpu.make_async_copy(gval_ref, gval_hbm, local_sem.at[10]),
        pltpu.make_async_copy(gout_ref, gout_hbm, local_sem.at[11]),
    ]
    for copy in weights_in + others_in:
        copy.start()

    barrier = pltpu.get_barrier_semaphore()
    pl.semaphore_signal(barrier, inc=1, device_id=x_peer, device_id_type=MESH)

    @pl.loop(1, seq_count, unroll=True)
    def _(step):
        pl.semaphore_signal(
            barrier,
            inc=1,
            device_id=(dp, lax.rem(seq + step, seq_count)),
            device_id_type=MESH,
        )

    for copy in weights_in:
        copy.wait()
    pl.semaphore_wait(barrier, seq_count)

    def region(group, owner, qy, qc):
        if group == 3:
            quarter = out_shard // 4
            start = pl.multiple_of(owner * out_shard + (qy * 2 + qc) * quarter, quarter)
            return wo_full.at[pl.ds(start, quarter), :]
        quarter = shard // 4
        start = pl.multiple_of(owner * shard + (qy * 2 + qc) * quarter, quarter)
        if group == 4:
            return w_full.at[:, pl.ds(start, quarter), pl.ds(0, split)]
        return w_full.at[group, pl.ds(start, quarter), pl.ds(split, split)]

    def weight_copy(group, hop):
        if hop == 0:
            ref, peer = region(group, dp, y, core), x_peer
        elif hop == 1:
            ref, peer = region(group, other, y, core), y_peer
        elif hop == 2:
            ref, peer = region(group, other, y, core), core_peer
        else:
            ref, peer = region(group, other, 1 - y, core), core_peer
        return pltpu.make_async_remote_copy(
            src_ref=ref,
            dst_ref=ref,
            send_sem=w_send_sem.at[group, hop],
            recv_sem=w_recv_sem.at[group, hop],
            device_id=peer,
            device_id_type=MESH,
        )

    def pass_on(group):
        weight_copy(group, 0).wait_recv()
        if group + 2 < 5:
            weight_copy(group + 2, 0).start()
        weight_copy(group, 1).start()
        weight_copy(group, 2).start()

    def pass_core(group):
        weight_copy(group, 1).wait_recv()
        weight_copy(group, 3).start()

    def weights_here(group):
        weight_copy(group, 2).wait_recv()
        weight_copy(group, 3).wait_recv()

    def column_copy(src, dst, phase, step):
        target = lax.rem(seq + step, seq_count)
        there = pl.ds(pl.multiple_of(target * cols, cols), cols)
        here = pl.ds(pl.multiple_of(seq * cols, cols), cols)
        return pltpu.make_async_remote_copy(
            src_ref=src.at[:, there, :],
            dst_ref=dst.at[:, here, :],
            send_sem=a_send_sem.at[phase],
            recv_sem=a_recv_sem.at[phase],
            device_id=(dp, target),
            device_id_type=MESH,
        )

    def one(ref, index):
        return ref.at[pl.ds(index, 1)]

    def exchange(src, dst, phase):
        @pl.loop(1, seq_count, unroll=True)
        def _(step):
            column_copy(src, dst, phase, step).start()

        here = pl.ds(pl.multiple_of(seq * cols, cols), cols)
        dst[:, here, :] = src[:, here, :]

    def whole_exchange(src, dst, phase):
        many = pl.ds(0, positions - cols)
        return pltpu.make_async_remote_copy(
            src_ref=src.at[:, many, :],
            dst_ref=dst.at[:, many, :],
            send_sem=a_send_sem.at[phase],
            recv_sem=a_recv_sem.at[phase],
            device_id=core_peer,
            device_id_type=MESH,
        )

    def arrived(src, dst, phase):
        whole_exchange(src, dst, phase).wait_recv()

    def sent(src, dst, phase):
        whole_exchange(src, dst, phase).wait_send()

    weight_copy(0, 0).start()
    weight_copy(1, 0).start()

    query_pos = lax.broadcasted_iota(jnp.int32, (positions, positions), 0)
    key_pos = lax.broadcasted_iota(jnp.int32, (positions, positions), 1)
    lane = lax.broadcasted_iota(jnp.int32, (1, 2 * HEAD_DIM), 1)
    first_lanes = lane < HEAD_DIM
    keep = (first_lanes.astype(F32).astype(BF16), (lane >= HEAD_DIM).astype(F32).astype(BF16))

    def store_bias(index, seen):
        bias[index] = jnp.where(seen, 0.0, -1e30)

    row, row2 = query_pos // cols, key_pos // cols
    matching = (lax.rem(query_pos, cols) == lax.rem(key_pos, cols)) & (row2 <= row)
    store_bias(0, key_pos <= query_pos)
    store_bias(1, (key_pos <= query_pos) & ((query_pos // ROWBLK) == (key_pos // ROWBLK)))
    store_bias(2, matching)
    store_bias(3, matching & ((row // COLBLK) == (row2 // COLBLK)))

    for copy in others_in:
        copy.wait()

    def head_bias(head):
        if head < half:
            bit = row_mask_ref[0, 1, 0, head]
            return jnp.where(bit == 1, bias[0], bias[1])
        column = lax.rem(lax.broadcasted_iota(jnp.int32, (1, positions), 1), cols)
        bits = jnp.zeros((1, positions), jnp.int32)
        for index in range(cols):
            bits = jnp.where(column == index, column_mask_ref[head - half, 1, 0, index], bits)
        return jnp.where(bits == 1, bias[2], bias[3])

    def softmax(head, query, key):
        scores = dot_nt(query, key) * (1.0 / math.sqrt(HEAD_DIM)) + head_bias(head)
        weights = jnp.exp(scores - jnp.max(scores, axis=-1, keepdims=True))
        return weights * (1.0 / jnp.sum(weights, axis=-1, keepdims=True))

    def pair_of(pair):
        return pl.ds(pair * 2 * HEAD_DIM, 2 * HEAD_DIM)

    def merge(halves):
        return jnp.where(first_lanes, halves[0], halves[1]).astype(BF16)

    def forward(base, query, key, value, slot):
        outs = []
        for side in range(2):
            weights = softmax(base + side, query * keep[side], key)
            probs[slot + side] = weights
            outs.append(dot_nn(weights.astype(BF16), value))
        return merge(outs)

    def backward(query, key, value, grad, slot):
        grads = ([], [], [])
        for side in range(2):
            weights = probs[slot + side]
            grad_side = grad * keep[side]
            grad_probs = dot_nt(grad_side, value)
            grad_scores = weights * (
                grad_probs - jnp.sum(weights * grad_probs, axis=-1, keepdims=True)
            )
            grad_scores = (grad_scores * (1.0 / math.sqrt(HEAD_DIM))).astype(BF16)
            grads[0].append(dot_nn(grad_scores, key))
            grads[1].append(dot_tn(grad_scores, query))
            grads[2].append(dot_tn(weights.astype(BF16), grad))
        return [merge(grad_pair) for grad_pair in grads]

    def rs_copy(which, hop):
        if hop == 0:
            src, dst, peer = part.at[which, :, :, 1 - core], part_recv1.at[which], core_peer
        elif hop == 1:
            src, dst, peer = acc1.at[which, other], part_recv2.at[which], x_peer
        elif hop == 2:
            src, dst, peer = acc2.at[which, :, 1 - y], part_recv3.at[which], y_peer
        else:
            z_there = lax.rem(z + hop - 2, z_count)
            src, dst = acc3.at[which, z_there], part_recv4.at[which, hop - 3]
            peer = (dp, z_there * 4 + y * 2 + core)
        return pltpu.make_async_remote_copy(
            src_ref=src,
            dst_ref=dst,
            send_sem=r_send_sem.at[which, hop],
            recv_sem=r_recv_sem.at[which, hop],
            device_id=peer,
            device_id_type=MESH,
        )

    def rs_start(which, full):
        part[which] = full.astype(BF16).reshape(part.shape[1:])
        rs_copy(which, 0).start()

    def rs_next(which, hop):
        rs_copy(which, hop).wait_recv()
        if hop == 0:
            acc1[which] = (
                part[which, :, :, core].astype(F32) + part_recv1[which].astype(F32)
            ).astype(BF16)
            rs_copy(which, 1).start()
        elif hop == 1:
            total = acc1[which, dp].astype(F32) + part_recv2[which].astype(F32)
            acc2[which] = total.astype(BF16).reshape(acc2.shape[1:])
            rs_copy(which, 2).start()
        else:
            acc3[which] = (
                acc2[which, :, y].astype(F32) + part_recv3[which].astype(F32)
            ).astype(BF16)
            for step in range(1, z_count):
                rs_copy(which, 2 + step).start()

    def rs_end(which):
        total = acc3[which, z].astype(F32)
        for step in range(1, z_count):
            rs_copy(which, 2 + step).wait_recv()
            total = total + part_recv4[which, step - 1].astype(F32)
        return total

    def project_columns(index):
        weights_here(index)
        qkv_send[index] = dot_nn(tokens_ref[...], w_full[index, :, split:]).astype(BF16)
        exchange(one(qkv_send, index), one(qkv_recv, index), index)

    pass_on(0)
    pass_on(1)
    pass_core(0)
    pass_on(2)
    project_columns(0)
    pass_core(1)
    project_columns(1)
    pass_core(2)
    pass_on(3)
    project_columns(2)
    pass_core(3)
    pass_on(4)
    weights_here(3)
    g_send[0] = dot_nt(cot_ref[...], wo_full[split:, :]).astype(BF16)
    exchange(g_send, g_recv, 3)
    g_rows[...] = dot_nt(cot_ref[...], wo_full[:split, :]).astype(BF16)
    tokens_t[...] = tokens_ref[...].T
    cot_t[...] = cot_ref[...].T

    for index in range(3):
        arrived(one(qkv_send, index), one(qkv_recv, index), index)
    for pair in range(split // (2 * HEAD_DIM)):
        query, key, value = (qkv_recv[index, :, pair_of(pair)] for index in range(3))
        out_send[0, :, pair_of(pair)] = forward(half + 2 * pair, query, key, value, 2 * pair)
    exchange(out_send, out_recv, 4)
    pass_core(4)

    arrived(g_send, g_recv, 3)
    for pair in range(split // (2 * HEAD_DIM)):
        query, key, value = (qkv_recv[index, :, pair_of(pair)] for index in range(3))
        grads = backward(query, key, value, g_recv[0, :, pair_of(pair)], 2 * pair)
        for index in range(3):
            grad_send[index, :, pair_of(pair)] = grads[index]
    exchange(grad_send, grad_recv, 5)

    weights_here(4)
    row_qkv = [dot_nn(tokens_ref[...], w_full[index, :, :split]).astype(BF16) for index in range(3)]
    for pair in range(split // (2 * HEAD_DIM)):
        lanes = slice(pair * 2 * HEAD_DIM, (pair + 1) * 2 * HEAD_DIM)
        query, key, value = (item[:, lanes] for item in row_qkv)
        attended[:, pair_of(pair)] = forward(2 * pair, query, key, value, 0)
        grads = backward(query, key, value, g_rows[:, pair_of(pair)], 0)
        for index in range(3):
            row_grads[index, :, pair_of(pair)] = grads[index]
    rs_start(0, dot_nn(cot_t[...], attended[:, :split]))
    rs_start(1, dot_nn(tokens_t[...], row_grads[2]))

    arrived(out_send, out_recv, 4)
    rs_start(2, dot_nn(cot_t[...], out_recv[0]))
    rs_next(0, 0)
    rs_next(1, 0)
    attended[:, pl.ds(split, split)] = out_recv[0]
    mixed_ref[...] = dot_nn(attended[...], wo_full[...]).astype(BF16)
    outs[0].start()
    rs_next(2, 0)

    arrived(grad_send, grad_recv, 5)
    rs_start(3, dot_nn(tokens_t[...], grad_recv[2]))
    rs_next(0, 1)
    gtok_part[...] = (
        dot_nt(row_grads[0], w_full[0, :, :split])
        + dot_nt(row_grads[1], w_full[1, :, :split])
        + dot_nt(row_grads[2], w_full[2, :, :split])
    )
    rs_next(3, 0)
    rs_next(1, 1)
    gtok_ref[...] = (
        gtok_part[...]
        + dot_nt(grad_recv[0], w_full[0, :, split:])
        + dot_nt(grad_recv[1], w_full[1, :, split:])
        + dot_nt(grad_recv[2], w_full[2, :, split:])
    ).astype(BF16)
    outs[1].start()
    rs_next(2, 1)
    rs_next(0, 2)
    rs_next(1, 2)
    for group in range(5):
        for hop in range(4):
            weight_copy(group, hop).wait_send()
    for index in range(3):
        sent(one(qkv_send, index), one(qkv_recv, index), index)
    sent(g_send, g_recv, 3)
    sent(out_send, out_recv, 4)
    sent(grad_send, grad_recv, 5)
    rs_next(3, 1)
    rs_next(2, 2)
    gout_ref[:, :split] = rs_end(0)
    gval_ref[:, :split] = rs_end(1)
    rs_next(3, 2)
    gout_ref[:, split:] = rs_end(2)
    outs[3].start()
    for which in range(3):
        for hop in range(2 + z_count):
            rs_copy(which, hop).wait_send()
    gval_ref[:, split:] = rs_end(3)
    outs[2].start()
    for hop in range(2 + z_count):
        rs_copy(3, hop).wait_send()
    for copy in outs:
        copy.wait()


def hand_out_kernel(*refs):
    count = len(refs) // 2
    sems = refs[-1]
    copies = [
        pltpu.make_async_copy(refs[index], refs[count + index], sems.at[index])
        for index in range(count)
    ]
    for copy in copies:
        copy.start()
    for copy in copies:
        copy.wait()


def hand_out(*arrays):
    return pl.pallas_call(
        hand_out_kernel,
        out_shape=[jax.ShapeDtypeStruct(item.shape, item.dtype) for item in arrays],
        in_specs=[pl.BlockSpec(memory_space=pltpu.HBM)] * len(arrays),
        out_specs=[pl.BlockSpec(memory_space=pltpu.HBM)] * len(arrays),
        scratch_shapes=[pltpu.SemaphoreType.DMA((len(arrays),))],
        compiler_params=pltpu.CompilerParams(vmem_limit_bytes=64 * 1024 * 1024 - 65536),
    )(*arrays)


def fused_fits(dp_count, seq_count, tokens, row_mask, column_mask, w_query, w_out):
    positions = tokens.shape[1] * tokens.shape[2]
    return (
        tokens.shape[0] == 1
        and tokens.shape[1] == 1
        and dp_count == 2
        and seq_count % 4 == 0
        and positions % (16 * seq_count) == 0
        and w_query.shape[0] % 64 == 0
        and w_out.shape[0] % 64 == 0
        and tokens.shape[3] % (16 * dp_count * seq_count) == 0
        and row_mask.shape[2] == 2
        and column_mask.shape[2] == 2
    )


def fused_body(tokens, cotangent, row_mask, column_mask, w_query, w_key, w_value, w_out):
    dp_count, seq_count = lax.axis_size("dp"), lax.axis_size("seq")
    if not fused_fits(dp_count, seq_count, tokens, row_mask, column_mask, w_query, w_out):
        return body(
            tokens, cotangent, row_mask, column_mask, w_query, w_key, w_value, w_out
        )
    positions, width = tokens.shape[1] * tokens.shape[2], tokens.shape[3]
    heads_width = w_query.shape[1]
    split = heads_width // 2
    rows = width // (dp_count * seq_count)
    z_count = seq_count // 4
    stored_row_mask = jnp.transpose(row_mask, (1, 2, 3, 0))
    stored_column_mask = jnp.transpose(column_mask, (0, 2, 3, 1))
    lead = (4, dp_count, seq_count // 2)
    call = pl.pallas_call(
        lambda *refs: fused_kernel(dp_count, seq_count, *refs),
        out_shape=(
            jax.ShapeDtypeStruct((positions, width), BF16),
            jax.ShapeDtypeStruct((positions, width), BF16),
            jax.ShapeDtypeStruct((rows, heads_width), F32),
            jax.ShapeDtypeStruct((rows, heads_width), F32),
        ),
        in_specs=[pl.BlockSpec(memory_space=pltpu.HBM)] * 8,
        out_specs=[pl.BlockSpec(memory_space=pltpu.HBM)] * 4,
        scratch_shapes=[
            pltpu.VMEM((positions, width), BF16),
            pltpu.VMEM((positions, width), BF16),
            pltpu.VMEM((width, positions), BF16),
            pltpu.VMEM((width, positions), BF16),
            pltpu.SMEM(stored_row_mask.shape, jnp.int32),
            pltpu.SMEM(stored_column_mask.shape, jnp.int32),
            pltpu.VMEM((4, positions, positions), F32),
            pltpu.VMEM((positions, width), BF16),
            pltpu.VMEM((positions, width), BF16),
            pltpu.VMEM((rows, heads_width), F32),
            pltpu.VMEM((rows, heads_width), F32),
            pltpu.VMEM((positions, width), F32),
            pltpu.VMEM((3, width, heads_width), BF16),
            pltpu.VMEM((heads_width, width), BF16),
            pltpu.VMEM((3, positions, split), BF16),
            pltpu.VMEM((3, positions, split), BF16),
            pltpu.VMEM((positions, split), BF16),
            pltpu.VMEM((1, positions, split), BF16),
            pltpu.VMEM((1, positions, split), BF16),
            pltpu.VMEM((1, positions, split), BF16),
            pltpu.VMEM((1, positions, split), BF16),
            pltpu.VMEM((3, positions, split), BF16),
            pltpu.VMEM((3, positions, split), BF16),
            pltpu.VMEM((3, positions, split), BF16),
            pltpu.VMEM((split // HEAD_DIM, positions, positions), F32),
            pltpu.VMEM((positions, heads_width), BF16),
            pltpu.VMEM(lead + (2, rows, split), BF16),
            pltpu.VMEM(lead + (rows, split), BF16),
            pltpu.VMEM(lead + (rows, split), BF16),
            pltpu.VMEM((4, seq_count // 2, rows, split), BF16),
            pltpu.VMEM((4, z_count, 2, rows, split), BF16),
            pltpu.VMEM((4, z_count, rows, split), BF16),
            pltpu.VMEM((4, z_count, rows, split), BF16),
            pltpu.VMEM((4, z_count - 1, rows, split), BF16),
            pltpu.SemaphoreType.DMA((5, 4)),
            pltpu.SemaphoreType.DMA((5, 4)),
            pltpu.SemaphoreType.DMA((6,)),
            pltpu.SemaphoreType.DMA((6,)),
            pltpu.SemaphoreType.DMA((4, 2 + z_count)),
            pltpu.SemaphoreType.DMA((4, 2 + z_count)),
            pltpu.SemaphoreType.DMA((12,)),
        ],
        compiler_params=pltpu.CompilerParams(
            collective_id=0, has_side_effects=True, vmem_limit_bytes=64 * 1024 * 1024 - 65536
        ),
        cost_estimate=pl.CostEstimate(
            flops=3_400_000_000, bytes_accessed=8_000_000, transcendentals=524288
        ),
    )
    mixed, grad_tokens, grad_value, grad_output = call(
        tokens.reshape(positions, width),
        cotangent.reshape(positions, width),
        stored_row_mask,
        stored_column_mask,
        w_query,
        w_key,
        w_value,
        w_out,
    )
    mixed, grad_tokens, grad_value, grad_output = hand_out(
        mixed, grad_tokens, grad_value, grad_output
    )
    return (
        mixed.reshape(tokens.shape),
        grad_tokens.reshape(tokens.shape),
        grad_value,
        jnp.transpose(grad_output),
    )


def solution(mesh):
    return jax.shard_map(
        fused_body,
        mesh=mesh,
        in_specs=(
            P("dp", "seq", None, None),
            P("dp", "seq", None, None),
            P(None, "seq", None, None),
            P(None, "seq", None, None),
            P("dp", None),
            P("dp", None),
            P("dp", None),
            P("dp", None),
        ),
        out_specs=(
            P("dp", "seq", None, None),
            P("dp", "seq", None, None),
            P(("dp", "seq"), None),
            P(None, ("dp", "seq")),
        ),
        check_vma=False,
    )
```

```python
import math

import jax
import jax.numpy as jnp
from jax import lax
from jax.experimental import pallas as pl
from jax.experimental.pallas import tpu as pltpu
from jax.sharding import PartitionSpec as P

HEAD_DIM = 64
ROWBLK = 128
COLBLK = 8


row_forms = ("blhe,bmhe->bhlm", "bhlm,bmhe->blhe")
column_forms = ("lbhe,mbhe->bhlm", "bhlm,mbhe->lbhe")
contract_last = (((1,), (1,)), ((), ()))
contract_first = (((0,), (0,)), ((), ()))


def allowed_cells(mask_blocks, block_size):
    expanded = jnp.repeat(jnp.repeat(mask_blocks, block_size, axis=-2), block_size, axis=-1)
    length = expanded.shape[-1]
    causal = jnp.arange(length)[:, None] >= jnp.arange(length)[None, :]
    return (expanded == 1) & causal


def attend(queries, key_part, value_part, allowed, forms):
    scale_factor = 1.0 / math.sqrt(queries.shape[-1])
    scores = (
        jnp.einsum(forms[0], queries.astype(jnp.float32), key_part.astype(jnp.float32))
        * scale_factor
    )
    scores = jnp.where(allowed, scores, -1e30)
    highest = lax.stop_gradient(jnp.max(scores, axis=-1, keepdims=True))
    weights = jnp.exp(scores - highest)
    weights = weights / jnp.sum(weights, axis=-1, keepdims=True)
    rounded = lax.optimization_barrier(weights.astype(jnp.bfloat16)).astype(jnp.float32)
    result = jnp.einsum(forms[1], rounded, value_part.astype(jnp.float32))
    return result.astype(jnp.bfloat16)


def body(tokens, cotangent, row_mask, column_mask, w_query, w_key, w_value, w_out):
    rows_here = tokens.shape[1]
    grid_cols = tokens.shape[2]
    width = tokens.shape[3]
    heads_width = w_query.shape[1]
    half = heads_width // HEAD_DIM // 2
    split = half * HEAD_DIM
    flat = tokens.reshape(-1, width)
    cot_flat = cotangent.reshape(-1, width)
    token_count = flat.shape[0]
    seq_count = lax.axis_size("seq")
    grid_rows = rows_here * seq_count
    cols_here = grid_cols // seq_count
    full_query, full_key, full_value, full_out = (
        lax.all_gather(w_query, "dp", axis=0, tiled=True),
        lax.all_gather(w_key, "dp", axis=0, tiled=True),
        lax.all_gather(w_value, "dp", axis=0, tiled=True),
        lax.all_gather(w_out, "dp", axis=0, tiled=True),
    )
    proj_query = jnp.dot(flat, full_query, preferred_element_type=jnp.float32)
    proj_key = jnp.dot(flat, full_key, preferred_element_type=jnp.float32)
    proj_value = jnp.dot(flat, full_value, preferred_element_type=jnp.float32)
    query_flat = proj_query.astype(jnp.bfloat16)
    key_flat = proj_key.astype(jnp.bfloat16)
    value_flat = proj_value.astype(jnp.bfloat16)
    row_allowed = allowed_cells(jnp.transpose(row_mask, (1, 0, 2, 3)), ROWBLK)
    column_allowed = allowed_cells(jnp.transpose(column_mask, (1, 0, 2, 3)), COLBLK)

    def row_core(first, second, third):
        return attend(first, second, third, row_allowed, row_forms)

    def column_core(first, second, third):
        return attend(first, second, third, column_allowed, column_forms)

    def row_heads(matrix):
        return matrix[:, :split].reshape(rows_here, grid_cols, half, HEAD_DIM)

    def column_heads(matrix):
        return matrix[:, split:].reshape(rows_here, grid_cols, split)

    def as_columns(block):
        return block.reshape(grid_rows, cols_here, half, HEAD_DIM)

    def joined(row_part, col_part):
        return jnp.concatenate(
            [row_part.reshape(token_count, split), col_part.reshape(token_count, split)], axis=1
        )

    col_query, col_key, col_value = (
        lax.all_to_all(column_heads(query_flat), "seq", split_axis=1, concat_axis=0, tiled=True),
        lax.all_to_all(column_heads(key_flat), "seq", split_axis=1, concat_axis=0, tiled=True),
        lax.all_to_all(column_heads(value_flat), "seq", split_axis=1, concat_axis=0, tiled=True),
    )
    row_out, row_back = jax.vjp(
        row_core, row_heads(query_flat), row_heads(key_flat), row_heads(value_flat)
    )
    column_out, column_back = jax.vjp(
        column_core, as_columns(col_query), as_columns(col_key), as_columns(col_value)
    )
    returned = lax.all_to_all(
        column_out.reshape(grid_rows, cols_here, split),
        "seq",
        split_axis=0,
        concat_axis=1,
        tiled=True,
    )
    attended = joined(row_out, returned)
    mixed = jnp.dot(attended, full_out, preferred_element_type=jnp.float32)
    grad_heads = lax.dot_general(
        cot_flat, full_out, contract_last, preferred_element_type=jnp.float32
    )
    mixed = mixed.astype(jnp.bfloat16).reshape(tokens.shape)
    grad_heads = grad_heads.astype(jnp.bfloat16)
    row_grads = row_back(grad_heads[:, :split].reshape(rows_here, grid_cols, half, HEAD_DIM))
    grad_columns = lax.all_to_all(
        grad_heads[:, split:].reshape(rows_here, grid_cols, split),
        "seq",
        split_axis=1,
        concat_axis=0,
        tiled=True,
    )
    col_grads = column_back(as_columns(grad_columns))
    back_grads = (
        lax.all_to_all(
            col_grads[0].reshape(grid_rows, cols_here, split),
            "seq",
            split_axis=0,
            concat_axis=1,
            tiled=True,
        ),
        lax.all_to_all(
            col_grads[1].reshape(grid_rows, cols_here, split),
            "seq",
            split_axis=0,
            concat_axis=1,
            tiled=True,
        ),
        lax.all_to_all(
            col_grads[2].reshape(grid_rows, cols_here, split),
            "seq",
            split_axis=0,
            concat_axis=1,
            tiled=True,
        ),
    )
    grad_query = joined(row_grads[0], back_grads[0])
    grad_key = joined(row_grads[1], back_grads[1])
    grad_val = joined(row_grads[2], back_grads[2])
    grad_tokens = (
        lax.dot_general(grad_query, full_query, contract_last, preferred_element_type=jnp.float32)
        + lax.dot_general(grad_key, full_key, contract_last, preferred_element_type=jnp.float32)
        + lax.dot_general(grad_val, full_value, contract_last, preferred_element_type=jnp.float32)
    )
    grad_tokens = grad_tokens.astype(jnp.bfloat16).reshape(tokens.shape)
    summed = lax.psum_scatter(
        jnp.concatenate(
            [
                lax.dot_general(flat, grad_val, contract_first, preferred_element_type=jnp.float32),
                lax.dot_general(
                    cot_flat, attended, contract_first, preferred_element_type=jnp.float32
                ),
            ],
            axis=1,
        ),
        ("dp", "seq"),
        scatter_dimension=0,
        tiled=True,
    )
    grad_value = summed[:, :heads_width]
    grad_output = jnp.transpose(summed[:, heads_width:])
    return (mixed, grad_tokens, grad_value, grad_output)


MESH = pl.DeviceIdType.MESH
F32 = jnp.float32
BF16 = jnp.bfloat16


def dot_nn(a, b):
    return jnp.dot(a, b, preferred_element_type=F32)


def dot_nt(a, b):
    return lax.dot_general(a, b, contract_last, preferred_element_type=F32)


def dot_tn(a, b):
    return lax.dot_general(a, b, contract_first, preferred_element_type=F32)


def fused_kernel(
    dp_count,
    seq_count,
    tokens_hbm,
    cot_hbm,
    row_mask_hbm,
    column_mask_hbm,
    wq_hbm,
    wk_hbm,
    wv_hbm,
    wo_hbm,
    mixed_hbm,
    gtok_hbm,
    gval_hbm,
    gout_hbm,
    tokens_ref,
    cot_ref,
    tokens_t,
    cot_t,
    row_mask_ref,
    column_mask_ref,
    bias,
    mixed_ref,
    gtok_ref,
    gval_ref,
    gout_ref,
    gtok_part,
    w_full,
    wo_full,
    qkv_send,
    qkv_recv,
    g_rows,
    g_send,
    g_recv,
    out_send,
    out_recv,
    grad_send,
    grad_recv,
    row_qkv,
    row_grads,
    probs,
    attended,
    part,
    part_recv1,
    acc1,
    recv_x_first,
    recv_y_first,
    acc_x_first,
    acc_y_first,
    part_recv3,
    acc3,
    part_recv4,
    w_send_sem,
    w_recv_sem,
    a_send_sem,
    a_recv_sem,
    r_send_sem,
    r_recv_sem,
    local_sem,
):
    dp = lax.axis_index("dp")
    seq = lax.axis_index("seq")
    core = lax.rem(seq, 2)
    y = lax.rem(seq // 2, 2)
    z = seq // 4
    z_count = seq_count // 4
    positions = tokens_ref.shape[0]
    cols = positions // seq_count
    shard = wq_hbm.shape[0]
    out_shard = wo_hbm.shape[0]
    split = qkv_send.shape[2]
    half = split // HEAD_DIM
    other = 1 - dp
    x_peer = (other, seq)
    core_peer = (dp, seq + 1 - 2 * core)
    y_peer = (dp, seq + 2 - 4 * y)

    own_rows = pl.ds(pl.multiple_of(dp * shard, shard), shard)
    own_out = pl.ds(pl.multiple_of(dp * out_shard, out_shard), out_shard)
    weights_in = [
        pltpu.make_async_copy(wq_hbm, w_full.at[0, own_rows, :], local_sem.at[0]),
        pltpu.make_async_copy(wk_hbm, w_full.at[1, own_rows, :], local_sem.at[1]),
        pltpu.make_async_copy(wv_hbm, w_full.at[2, own_rows, :], local_sem.at[2]),
        pltpu.make_async_copy(wo_hbm, wo_full.at[own_out, :], local_sem.at[3]),
    ]
    others_in = [
        pltpu.make_async_copy(tokens_hbm, tokens_ref, local_sem.at[4]),
        pltpu.make_async_copy(cot_hbm, cot_ref, local_sem.at[5]),
        pltpu.make_async_copy(row_mask_hbm, row_mask_ref, local_sem.at[6]),
        pltpu.make_async_copy(column_mask_hbm, column_mask_ref, local_sem.at[7]),
    ]
    outs = [
        pltpu.make_async_copy(mixed_ref, mixed_hbm, local_sem.at[8]),
        pltpu.make_async_copy(gtok_ref, gtok_hbm, local_sem.at[9]),
        pltpu.make_async_copy(gval_ref, gval_hbm, local_sem.at[10]),
        pltpu.make_async_copy(gout_ref, gout_hbm, local_sem.at[11]),
    ]
    for copy in weights_in + others_in:
        copy.start()

    barrier = pltpu.get_barrier_semaphore()
    pl.semaphore_signal(barrier, inc=1, device_id=x_peer, device_id_type=MESH)

    @pl.loop(1, seq_count, unroll=True)
    def _(step):
        pl.semaphore_signal(
            barrier,
            inc=1,
            device_id=(dp, lax.rem(seq + step, seq_count)),
            device_id_type=MESH,
        )

    for copy in weights_in:
        copy.wait()
    pl.semaphore_wait(barrier, seq_count)

    def region(group, owner, qy, qc):
        if group == 3:
            quarter = out_shard // 4
            start = pl.multiple_of(owner * out_shard + (qy * 2 + qc) * quarter, quarter)
            return wo_full.at[pl.ds(start, quarter), :]
        quarter = shard // 4
        start = pl.multiple_of(owner * shard + (qy * 2 + qc) * quarter, quarter)
        if group == 4:
            return w_full.at[:, pl.ds(start, quarter), pl.ds(0, split)]
        return w_full.at[group, pl.ds(start, quarter), pl.ds(split, split)]

    def weight_copy(group, hop):
        if hop == 0:
            ref, peer = region(group, dp, y, core), x_peer
        elif hop == 1:
            ref, peer = region(group, other, y, core), y_peer
        elif hop == 2:
            ref, peer = region(group, other, y, core), core_peer
        else:
            ref, peer = region(group, other, 1 - y, core), core_peer
        return pltpu.make_async_remote_copy(
            src_ref=ref,
            dst_ref=ref,
            send_sem=w_send_sem.at[group, hop],
            recv_sem=w_recv_sem.at[group, hop],
            device_id=peer,
            device_id_type=MESH,
        )

    def pass_on(group):
        weight_copy(group, 0).wait_recv()
        if group + 2 < 5:
            weight_copy(group + 2, 0).start()
        weight_copy(group, 1).start()
        weight_copy(group, 2).start()

    def pass_core(group):
        weight_copy(group, 1).wait_recv()
        weight_copy(group, 3).start()

    def weights_here(group):
        weight_copy(group, 2).wait_recv()
        weight_copy(group, 3).wait_recv()

    def column_copy(src, dst, phase, step):
        target = lax.rem(seq + step, seq_count)
        there = pl.ds(pl.multiple_of(target * cols, cols), cols)
        here = pl.ds(pl.multiple_of(seq * cols, cols), cols)
        return pltpu.make_async_remote_copy(
            src_ref=src.at[:, there, :],
            dst_ref=dst.at[:, here, :],
            send_sem=a_send_sem.at[phase],
            recv_sem=a_recv_sem.at[phase],
            device_id=(dp, target),
            device_id_type=MESH,
        )

    def one(ref, index):
        return ref.at[pl.ds(index, 1)]

    def exchange(src, dst, phase):
        @pl.loop(1, seq_count, unroll=True)
        def _(step):
            column_copy(src, dst, phase, step).start()

        here = pl.ds(pl.multiple_of(seq * cols, cols), cols)
        dst[:, here, :] = src[:, here, :]

    def whole_exchange(src, dst, phase):
        many = pl.ds(0, positions - cols)
        return pltpu.make_async_remote_copy(
            src_ref=src.at[:, many, :],
            dst_ref=dst.at[:, many, :],
            send_sem=a_send_sem.at[phase],
            recv_sem=a_recv_sem.at[phase],
            device_id=core_peer,
            device_id_type=MESH,
        )

    def arrived(src, dst, phase):
        whole_exchange(src, dst, phase).wait_recv()

    def sent(src, dst, phase):
        whole_exchange(src, dst, phase).wait_send()

    weight_copy(0, 0).start()
    weight_copy(1, 0).start()

    query_pos = lax.broadcasted_iota(jnp.int32, (positions, positions), 0)
    key_pos = lax.broadcasted_iota(jnp.int32, (positions, positions), 1)
    lane = lax.broadcasted_iota(jnp.int32, (1, 2 * HEAD_DIM), 1)
    first_lanes = lane < HEAD_DIM
    keep = (first_lanes.astype(F32).astype(BF16), (lane >= HEAD_DIM).astype(F32).astype(BF16))

    def store_bias(index, seen):
        bias[index] = jnp.where(seen, 0.0, -1e30)

    row, row2 = query_pos // cols, key_pos // cols
    matching = (lax.rem(query_pos, cols) == lax.rem(key_pos, cols)) & (row2 <= row)
    store_bias(0, key_pos <= query_pos)
    store_bias(1, (key_pos <= query_pos) & ((query_pos // ROWBLK) == (key_pos // ROWBLK)))
    store_bias(2, matching)
    store_bias(3, matching & ((row // COLBLK) == (row2 // COLBLK)))

    for copy in others_in:
        copy.wait()

    def head_bias(head):
        if head < half:
            bit = row_mask_ref[0, 1, 0, head]
            return jnp.where(bit == 1, bias[0], bias[1])
        column = lax.rem(lax.broadcasted_iota(jnp.int32, (1, positions), 1), cols)
        bits = jnp.zeros((1, positions), jnp.int32)
        for index in range(cols):
            bits = jnp.where(column == index, column_mask_ref[head - half, 1, 0, index], bits)
        return jnp.where(bits == 1, bias[2], bias[3])

    def softmax(head, query, key):
        scores = dot_nt(query, key) * (1.0 / math.sqrt(HEAD_DIM)) + head_bias(head)
        weights = jnp.exp(scores - jnp.max(scores, axis=-1, keepdims=True))
        return weights * (1.0 / jnp.sum(weights, axis=-1, keepdims=True))

    def pair_of(pair):
        return pl.ds(pair * 2 * HEAD_DIM, 2 * HEAD_DIM)

    def merge(halves):
        return jnp.where(first_lanes, halves[0], halves[1]).astype(BF16)

    def forward(base, query, key, value, slot):
        outs = []
        for side in range(2):
            weights = softmax(base + side, query * keep[side], key)
            probs[slot + side] = weights
            outs.append(dot_nn(weights.astype(BF16), value))
        return merge(outs)

    def value_grad(grad, slot):
        sides = [dot_tn(probs[slot + side].astype(BF16), grad) for side in range(2)]
        return merge(sides)

    def query_key_grads(query, key, value, grad, slot):
        grads = ([], [])
        for side in range(2):
            weights = probs[slot + side]
            grad_probs = dot_nt(grad * keep[side], value)
            grad_scores = weights * (
                grad_probs - jnp.sum(weights * grad_probs, axis=-1, keepdims=True)
            )
            grad_scores = (grad_scores * (1.0 / math.sqrt(HEAD_DIM))).astype(BF16)
            grads[0].append(dot_nn(grad_scores, key))
            grads[1].append(dot_tn(grad_scores, query))
        return [merge(grad_pair) for grad_pair in grads]

    def rs_copy(which, hop):
        piece, order = which // 2, which % 2
        if hop == 0:
            src, dst, peer = part.at[which, :, :, :, 1 - core], part_recv1.at[which], core_peer
        elif hop == 1 and order == 0:
            src, dst, peer = acc1.at[which, other], recv_x_first.at[piece], x_peer
        elif hop == 1:
            src, dst, peer = acc1.at[which, :, :, 1 - y], recv_y_first.at[piece], y_peer
        elif hop == 2 and order == 0:
            src, dst, peer = acc_x_first.at[piece, :, 1 - y], part_recv3.at[which], y_peer
        elif hop == 2:
            src, dst, peer = acc_y_first.at[piece, other], part_recv3.at[which], x_peer
        else:
            z_there = lax.rem(z + hop - 2, z_count)
            src, dst = acc3.at[which, z_there], part_recv4.at[which, hop - 3]
            peer = (dp, z_there * 4 + y * 2 + core)
        return pltpu.make_async_remote_copy(
            src_ref=src,
            dst_ref=dst,
            send_sem=r_send_sem.at[which, hop],
            recv_sem=r_recv_sem.at[which, hop],
            device_id=peer,
            device_id_type=MESH,
        )

    def rs_start(piece, full):
        lanes = split // 2
        for order in range(2):
            half_piece = full[:, order * lanes : (order + 1) * lanes].astype(BF16)
            part[2 * piece + order] = half_piece.reshape(part.shape[1:])
            rs_copy(2 * piece + order, 0).start()

    def rs_next(piece, hop):
        for order in range(2):
            which = 2 * piece + order
            rs_copy(which, hop).wait_recv()
            if hop == 0:
                acc1[which] = (
                    part[which, :, :, :, core].astype(F32) + part_recv1[which].astype(F32)
                ).astype(BF16)
            elif hop == 1 and order == 0:
                acc_x_first[piece] = (
                    acc1[which, dp].astype(F32) + recv_x_first[piece].astype(F32)
                ).astype(BF16)
            elif hop == 1:
                acc_y_first[piece] = (
                    acc1[which, :, :, y].astype(F32) + recv_y_first[piece].astype(F32)
                ).astype(BF16)
            elif order == 0:
                acc3[which] = (
                    acc_x_first[piece, :, y].astype(F32) + part_recv3[which].astype(F32)
                ).astype(BF16)
            else:
                acc3[which] = (
                    acc_y_first[piece, dp].astype(F32) + part_recv3[which].astype(F32)
                ).astype(BF16)
            if hop < 2:
                rs_copy(which, hop + 1).start()
            else:
                for step in range(1, z_count):
                    rs_copy(which, 2 + step).start()

    def rs_end(piece, out, first_lane):
        for order in range(2):
            which = 2 * piece + order
            total = acc3[which, z].astype(F32)
            for step in range(1, z_count):
                rs_copy(which, 2 + step).wait_recv()
                total = total + part_recv4[which, step - 1].astype(F32)
            out[:, pl.ds(first_lane + order * (split // 2), split // 2)] = total

    def project_columns(index):
        weights_here(index)
        qkv_send[index] = dot_nn(tokens_ref[...], w_full[index, :, split:]).astype(BF16)
        exchange(one(qkv_send, index), one(qkv_recv, index), index)

    pass_on(0)
    pass_on(1)
    pass_core(0)
    pass_on(2)
    project_columns(0)
    pass_core(1)
    project_columns(1)
    pass_core(2)
    pass_on(3)
    project_columns(2)
    pass_core(3)
    pass_on(4)
    weights_here(3)
    g_send[0] = dot_nt(cot_ref[...], wo_full[split:, :]).astype(BF16)
    exchange(g_send, g_recv, 3)
    g_rows[...] = dot_nt(cot_ref[...], wo_full[:split, :]).astype(BF16)
    tokens_t[...] = tokens_ref[...].T
    cot_t[...] = cot_ref[...].T

    for index in range(3):
        arrived(one(qkv_send, index), one(qkv_recv, index), index)
    for pair in range(split // (2 * HEAD_DIM)):
        query, key, value = (qkv_recv[index, :, pair_of(pair)] for index in range(3))
        out_send[0, :, pair_of(pair)] = forward(half + 2 * pair, query, key, value, 2 * pair)
    exchange(out_send, out_recv, 4)
    pass_core(4)

    arrived(g_send, g_recv, 3)
    pairs = range(split // (2 * HEAD_DIM))
    for pair in pairs:
        grad_send[2, :, pair_of(pair)] = value_grad(g_recv[0, :, pair_of(pair)], 2 * pair)
    exchange(one(grad_send, 2), one(grad_recv, 2), 5)
    for pair in pairs:
        query, key, value = (qkv_recv[index, :, pair_of(pair)] for index in range(3))
        grads = query_key_grads(query, key, value, g_recv[0, :, pair_of(pair)], 2 * pair)
        for index in range(2):
            grad_send[index, :, pair_of(pair)] = grads[index]
    exchange(grad_send.at[pl.ds(0, 2)], grad_recv.at[pl.ds(0, 2)], 6)

    weights_here(4)
    for index in range(3):
        row_qkv[index] = dot_nn(tokens_ref[...], w_full[index, :, :split]).astype(BF16)
    for pair in pairs:
        query, key, value = (row_qkv[index, :, pair_of(pair)] for index in range(3))
        slot = half + 2 * pair
        attended[:, pair_of(pair)] = forward(2 * pair, query, key, value, slot)
        row_grads[2, :, pair_of(pair)] = value_grad(g_rows[:, pair_of(pair)], slot)
    rs_start(0, dot_nn(cot_t[...], attended[:, :split]))
    rs_start(1, dot_nn(tokens_t[...], row_grads[2]))
    arrived(out_send, out_recv, 4)
    rs_start(2, dot_nn(cot_t[...], out_recv[0]))
    rs_next(0, 0)
    arrived(one(grad_send, 2), one(grad_recv, 2), 5)
    rs_start(3, dot_nn(tokens_t[...], grad_recv[2]))
    rs_next(1, 0)

    def row_query_key(pair):
        query, key, value = (row_qkv[index, :, pair_of(pair)] for index in range(3))
        grads = query_key_grads(query, key, value, g_rows[:, pair_of(pair)], half + 2 * pair)
        for index in range(2):
            row_grads[index, :, pair_of(pair)] = grads[index]

    for pair in pairs:
        row_query_key(pair)
        if pair == 0:
            rs_next(2, 0)
            rs_next(3, 0)
    rs_next(0, 1)
    rs_next(1, 1)
    attended[:, pl.ds(split, split)] = out_recv[0]
    mixed_ref[...] = dot_nn(attended[...], wo_full[...]).astype(BF16)
    outs[0].start()
    rs_next(2, 1)
    gtok_part[...] = (
        dot_nt(row_grads[0], w_full[0, :, :split])
        + dot_nt(row_grads[1], w_full[1, :, :split])
        + dot_nt(row_grads[2], w_full[2, :, :split])
    )
    rs_next(3, 1)
    rs_next(0, 2)
    rs_next(1, 2)
    arrived(grad_send.at[pl.ds(0, 2)], grad_recv.at[pl.ds(0, 2)], 6)
    gtok_ref[...] = (
        gtok_part[...]
        + dot_nt(grad_recv[0], w_full[0, :, split:])
        + dot_nt(grad_recv[1], w_full[1, :, split:])
        + dot_nt(grad_recv[2], w_full[2, :, split:])
    ).astype(BF16)
    outs[1].start()
    rs_next(2, 2)
    rs_next(3, 2)
    for group in range(5):
        for hop in range(4):
            weight_copy(group, hop).wait_send()
    for index in range(3):
        sent(one(qkv_send, index), one(qkv_recv, index), index)
    sent(g_send, g_recv, 3)
    sent(out_send, out_recv, 4)
    sent(one(grad_send, 2), one(grad_recv, 2), 5)
    sent(grad_send.at[pl.ds(0, 2)], grad_recv.at[pl.ds(0, 2)], 6)
    rs_end(0, gout_ref, 0)
    rs_end(2, gout_ref, split)
    outs[3].start()
    rs_end(1, gval_ref, 0)
    rs_end(3, gval_ref, split)
    outs[2].start()
    for which in range(8):
        for hop in range(2 + z_count):
            rs_copy(which, hop).wait_send()
    for copy in outs:
        copy.wait()


def hand_out_kernel(*refs):
    count = (len(refs) - 2) // 3
    ins, outs, held = refs[:count], refs[count : 2 * count], refs[2 * count : 3 * count]
    in_sems, out_sems = refs[-2:]
    fetches = [
        pltpu.make_async_copy(ins[index], held[index], in_sems.at[index]) for index in range(count)
    ]
    stores = [
        pltpu.make_async_copy(held[index], outs[index], out_sems.at[index])
        for index in range(count)
    ]
    for copy in fetches:
        copy.start()
    for index in range(count):
        fetches[index].wait()
        stores[index].start()
    for copy in stores:
        copy.wait()


def hand_out(*arrays):
    count = len(arrays)
    return pl.pallas_call(
        hand_out_kernel,
        out_shape=[jax.ShapeDtypeStruct(item.shape, item.dtype) for item in arrays],
        in_specs=[pl.BlockSpec(memory_space=pltpu.HBM)] * count,
        out_specs=[pl.BlockSpec(memory_space=pltpu.HBM)] * count,
        scratch_shapes=[pltpu.VMEM(item.shape, item.dtype) for item in arrays]
        + [pltpu.SemaphoreType.DMA((count,)), pltpu.SemaphoreType.DMA((count,))],
        compiler_params=pltpu.CompilerParams(vmem_limit_bytes=64 * 1024 * 1024 - 65536),
    )(*arrays)


def fused_fits(dp_count, seq_count, tokens, row_mask, column_mask, w_query, w_out):
    positions = tokens.shape[1] * tokens.shape[2]
    return (
        tokens.shape[0] == 1
        and tokens.shape[1] == 1
        and dp_count == 2
        and seq_count % 4 == 0
        and positions % (16 * seq_count) == 0
        and w_query.shape[0] % 64 == 0
        and w_query.shape[1] % 512 == 0
        and w_out.shape[0] % 64 == 0
        and tokens.shape[3] % (16 * dp_count * seq_count) == 0
        and row_mask.shape[2] == 2
        and column_mask.shape[2] == 2
    )


def fused_body(tokens, cotangent, row_mask, column_mask, w_query, w_key, w_value, w_out):
    dp_count, seq_count = lax.axis_size("dp"), lax.axis_size("seq")
    if not fused_fits(dp_count, seq_count, tokens, row_mask, column_mask, w_query, w_out):
        return body(
            tokens, cotangent, row_mask, column_mask, w_query, w_key, w_value, w_out
        )
    positions, width = tokens.shape[1] * tokens.shape[2], tokens.shape[3]
    heads_width = w_query.shape[1]
    split = heads_width // 2
    rows = width // (dp_count * seq_count)
    z_count = seq_count // 4
    stored_row_mask = jnp.transpose(row_mask, (1, 2, 3, 0))
    stored_column_mask = jnp.transpose(column_mask, (0, 2, 3, 1))
    lead = (8, dp_count, z_count, 2)
    lanes = split // 2
    call = pl.pallas_call(
        lambda *refs: fused_kernel(dp_count, seq_count, *refs),
        out_shape=(
            jax.ShapeDtypeStruct((positions, width), BF16),
            jax.ShapeDtypeStruct((positions, width), BF16),
            jax.ShapeDtypeStruct((rows, heads_width), F32),
            jax.ShapeDtypeStruct((rows, heads_width), F32),
        ),
        in_specs=[pl.BlockSpec(memory_space=pltpu.HBM)] * 8,
        out_specs=[pl.BlockSpec(memory_space=pltpu.HBM)] * 4,
        scratch_shapes=[
            pltpu.VMEM((positions, width), BF16),
            pltpu.VMEM((positions, width), BF16),
            pltpu.VMEM((width, positions), BF16),
            pltpu.VMEM((width, positions), BF16),
            pltpu.SMEM(stored_row_mask.shape, jnp.int32),
            pltpu.SMEM(stored_column_mask.shape, jnp.int32),
            pltpu.VMEM((4, positions, positions), F32),
            pltpu.VMEM((positions, width), BF16),
            pltpu.VMEM((positions, width), BF16),
            pltpu.VMEM((rows, heads_width), F32),
            pltpu.VMEM((rows, heads_width), F32),
            pltpu.VMEM((positions, width), F32),
            pltpu.VMEM((3, width, heads_width), BF16),
            pltpu.VMEM((heads_width, width), BF16),
            pltpu.VMEM((3, positions, split), BF16),
            pltpu.VMEM((3, positions, split), BF16),
            pltpu.VMEM((positions, split), BF16),
            pltpu.VMEM((1, positions, split), BF16),
            pltpu.VMEM((1, positions, split), BF16),
            pltpu.VMEM((1, positions, split), BF16),
            pltpu.VMEM((1, positions, split), BF16),
            pltpu.VMEM((3, positions, split), BF16),
            pltpu.VMEM((3, positions, split), BF16),
            pltpu.VMEM((3, positions, split), BF16),
            pltpu.VMEM((3, positions, split), BF16),
            pltpu.VMEM((heads_width // HEAD_DIM, positions, positions), F32),
            pltpu.VMEM((positions, heads_width), BF16),
            pltpu.VMEM(lead + (2, rows, lanes), BF16),
            pltpu.VMEM(lead + (rows, lanes), BF16),
            pltpu.VMEM(lead + (rows, lanes), BF16),
            pltpu.VMEM((4, z_count, 2, rows, lanes), BF16),
            pltpu.VMEM((4, 2, z_count, rows, lanes), BF16),
            pltpu.VMEM((4, z_count, 2, rows, lanes), BF16),
            pltpu.VMEM((4, 2, z_count, rows, lanes), BF16),
            pltpu.VMEM((8, z_count, rows, lanes), BF16),
            pltpu.VMEM((8, z_count, rows, lanes), BF16),
            pltpu.VMEM((8, z_count - 1, rows, lanes), BF16),
            pltpu.SemaphoreType.DMA((5, 4)),
            pltpu.SemaphoreType.DMA((5, 4)),
            pltpu.SemaphoreType.DMA((7,)),
            pltpu.SemaphoreType.DMA((7,)),
            pltpu.SemaphoreType.DMA((8, 2 + z_count)),
            pltpu.SemaphoreType.DMA((8, 2 + z_count)),
            pltpu.SemaphoreType.DMA((12,)),
        ],
        compiler_params=pltpu.CompilerParams(
            collective_id=0, has_side_effects=True, vmem_limit_bytes=64 * 1024 * 1024 - 65536
        ),
        cost_estimate=pl.CostEstimate(
            flops=3_400_000_000, bytes_accessed=8_000_000, transcendentals=524288
        ),
    )
    mixed, grad_tokens, grad_value, grad_output = call(
        tokens.reshape(positions, width),
        cotangent.reshape(positions, width),
        stored_row_mask,
        stored_column_mask,
        w_query,
        w_key,
        w_value,
        w_out,
    )
    mixed, grad_tokens, grad_value, grad_output = hand_out(
        mixed, grad_tokens, grad_value, grad_output
    )
    return (
        mixed.reshape(tokens.shape),
        grad_tokens.reshape(tokens.shape),
        grad_value,
        jnp.transpose(grad_output),
    )


def solution(mesh):
    return jax.shard_map(
        fused_body,
        mesh=mesh,
        in_specs=(
            P("dp", "seq", None, None),
            P("dp", "seq", None, None),
            P(None, "seq", None, None),
            P(None, "seq", None, None),
            P("dp", None),
            P("dp", None),
            P("dp", None),
            P("dp", None),
        ),
        out_specs=(
            P("dp", "seq", None, None),
            P("dp", "seq", None, None),
            P(("dp", "seq"), None),
            P(None, ("dp", "seq")),
        ),
        check_vma=False,
    )
```

```python
import math

import jax
import jax.numpy as jnp
from jax import lax
from jax.experimental import pallas as pl
from jax.experimental.pallas import tpu as pltpu
from jax.sharding import PartitionSpec as P

HEAD_DIM = 64
ROWBLK = 128
COLBLK = 8


row_forms = ("blhe,bmhe->bhlm", "bhlm,bmhe->blhe")
column_forms = ("lbhe,mbhe->bhlm", "bhlm,mbhe->lbhe")
contract_last = (((1,), (1,)), ((), ()))
contract_first = (((0,), (0,)), ((), ()))


def allowed_cells(mask_blocks, block_size):
    expanded = jnp.repeat(jnp.repeat(mask_blocks, block_size, axis=-2), block_size, axis=-1)
    length = expanded.shape[-1]
    causal = jnp.arange(length)[:, None] >= jnp.arange(length)[None, :]
    return (expanded == 1) & causal


def attend(queries, key_part, value_part, allowed, forms):
    scale_factor = 1.0 / math.sqrt(queries.shape[-1])
    scores = (
        jnp.einsum(forms[0], queries.astype(jnp.float32), key_part.astype(jnp.float32))
        * scale_factor
    )
    scores = jnp.where(allowed, scores, -1e30)
    highest = lax.stop_gradient(jnp.max(scores, axis=-1, keepdims=True))
    weights = jnp.exp(scores - highest)
    weights = weights / jnp.sum(weights, axis=-1, keepdims=True)
    rounded = lax.optimization_barrier(weights.astype(jnp.bfloat16)).astype(jnp.float32)
    result = jnp.einsum(forms[1], rounded, value_part.astype(jnp.float32))
    return result.astype(jnp.bfloat16)


def body(tokens, cotangent, row_mask, column_mask, w_query, w_key, w_value, w_out):
    rows_here = tokens.shape[1]
    grid_cols = tokens.shape[2]
    width = tokens.shape[3]
    heads_width = w_query.shape[1]
    half = heads_width // HEAD_DIM // 2
    split = half * HEAD_DIM
    flat = tokens.reshape(-1, width)
    cot_flat = cotangent.reshape(-1, width)
    token_count = flat.shape[0]
    seq_count = lax.axis_size("seq")
    grid_rows = rows_here * seq_count
    cols_here = grid_cols // seq_count
    full_query, full_key, full_value, full_out = (
        lax.all_gather(w_query, "dp", axis=0, tiled=True),
        lax.all_gather(w_key, "dp", axis=0, tiled=True),
        lax.all_gather(w_value, "dp", axis=0, tiled=True),
        lax.all_gather(w_out, "dp", axis=0, tiled=True),
    )
    proj_query = jnp.dot(flat, full_query, preferred_element_type=jnp.float32)
    proj_key = jnp.dot(flat, full_key, preferred_element_type=jnp.float32)
    proj_value = jnp.dot(flat, full_value, preferred_element_type=jnp.float32)
    query_flat = proj_query.astype(jnp.bfloat16)
    key_flat = proj_key.astype(jnp.bfloat16)
    value_flat = proj_value.astype(jnp.bfloat16)
    row_allowed = allowed_cells(jnp.transpose(row_mask, (1, 0, 2, 3)), ROWBLK)
    column_allowed = allowed_cells(jnp.transpose(column_mask, (1, 0, 2, 3)), COLBLK)

    def row_core(first, second, third):
        return attend(first, second, third, row_allowed, row_forms)

    def column_core(first, second, third):
        return attend(first, second, third, column_allowed, column_forms)

    def row_heads(matrix):
        return matrix[:, :split].reshape(rows_here, grid_cols, half, HEAD_DIM)

    def column_heads(matrix):
        return matrix[:, split:].reshape(rows_here, grid_cols, split)

    def as_columns(block):
        return block.reshape(grid_rows, cols_here, half, HEAD_DIM)

    def joined(row_part, col_part):
        return jnp.concatenate(
            [row_part.reshape(token_count, split), col_part.reshape(token_count, split)], axis=1
        )

    col_query, col_key, col_value = (
        lax.all_to_all(column_heads(query_flat), "seq", split_axis=1, concat_axis=0, tiled=True),
        lax.all_to_all(column_heads(key_flat), "seq", split_axis=1, concat_axis=0, tiled=True),
        lax.all_to_all(column_heads(value_flat), "seq", split_axis=1, concat_axis=0, tiled=True),
    )
    row_out, row_back = jax.vjp(
        row_core, row_heads(query_flat), row_heads(key_flat), row_heads(value_flat)
    )
    column_out, column_back = jax.vjp(
        column_core, as_columns(col_query), as_columns(col_key), as_columns(col_value)
    )
    returned = lax.all_to_all(
        column_out.reshape(grid_rows, cols_here, split),
        "seq",
        split_axis=0,
        concat_axis=1,
        tiled=True,
    )
    attended = joined(row_out, returned)
    mixed = jnp.dot(attended, full_out, preferred_element_type=jnp.float32)
    grad_heads = lax.dot_general(
        cot_flat, full_out, contract_last, preferred_element_type=jnp.float32
    )
    mixed = mixed.astype(jnp.bfloat16).reshape(tokens.shape)
    grad_heads = grad_heads.astype(jnp.bfloat16)
    row_grads = row_back(grad_heads[:, :split].reshape(rows_here, grid_cols, half, HEAD_DIM))
    grad_columns = lax.all_to_all(
        grad_heads[:, split:].reshape(rows_here, grid_cols, split),
        "seq",
        split_axis=1,
        concat_axis=0,
        tiled=True,
    )
    col_grads = column_back(as_columns(grad_columns))
    back_grads = (
        lax.all_to_all(
            col_grads[0].reshape(grid_rows, cols_here, split),
            "seq",
            split_axis=0,
            concat_axis=1,
            tiled=True,
        ),
        lax.all_to_all(
            col_grads[1].reshape(grid_rows, cols_here, split),
            "seq",
            split_axis=0,
            concat_axis=1,
            tiled=True,
        ),
        lax.all_to_all(
            col_grads[2].reshape(grid_rows, cols_here, split),
            "seq",
            split_axis=0,
            concat_axis=1,
            tiled=True,
        ),
    )
    grad_query = joined(row_grads[0], back_grads[0])
    grad_key = joined(row_grads[1], back_grads[1])
    grad_val = joined(row_grads[2], back_grads[2])
    grad_tokens = (
        lax.dot_general(grad_query, full_query, contract_last, preferred_element_type=jnp.float32)
        + lax.dot_general(grad_key, full_key, contract_last, preferred_element_type=jnp.float32)
        + lax.dot_general(grad_val, full_value, contract_last, preferred_element_type=jnp.float32)
    )
    grad_tokens = grad_tokens.astype(jnp.bfloat16).reshape(tokens.shape)
    summed = lax.psum_scatter(
        jnp.concatenate(
            [
                lax.dot_general(flat, grad_val, contract_first, preferred_element_type=jnp.float32),
                lax.dot_general(
                    cot_flat, attended, contract_first, preferred_element_type=jnp.float32
                ),
            ],
            axis=1,
        ),
        ("dp", "seq"),
        scatter_dimension=0,
        tiled=True,
    )
    grad_value = summed[:, :heads_width]
    grad_output = jnp.transpose(summed[:, heads_width:])
    return (mixed, grad_tokens, grad_value, grad_output)


MESH = pl.DeviceIdType.MESH
F32 = jnp.float32
BF16 = jnp.bfloat16


def dot_nn(a, b):
    return jnp.dot(a, b, preferred_element_type=F32)


def dot_nt(a, b):
    return lax.dot_general(a, b, contract_last, preferred_element_type=F32)


def dot_tn(a, b):
    return lax.dot_general(a, b, contract_first, preferred_element_type=F32)


def fused_kernel(
    dp_count,
    seq_count,
    tokens_hbm,
    cot_hbm,
    row_mask_hbm,
    column_mask_hbm,
    wq_hbm,
    wk_hbm,
    wv_hbm,
    wo_hbm,
    mixed_hbm,
    gtok_hbm,
    gval_hbm,
    gout_hbm,
    tokens_ref,
    cot_ref,
    tokens_t,
    cot_t,
    row_mask_ref,
    column_mask_ref,
    bias,
    mixed_ref,
    gtok_ref,
    gval_ref,
    gout_ref,
    gtok_part,
    w_full,
    wo_full,
    qkv_send,
    qkv_recv,
    g_rows,
    g_send,
    g_recv,
    out_send,
    out_recv,
    grad_send,
    grad_recv,
    row_qkv,
    row_grads,
    probs,
    attended,
    part,
    part_recv1,
    acc1,
    recv_x_first,
    recv_y_first,
    acc_x_first,
    acc_y_first,
    part_recv3,
    acc3,
    part_recv4,
    w_send_sem,
    w_recv_sem,
    a_send_sem,
    a_recv_sem,
    r_send_sem,
    r_recv_sem,
    local_sem,
):
    dp = lax.axis_index("dp")
    seq = lax.axis_index("seq")
    core = lax.rem(seq, 2)
    y = lax.rem(seq // 2, 2)
    z = seq // 4
    z_count = seq_count // 4
    positions = tokens_ref.shape[0]
    cols = positions // seq_count
    shard = wq_hbm.shape[0]
    out_shard = wo_hbm.shape[0]
    split = qkv_send.shape[2]
    half = split // HEAD_DIM
    other = 1 - dp
    x_peer = (other, seq)
    core_peer = (dp, seq + 1 - 2 * core)
    y_peer = (dp, seq + 2 - 4 * y)

    own_rows = pl.ds(pl.multiple_of(dp * shard, shard), shard)
    own_out = pl.ds(pl.multiple_of(dp * out_shard, out_shard), out_shard)
    weights_in = [
        pltpu.make_async_copy(wq_hbm, w_full.at[0, own_rows, :], local_sem.at[0]),
        pltpu.make_async_copy(wk_hbm, w_full.at[1, own_rows, :], local_sem.at[1]),
        pltpu.make_async_copy(wv_hbm, w_full.at[2, own_rows, :], local_sem.at[2]),
        pltpu.make_async_copy(wo_hbm, wo_full.at[own_out, :], local_sem.at[3]),
    ]
    others_in = [
        pltpu.make_async_copy(tokens_hbm, tokens_ref, local_sem.at[4]),
        pltpu.make_async_copy(cot_hbm, cot_ref, local_sem.at[5]),
        pltpu.make_async_copy(row_mask_hbm, row_mask_ref, local_sem.at[6]),
        pltpu.make_async_copy(column_mask_hbm, column_mask_ref, local_sem.at[7]),
    ]
    outs = [
        pltpu.make_async_copy(mixed_ref, mixed_hbm, local_sem.at[8]),
        pltpu.make_async_copy(gtok_ref, gtok_hbm, local_sem.at[9]),
        pltpu.make_async_copy(gval_ref, gval_hbm, local_sem.at[10]),
        pltpu.make_async_copy(gout_ref, gout_hbm, local_sem.at[11]),
    ]
    for copy in weights_in + others_in:
        copy.start()

    barrier = pltpu.get_barrier_semaphore()
    pl.semaphore_signal(barrier, inc=1, device_id=x_peer, device_id_type=MESH)

    @pl.loop(1, seq_count, unroll=True)
    def _(step):
        pl.semaphore_signal(
            barrier,
            inc=1,
            device_id=(dp, lax.rem(seq + step, seq_count)),
            device_id_type=MESH,
        )

    for copy in weights_in:
        copy.wait()
    pl.semaphore_wait(barrier, seq_count)

    def region(group, owner, qy, qc):
        if group == 4:
            quarter = out_shard // 4
            start = pl.multiple_of(owner * out_shard + (qy * 2 + qc) * quarter, quarter)
            return wo_full.at[pl.ds(start, quarter), :]
        quarter = shard // 4
        start = pl.multiple_of(owner * shard + (qy * 2 + qc) * quarter, quarter)
        if group == 3:
            return w_full.at[:, pl.ds(start, quarter), pl.ds(0, split)]
        return w_full.at[group, pl.ds(start, quarter), pl.ds(split, split)]

    def weight_copy(group, hop):
        if hop == 0:
            ref, peer = region(group, dp, y, core), x_peer
        elif hop == 1:
            ref, peer = region(group, other, y, core), y_peer
        elif hop == 2:
            ref, peer = region(group, other, y, core), core_peer
        else:
            ref, peer = region(group, other, 1 - y, core), core_peer
        return pltpu.make_async_remote_copy(
            src_ref=ref,
            dst_ref=ref,
            send_sem=w_send_sem.at[group, hop],
            recv_sem=w_recv_sem.at[group, hop],
            device_id=peer,
            device_id_type=MESH,
        )

    def pass_on(group):
        weight_copy(group, 0).wait_recv()
        if group + 2 < 5:
            weight_copy(group + 2, 0).start()
        weight_copy(group, 1).start()
        weight_copy(group, 2).start()

    def pass_core(group):
        weight_copy(group, 1).wait_recv()
        weight_copy(group, 3).start()

    def weights_here(group):
        weight_copy(group, 2).wait_recv()
        weight_copy(group, 3).wait_recv()

    def column_copy(src, dst, phase, step):
        target = lax.rem(seq + step, seq_count)
        there = pl.ds(pl.multiple_of(target * cols, cols), cols)
        here = pl.ds(pl.multiple_of(seq * cols, cols), cols)
        return pltpu.make_async_remote_copy(
            src_ref=src.at[:, there, :],
            dst_ref=dst.at[:, here, :],
            send_sem=a_send_sem.at[phase],
            recv_sem=a_recv_sem.at[phase],
            device_id=(dp, target),
            device_id_type=MESH,
        )

    def one(ref, index):
        return ref.at[pl.ds(index, 1)]

    def exchange(src, dst, phase):
        @pl.loop(1, seq_count, unroll=True)
        def _(step):
            column_copy(src, dst, phase, step).start()

        here = pl.ds(pl.multiple_of(seq * cols, cols), cols)
        dst[:, here, :] = src[:, here, :]

    def whole_exchange(src, dst, phase):
        many = pl.ds(0, positions - cols)
        return pltpu.make_async_remote_copy(
            src_ref=src.at[:, many, :],
            dst_ref=dst.at[:, many, :],
            send_sem=a_send_sem.at[phase],
            recv_sem=a_recv_sem.at[phase],
            device_id=core_peer,
            device_id_type=MESH,
        )

    def arrived(src, dst, phase):
        whole_exchange(src, dst, phase).wait_recv()

    def sent(src, dst, phase):
        whole_exchange(src, dst, phase).wait_send()

    weight_copy(0, 0).start()
    weight_copy(1, 0).start()

    query_pos = lax.broadcasted_iota(jnp.int32, (positions, positions), 0)
    key_pos = lax.broadcasted_iota(jnp.int32, (positions, positions), 1)
    lane = lax.broadcasted_iota(jnp.int32, (1, 2 * HEAD_DIM), 1)
    first_lanes = lane < HEAD_DIM
    keep = (first_lanes.astype(F32).astype(BF16), (lane >= HEAD_DIM).astype(F32).astype(BF16))

    def store_bias(index, seen):
        bias[index] = jnp.where(seen, 0.0, -1e30)

    row, row2 = query_pos // cols, key_pos // cols
    matching = (lax.rem(query_pos, cols) == lax.rem(key_pos, cols)) & (row2 <= row)
    store_bias(0, key_pos <= query_pos)
    store_bias(1, (key_pos <= query_pos) & ((query_pos // ROWBLK) == (key_pos // ROWBLK)))
    store_bias(2, matching)
    store_bias(3, matching & ((row // COLBLK) == (row2 // COLBLK)))

    for copy in others_in:
        copy.wait()

    def head_bias(head):
        if head < half:
            bit = row_mask_ref[0, 1, 0, head]
            return jnp.where(bit == 1, bias[0], bias[1])
        column = lax.rem(lax.broadcasted_iota(jnp.int32, (1, positions), 1), cols)
        bits = jnp.zeros((1, positions), jnp.int32)
        for index in range(cols):
            bits = jnp.where(column == index, column_mask_ref[head - half, 1, 0, index], bits)
        return jnp.where(bits == 1, bias[2], bias[3])

    def softmax(head, query, key):
        scores = dot_nt(query, key) * (1.0 / math.sqrt(HEAD_DIM)) + head_bias(head)
        weights = jnp.exp(scores - jnp.max(scores, axis=-1, keepdims=True))
        return weights * (1.0 / jnp.sum(weights, axis=-1, keepdims=True))

    def pair_of(pair):
        return pl.ds(pair * 2 * HEAD_DIM, 2 * HEAD_DIM)

    def merge(halves):
        return jnp.where(first_lanes, halves[0], halves[1]).astype(BF16)

    def forward(base, query, key, value, slot):
        outs = []
        for side in range(2):
            weights = softmax(base + side, query * keep[side], key)
            probs[slot + side] = weights
            outs.append(dot_nn(weights.astype(BF16), value))
        return merge(outs)

    def value_grad(grad, slot):
        sides = [dot_tn(probs[slot + side].astype(BF16), grad) for side in range(2)]
        return merge(sides)

    def query_key_grads(query, key, value, grad, slot):
        grads = ([], [])
        for side in range(2):
            weights = probs[slot + side]
            grad_probs = dot_nt(grad * keep[side], value)
            grad_scores = weights * (
                grad_probs - jnp.sum(weights * grad_probs, axis=-1, keepdims=True)
            )
            grad_scores = (grad_scores * (1.0 / math.sqrt(HEAD_DIM))).astype(BF16)
            grads[0].append(dot_nn(grad_scores, key))
            grads[1].append(dot_tn(grad_scores, query))
        return [merge(grad_pair) for grad_pair in grads]

    def rs_copy(which, hop):
        piece, order = which // 2, which % 2
        if hop == 0:
            src, dst, peer = part.at[which, :, :, :, 1 - core], part_recv1.at[which], core_peer
        elif hop == 1 and order == 0:
            src, dst, peer = acc1.at[which, other], recv_x_first.at[piece], x_peer
        elif hop == 1:
            src, dst, peer = acc1.at[which, :, :, 1 - y], recv_y_first.at[piece], y_peer
        elif hop == 2 and order == 0:
            src, dst, peer = acc_x_first.at[piece, :, 1 - y], part_recv3.at[which], y_peer
        elif hop == 2:
            src, dst, peer = acc_y_first.at[piece, other], part_recv3.at[which], x_peer
        else:
            z_there = lax.rem(z + hop - 2, z_count)
            src, dst = acc3.at[which, z_there], part_recv4.at[which, hop - 3]
            peer = (dp, z_there * 4 + y * 2 + core)
        return pltpu.make_async_remote_copy(
            src_ref=src,
            dst_ref=dst,
            send_sem=r_send_sem.at[which, hop],
            recv_sem=r_recv_sem.at[which, hop],
            device_id=peer,
            device_id_type=MESH,
        )

    def rs_start(piece, full):
        lanes = split // 2
        for order in range(2):
            half_piece = full[:, order * lanes : (order + 1) * lanes].astype(BF16)
            part[2 * piece + order] = half_piece.reshape(part.shape[1:])
            rs_copy(2 * piece + order, 0).start()

    def rs_next(piece, hop):
        for order in range(2):
            which = 2 * piece + order
            rs_copy(which, hop).wait_recv()
            if hop == 0:
                acc1[which] = (
                    part[which, :, :, :, core].astype(F32) + part_recv1[which].astype(F32)
                ).astype(BF16)
            elif hop == 1 and order == 0:
                acc_x_first[piece] = (
                    acc1[which, dp].astype(F32) + recv_x_first[piece].astype(F32)
                ).astype(BF16)
            elif hop == 1:
                acc_y_first[piece] = (
                    acc1[which, :, :, y].astype(F32) + recv_y_first[piece].astype(F32)
                ).astype(BF16)
            elif order == 0:
                acc3[which] = (
                    acc_x_first[piece, :, y].astype(F32) + part_recv3[which].astype(F32)
                ).astype(BF16)
            else:
                acc3[which] = (
                    acc_y_first[piece, dp].astype(F32) + part_recv3[which].astype(F32)
                ).astype(BF16)
            if hop < 2:
                rs_copy(which, hop + 1).start()
            else:
                for step in range(1, z_count):
                    rs_copy(which, 2 + step).start()

    def rs_end(piece, out, first_lane):
        for order in range(2):
            which = 2 * piece + order
            total = acc3[which, z].astype(F32)
            for step in range(1, z_count):
                rs_copy(which, 2 + step).wait_recv()
                total = total + part_recv4[which, step - 1].astype(F32)
            out[:, pl.ds(first_lane + order * (split // 2), split // 2)] = total

    def project_columns(index):
        weights_here(index)
        qkv_send[index] = dot_nn(tokens_ref[...], w_full[index, :, split:]).astype(BF16)
        exchange(one(qkv_send, index), one(qkv_recv, index), index)

    pairs = range(split // (2 * HEAD_DIM))

    def row_forward(pair):
        query, key, value = (row_qkv[index, :, pair_of(pair)] for index in range(3))
        attended[:, pair_of(pair)] = forward(2 * pair, query, key, value, half + 2 * pair)

    pass_on(0)
    pass_on(1)
    pass_core(0)
    pass_on(2)
    project_columns(0)
    pass_core(1)
    project_columns(1)
    pass_core(2)
    pass_on(3)
    project_columns(2)
    tokens_t[...] = tokens_ref[...].T
    pass_core(3)
    pass_on(4)
    cot_t[...] = cot_ref[...].T
    weights_here(3)
    for index in range(3):
        row_qkv[index] = dot_nn(tokens_ref[...], w_full[index, :, :split]).astype(BF16)
    pass_core(4)
    row_forward(0)
    weights_here(4)
    g_send[0] = dot_nt(cot_ref[...], wo_full[split:, :]).astype(BF16)
    exchange(g_send, g_recv, 3)
    g_rows[...] = dot_nt(cot_ref[...], wo_full[:split, :]).astype(BF16)
    for pair in pairs[1:]:
        row_forward(pair)

    for index in range(3):
        arrived(one(qkv_send, index), one(qkv_recv, index), index)
    for pair in pairs:
        query, key, value = (qkv_recv[index, :, pair_of(pair)] for index in range(3))
        out_send[0, :, pair_of(pair)] = forward(half + 2 * pair, query, key, value, 2 * pair)
    exchange(out_send, out_recv, 4)

    arrived(g_send, g_recv, 3)
    for pair in pairs:
        grad_send[2, :, pair_of(pair)] = value_grad(g_recv[0, :, pair_of(pair)], 2 * pair)
    exchange(one(grad_send, 2), one(grad_recv, 2), 5)
    for pair in pairs:
        query, key, value = (qkv_recv[index, :, pair_of(pair)] for index in range(3))
        grads = query_key_grads(query, key, value, g_recv[0, :, pair_of(pair)], 2 * pair)
        for index in range(2):
            grad_send[index, :, pair_of(pair)] = grads[index]
    exchange(grad_send.at[pl.ds(0, 2)], grad_recv.at[pl.ds(0, 2)], 6)

    for pair in pairs:
        row_grads[2, :, pair_of(pair)] = value_grad(g_rows[:, pair_of(pair)], half + 2 * pair)
    rs_start(1, dot_nn(tokens_t[...], row_grads[2]))
    rs_start(0, dot_nn(cot_t[...], attended[:, :split]))
    arrived(out_send, out_recv, 4)
    rs_start(2, dot_nn(cot_t[...], out_recv[0]))
    rs_next(1, 0)
    arrived(one(grad_send, 2), one(grad_recv, 2), 5)
    rs_start(3, dot_nn(tokens_t[...], grad_recv[2]))
    rs_next(0, 0)

    def row_query_key(pair):
        query, key, value = (row_qkv[index, :, pair_of(pair)] for index in range(3))
        grads = query_key_grads(query, key, value, g_rows[:, pair_of(pair)], half + 2 * pair)
        for index in range(2):
            row_grads[index, :, pair_of(pair)] = grads[index]

    for pair in pairs:
        row_query_key(pair)
        if pair == 0:
            rs_next(2, 0)
            rs_next(3, 0)
    rs_next(0, 1)
    rs_next(1, 1)
    attended[:, pl.ds(split, split)] = out_recv[0]
    mixed_ref[...] = dot_nn(attended[...], wo_full[...]).astype(BF16)
    outs[0].start()
    rs_next(2, 1)
    gtok_part[...] = (
        dot_nt(row_grads[0], w_full[0, :, :split])
        + dot_nt(row_grads[1], w_full[1, :, :split])
        + dot_nt(row_grads[2], w_full[2, :, :split])
    )
    rs_next(3, 1)
    rs_next(0, 2)
    rs_next(1, 2)
    arrived(grad_send.at[pl.ds(0, 2)], grad_recv.at[pl.ds(0, 2)], 6)
    gtok_ref[...] = (
        gtok_part[...]
        + dot_nt(grad_recv[0], w_full[0, :, split:])
        + dot_nt(grad_recv[1], w_full[1, :, split:])
        + dot_nt(grad_recv[2], w_full[2, :, split:])
    ).astype(BF16)
    outs[1].start()
    rs_next(2, 2)
    rs_next(3, 2)
    for group in range(5):
        for hop in range(4):
            weight_copy(group, hop).wait_send()
    for index in range(3):
        sent(one(qkv_send, index), one(qkv_recv, index), index)
    sent(g_send, g_recv, 3)
    sent(out_send, out_recv, 4)
    sent(one(grad_send, 2), one(grad_recv, 2), 5)
    sent(grad_send.at[pl.ds(0, 2)], grad_recv.at[pl.ds(0, 2)], 6)
    rs_end(0, gout_ref, 0)
    rs_end(2, gout_ref, split)
    outs[3].start()
    rs_end(1, gval_ref, 0)
    rs_end(3, gval_ref, split)
    outs[2].start()
    for which in range(8):
        for hop in range(2 + z_count):
            rs_copy(which, hop).wait_send()
    for copy in outs:
        copy.wait()


def hand_out_kernel(*refs):
    count = (len(refs) - 2) // 3
    ins, outs, held = refs[:count], refs[count : 2 * count], refs[2 * count : 3 * count]
    in_sems, out_sems = refs[-2:]
    fetches = [
        pltpu.make_async_copy(ins[index], held[index], in_sems.at[index]) for index in range(count)
    ]
    stores = [
        pltpu.make_async_copy(held[index], outs[index], out_sems.at[index])
        for index in range(count)
    ]
    for copy in fetches:
        copy.start()
    for index in range(count):
        fetches[index].wait()
        stores[index].start()
    for copy in stores:
        copy.wait()


def hand_out(*arrays):
    count = len(arrays)
    return pl.pallas_call(
        hand_out_kernel,
        out_shape=[jax.ShapeDtypeStruct(item.shape, item.dtype) for item in arrays],
        in_specs=[pl.BlockSpec(memory_space=pltpu.HBM)] * count,
        out_specs=[pl.BlockSpec(memory_space=pltpu.HBM)] * count,
        scratch_shapes=[pltpu.VMEM(item.shape, item.dtype) for item in arrays]
        + [pltpu.SemaphoreType.DMA((count,)), pltpu.SemaphoreType.DMA((count,))],
        compiler_params=pltpu.CompilerParams(vmem_limit_bytes=64 * 1024 * 1024 - 65536),
    )(*arrays)


def fused_fits(dp_count, seq_count, tokens, row_mask, column_mask, w_query, w_out):
    positions = tokens.shape[1] * tokens.shape[2]
    return (
        tokens.shape[0] == 1
        and tokens.shape[1] == 1
        and dp_count == 2
        and seq_count % 4 == 0
        and positions % (16 * seq_count) == 0
        and w_query.shape[0] % 64 == 0
        and w_query.shape[1] % 512 == 0
        and w_out.shape[0] % 64 == 0
        and tokens.shape[3] % (16 * dp_count * seq_count) == 0
        and row_mask.shape[2] == 2
        and column_mask.shape[2] == 2
    )


def fused_body(tokens, cotangent, row_mask, column_mask, w_query, w_key, w_value, w_out):
    dp_count, seq_count = lax.axis_size("dp"), lax.axis_size("seq")
    if not fused_fits(dp_count, seq_count, tokens, row_mask, column_mask, w_query, w_out):
        return body(
            tokens, cotangent, row_mask, column_mask, w_query, w_key, w_value, w_out
        )
    positions, width = tokens.shape[1] * tokens.shape[2], tokens.shape[3]
    heads_width = w_query.shape[1]
    split = heads_width // 2
    rows = width // (dp_count * seq_count)
    z_count = seq_count // 4
    stored_row_mask = jnp.transpose(row_mask, (1, 2, 3, 0))
    stored_column_mask = jnp.transpose(column_mask, (0, 2, 3, 1))
    lead = (8, dp_count, z_count, 2)
    lanes = split // 2
    call = pl.pallas_call(
        lambda *refs: fused_kernel(dp_count, seq_count, *refs),
        out_shape=(
            jax.ShapeDtypeStruct((positions, width), BF16),
            jax.ShapeDtypeStruct((positions, width), BF16),
            jax.ShapeDtypeStruct((rows, heads_width), F32),
            jax.ShapeDtypeStruct((rows, heads_width), F32),
        ),
        in_specs=[pl.BlockSpec(memory_space=pltpu.HBM)] * 8,
        out_specs=[pl.BlockSpec(memory_space=pltpu.HBM)] * 4,
        scratch_shapes=[
            pltpu.VMEM((positions, width), BF16),
            pltpu.VMEM((positions, width), BF16),
            pltpu.VMEM((width, positions), BF16),
            pltpu.VMEM((width, positions), BF16),
            pltpu.SMEM(stored_row_mask.shape, jnp.int32),
            pltpu.SMEM(stored_column_mask.shape, jnp.int32),
            pltpu.VMEM((4, positions, positions), F32),
            pltpu.VMEM((positions, width), BF16),
            pltpu.VMEM((positions, width), BF16),
            pltpu.VMEM((rows, heads_width), F32),
            pltpu.VMEM((rows, heads_width), F32),
            pltpu.VMEM((positions, width), F32),
            pltpu.VMEM((3, width, heads_width), BF16),
            pltpu.VMEM((heads_width, width), BF16),
            pltpu.VMEM((3, positions, split), BF16),
            pltpu.VMEM((3, positions, split), BF16),
            pltpu.VMEM((positions, split), BF16),
            pltpu.VMEM((1, positions, split), BF16),
            pltpu.VMEM((1, positions, split), BF16),
            pltpu.VMEM((1, positions, split), BF16),
            pltpu.VMEM((1, positions, split), BF16),
            pltpu.VMEM((3, positions, split), BF16),
            pltpu.VMEM((3, positions, split), BF16),
            pltpu.VMEM((3, positions, split), BF16),
            pltpu.VMEM((3, positions, split), BF16),
            pltpu.VMEM((heads_width // HEAD_DIM, positions, positions), F32),
            pltpu.VMEM((positions, heads_width), BF16),
            pltpu.VMEM(lead + (2, rows, lanes), BF16),
            pltpu.VMEM(lead + (rows, lanes), BF16),
            pltpu.VMEM(lead + (rows, lanes), BF16),
            pltpu.VMEM((4, z_count, 2, rows, lanes), BF16),
            pltpu.VMEM((4, 2, z_count, rows, lanes), BF16),
            pltpu.VMEM((4, z_count, 2, rows, lanes), BF16),
            pltpu.VMEM((4, 2, z_count, rows, lanes), BF16),
            pltpu.VMEM((8, z_count, rows, lanes), BF16),
            pltpu.VMEM((8, z_count, rows, lanes), BF16),
            pltpu.VMEM((8, z_count - 1, rows, lanes), BF16),
            pltpu.SemaphoreType.DMA((5, 4)),
            pltpu.SemaphoreType.DMA((5, 4)),
            pltpu.SemaphoreType.DMA((7,)),
            pltpu.SemaphoreType.DMA((7,)),
            pltpu.SemaphoreType.DMA((8, 2 + z_count)),
            pltpu.SemaphoreType.DMA((8, 2 + z_count)),
            pltpu.SemaphoreType.DMA((12,)),
        ],
        compiler_params=pltpu.CompilerParams(
            collective_id=0, has_side_effects=True, vmem_limit_bytes=64 * 1024 * 1024 - 65536
        ),
        cost_estimate=pl.CostEstimate(
            flops=3_400_000_000, bytes_accessed=8_000_000, transcendentals=524288
        ),
    )
    mixed, grad_tokens, grad_value, grad_output = call(
        tokens.reshape(positions, width),
        cotangent.reshape(positions, width),
        stored_row_mask,
        stored_column_mask,
        w_query,
        w_key,
        w_value,
        w_out,
    )
    mixed, grad_tokens, grad_value, grad_output = hand_out(
        mixed, grad_tokens, grad_value, grad_output
    )
    return (
        mixed.reshape(tokens.shape),
        grad_tokens.reshape(tokens.shape),
        grad_value,
        jnp.transpose(grad_output),
    )


def solution(mesh):
    return jax.shard_map(
        fused_body,
        mesh=mesh,
        in_specs=(
            P("dp", "seq", None, None),
            P("dp", "seq", None, None),
            P(None, "seq", None, None),
            P(None, "seq", None, None),
            P("dp", None),
            P("dp", None),
            P("dp", None),
            P("dp", None),
        ),
        out_specs=(
            P("dp", "seq", None, None),
            P("dp", "seq", None, None),
            P(("dp", "seq"), None),
            P(None, ("dp", "seq")),
        ),
        check_vma=False,
    )
```

```python
import math

import jax
import jax.numpy as jnp
from jax import lax
from jax.experimental import pallas as pl
from jax.experimental.pallas import tpu as pltpu
from jax.sharding import PartitionSpec as P

HEAD_DIM = 64
ROWBLK = 128
COLBLK = 8


row_forms = ("blhe,bmhe->bhlm", "bhlm,bmhe->blhe")
column_forms = ("lbhe,mbhe->bhlm", "bhlm,mbhe->lbhe")
contract_last = (((1,), (1,)), ((), ()))
contract_first = (((0,), (0,)), ((), ()))


def allowed_cells(mask_blocks, block_size):
    expanded = jnp.repeat(jnp.repeat(mask_blocks, block_size, axis=-2), block_size, axis=-1)
    length = expanded.shape[-1]
    causal = jnp.arange(length)[:, None] >= jnp.arange(length)[None, :]
    return (expanded == 1) & causal


def attend(queries, key_part, value_part, allowed, forms):
    scale_factor = 1.0 / math.sqrt(queries.shape[-1])
    scores = (
        jnp.einsum(forms[0], queries.astype(jnp.float32), key_part.astype(jnp.float32))
        * scale_factor
    )
    scores = jnp.where(allowed, scores, -1e30)
    highest = lax.stop_gradient(jnp.max(scores, axis=-1, keepdims=True))
    weights = jnp.exp(scores - highest)
    weights = weights / jnp.sum(weights, axis=-1, keepdims=True)
    rounded = lax.optimization_barrier(weights.astype(jnp.bfloat16)).astype(jnp.float32)
    result = jnp.einsum(forms[1], rounded, value_part.astype(jnp.float32))
    return result.astype(jnp.bfloat16)


def body(tokens, cotangent, row_mask, column_mask, w_query, w_key, w_value, w_out):
    rows_here = tokens.shape[1]
    grid_cols = tokens.shape[2]
    width = tokens.shape[3]
    heads_width = w_query.shape[1]
    half = heads_width // HEAD_DIM // 2
    split = half * HEAD_DIM
    flat = tokens.reshape(-1, width)
    cot_flat = cotangent.reshape(-1, width)
    token_count = flat.shape[0]
    seq_count = lax.axis_size("seq")
    grid_rows = rows_here * seq_count
    cols_here = grid_cols // seq_count
    full_query, full_key, full_value, full_out = (
        lax.all_gather(w_query, "dp", axis=0, tiled=True),
        lax.all_gather(w_key, "dp", axis=0, tiled=True),
        lax.all_gather(w_value, "dp", axis=0, tiled=True),
        lax.all_gather(w_out, "dp", axis=0, tiled=True),
    )
    proj_query = jnp.dot(flat, full_query, preferred_element_type=jnp.float32)
    proj_key = jnp.dot(flat, full_key, preferred_element_type=jnp.float32)
    proj_value = jnp.dot(flat, full_value, preferred_element_type=jnp.float32)
    query_flat = proj_query.astype(jnp.bfloat16)
    key_flat = proj_key.astype(jnp.bfloat16)
    value_flat = proj_value.astype(jnp.bfloat16)
    row_allowed = allowed_cells(jnp.transpose(row_mask, (1, 0, 2, 3)), ROWBLK)
    column_allowed = allowed_cells(jnp.transpose(column_mask, (1, 0, 2, 3)), COLBLK)

    def row_core(first, second, third):
        return attend(first, second, third, row_allowed, row_forms)

    def column_core(first, second, third):
        return attend(first, second, third, column_allowed, column_forms)

    def row_heads(matrix):
        return matrix[:, :split].reshape(rows_here, grid_cols, half, HEAD_DIM)

    def column_heads(matrix):
        return matrix[:, split:].reshape(rows_here, grid_cols, split)

    def as_columns(block):
        return block.reshape(grid_rows, cols_here, half, HEAD_DIM)

    def joined(row_part, col_part):
        return jnp.concatenate(
            [row_part.reshape(token_count, split), col_part.reshape(token_count, split)], axis=1
        )

    col_query, col_key, col_value = (
        lax.all_to_all(column_heads(query_flat), "seq", split_axis=1, concat_axis=0, tiled=True),
        lax.all_to_all(column_heads(key_flat), "seq", split_axis=1, concat_axis=0, tiled=True),
        lax.all_to_all(column_heads(value_flat), "seq", split_axis=1, concat_axis=0, tiled=True),
    )
    row_out, row_back = jax.vjp(
        row_core, row_heads(query_flat), row_heads(key_flat), row_heads(value_flat)
    )
    column_out, column_back = jax.vjp(
        column_core, as_columns(col_query), as_columns(col_key), as_columns(col_value)
    )
    returned = lax.all_to_all(
        column_out.reshape(grid_rows, cols_here, split),
        "seq",
        split_axis=0,
        concat_axis=1,
        tiled=True,
    )
    attended = joined(row_out, returned)
    mixed = jnp.dot(attended, full_out, preferred_element_type=jnp.float32)
    grad_heads = lax.dot_general(
        cot_flat, full_out, contract_last, preferred_element_type=jnp.float32
    )
    mixed = mixed.astype(jnp.bfloat16).reshape(tokens.shape)
    grad_heads = grad_heads.astype(jnp.bfloat16)
    row_grads = row_back(grad_heads[:, :split].reshape(rows_here, grid_cols, half, HEAD_DIM))
    grad_columns = lax.all_to_all(
        grad_heads[:, split:].reshape(rows_here, grid_cols, split),
        "seq",
        split_axis=1,
        concat_axis=0,
        tiled=True,
    )
    col_grads = column_back(as_columns(grad_columns))
    back_grads = (
        lax.all_to_all(
            col_grads[0].reshape(grid_rows, cols_here, split),
            "seq",
            split_axis=0,
            concat_axis=1,
            tiled=True,
        ),
        lax.all_to_all(
            col_grads[1].reshape(grid_rows, cols_here, split),
            "seq",
            split_axis=0,
            concat_axis=1,
            tiled=True,
        ),
        lax.all_to_all(
            col_grads[2].reshape(grid_rows, cols_here, split),
            "seq",
            split_axis=0,
            concat_axis=1,
            tiled=True,
        ),
    )
    grad_query = joined(row_grads[0], back_grads[0])
    grad_key = joined(row_grads[1], back_grads[1])
    grad_val = joined(row_grads[2], back_grads[2])
    grad_tokens = (
        lax.dot_general(grad_query, full_query, contract_last, preferred_element_type=jnp.float32)
        + lax.dot_general(grad_key, full_key, contract_last, preferred_element_type=jnp.float32)
        + lax.dot_general(grad_val, full_value, contract_last, preferred_element_type=jnp.float32)
    )
    grad_tokens = grad_tokens.astype(jnp.bfloat16).reshape(tokens.shape)
    summed = lax.psum_scatter(
        jnp.concatenate(
            [
                lax.dot_general(flat, grad_val, contract_first, preferred_element_type=jnp.float32),
                lax.dot_general(
                    cot_flat, attended, contract_first, preferred_element_type=jnp.float32
                ),
            ],
            axis=1,
        ),
        ("dp", "seq"),
        scatter_dimension=0,
        tiled=True,
    )
    grad_value = summed[:, :heads_width]
    grad_output = jnp.transpose(summed[:, heads_width:])
    return (mixed, grad_tokens, grad_value, grad_output)


MESH = pl.DeviceIdType.MESH
F32 = jnp.float32
BF16 = jnp.bfloat16


def dot_nn(a, b):
    return jnp.dot(a, b, preferred_element_type=F32)


def dot_nt(a, b):
    return lax.dot_general(a, b, contract_last, preferred_element_type=F32)


def dot_tn(a, b):
    return lax.dot_general(a, b, contract_first, preferred_element_type=F32)


def fused_kernel(
    dp_count,
    seq_count,
    tokens_hbm,
    cot_hbm,
    row_mask_hbm,
    column_mask_hbm,
    wq_hbm,
    wk_hbm,
    wv_hbm,
    wo_hbm,
    mixed_hbm,
    gtok_hbm,
    gval_hbm,
    gout_hbm,
    tokens_ref,
    cot_ref,
    tokens_t,
    cot_t,
    row_mask_ref,
    column_mask_ref,
    bias,
    mixed_ref,
    gtok_ref,
    gval_ref,
    gout_ref,
    gtok_part,
    w_full,
    wo_full,
    qkv_send,
    qkv_recv,
    g_rows,
    g_send,
    g_recv,
    out_send,
    out_recv,
    grad_send,
    grad_recv,
    row_qkv,
    row_grads,
    probs,
    attended,
    part,
    part_recv1,
    acc1,
    recv_x_first,
    recv_y_first,
    acc_x_first,
    acc_y_first,
    part_recv3,
    acc3,
    part_recv4,
    w_send_sem,
    w_recv_sem,
    a_send_sem,
    a_recv_sem,
    r_send_sem,
    r_recv_sem,
    local_sem,
):
    dp = lax.axis_index("dp")
    seq = lax.axis_index("seq")
    core = lax.rem(seq, 2)
    y = lax.rem(seq // 2, 2)
    z = seq // 4
    z_count = seq_count // 4
    positions = tokens_ref.shape[0]
    cols = positions // seq_count
    shard = wq_hbm.shape[0]
    out_shard = wo_hbm.shape[0]
    split = qkv_send.shape[2]
    half = split // HEAD_DIM
    other = 1 - dp
    x_peer = (other, seq)
    core_peer = (dp, seq + 1 - 2 * core)
    y_peer = (dp, seq + 2 - 4 * y)

    own_rows = pl.ds(pl.multiple_of(dp * shard, shard), shard)
    own_out = pl.ds(pl.multiple_of(dp * out_shard, out_shard), out_shard)
    weights_in = [
        pltpu.make_async_copy(wq_hbm, w_full.at[0, own_rows, :], local_sem.at[0]),
        pltpu.make_async_copy(wk_hbm, w_full.at[1, own_rows, :], local_sem.at[1]),
        pltpu.make_async_copy(wv_hbm, w_full.at[2, own_rows, :], local_sem.at[2]),
        pltpu.make_async_copy(wo_hbm, wo_full.at[own_out, :], local_sem.at[3]),
    ]
    others_in = [
        pltpu.make_async_copy(tokens_hbm, tokens_ref, local_sem.at[4]),
        pltpu.make_async_copy(cot_hbm, cot_ref, local_sem.at[5]),
        pltpu.make_async_copy(row_mask_hbm, row_mask_ref, local_sem.at[6]),
        pltpu.make_async_copy(column_mask_hbm, column_mask_ref, local_sem.at[7]),
    ]
    outs = [
        pltpu.make_async_copy(mixed_ref, mixed_hbm, local_sem.at[8]),
        pltpu.make_async_copy(gtok_ref, gtok_hbm, local_sem.at[9]),
        pltpu.make_async_copy(gval_ref, gval_hbm, local_sem.at[10]),
        pltpu.make_async_copy(gout_ref, gout_hbm, local_sem.at[11]),
    ]
    for copy in weights_in + others_in:
        copy.start()

    barrier = pltpu.get_barrier_semaphore()
    pl.semaphore_signal(barrier, inc=1, device_id=x_peer, device_id_type=MESH)

    @pl.loop(1, seq_count, unroll=True)
    def _(step):
        pl.semaphore_signal(
            barrier,
            inc=1,
            device_id=(dp, lax.rem(seq + step, seq_count)),
            device_id_type=MESH,
        )

    for copy in weights_in:
        copy.wait()
    pl.semaphore_wait(barrier, seq_count)

    def region(group, owner, qy, qc):
        if group in (3, 4):
            quarter = out_shard // 4
            start = pl.multiple_of(owner * out_shard + (qy * 2 + qc) * quarter, quarter)
            width = wo_full.shape[1] // 2
            return wo_full.at[pl.ds(start, quarter), pl.ds((group - 3) * width, width)]
        quarter = shard // 4
        start = pl.multiple_of(owner * shard + (qy * 2 + qc) * quarter, quarter)
        if group == 5:
            return w_full.at[:, pl.ds(start, quarter), pl.ds(0, split)]
        return w_full.at[group, pl.ds(start, quarter), pl.ds(split, split)]

    def weight_copy(group, hop):
        if hop == 0:
            ref, peer = region(group, dp, y, core), x_peer
        elif hop == 1:
            ref, peer = region(group, other, y, core), y_peer
        elif hop == 2:
            ref, peer = region(group, other, y, core), core_peer
        else:
            ref, peer = region(group, other, 1 - y, core), core_peer
        return pltpu.make_async_remote_copy(
            src_ref=ref,
            dst_ref=ref,
            send_sem=w_send_sem.at[group, hop],
            recv_sem=w_recv_sem.at[group, hop],
            device_id=peer,
            device_id_type=MESH,
        )

    def pass_on(group):
        weight_copy(group, 0).wait_recv()
        if group < 3:
            weight_copy(group + 2, 0).start()
        elif group == 4:
            weight_copy(5, 0).start()
        weight_copy(group, 1).start()
        weight_copy(group, 2).start()

    def pass_core(group):
        weight_copy(group, 1).wait_recv()
        weight_copy(group, 3).start()

    def weights_here(group):
        weight_copy(group, 2).wait_recv()
        weight_copy(group, 3).wait_recv()

    def column_copy(src, dst, phase, step):
        target = lax.rem(seq + step, seq_count)
        there = pl.ds(pl.multiple_of(target * cols, cols), cols)
        here = pl.ds(pl.multiple_of(seq * cols, cols), cols)
        return pltpu.make_async_remote_copy(
            src_ref=src.at[:, there, :],
            dst_ref=dst.at[:, here, :],
            send_sem=a_send_sem.at[phase],
            recv_sem=a_recv_sem.at[phase],
            device_id=(dp, target),
            device_id_type=MESH,
        )

    def one(ref, index):
        return ref.at[pl.ds(index, 1)]

    def exchange(src, dst, phase):
        @pl.loop(1, seq_count, unroll=True)
        def _(step):
            column_copy(src, dst, phase, step).start()

        here = pl.ds(pl.multiple_of(seq * cols, cols), cols)
        dst[:, here, :] = src[:, here, :]

    def whole_exchange(src, dst, phase):
        many = pl.ds(0, positions - cols)
        return pltpu.make_async_remote_copy(
            src_ref=src.at[:, many, :],
            dst_ref=dst.at[:, many, :],
            send_sem=a_send_sem.at[phase],
            recv_sem=a_recv_sem.at[phase],
            device_id=core_peer,
            device_id_type=MESH,
        )

    def arrived(src, dst, phase):
        whole_exchange(src, dst, phase).wait_recv()

    def sent(src, dst, phase):
        whole_exchange(src, dst, phase).wait_send()

    weight_copy(0, 0).start()
    weight_copy(1, 0).start()

    lane = lax.broadcasted_iota(jnp.int32, (1, 2 * HEAD_DIM), 1)
    first_lanes = lane < HEAD_DIM
    keep = (first_lanes.astype(F32).astype(BF16), (lane >= HEAD_DIM).astype(F32).astype(BF16))

    def store_bias(index, seen):
        bias[index] = jnp.where(seen, 0.0, -1e30)

    def build_bias():
        query_pos = lax.broadcasted_iota(jnp.int32, (positions, positions), 0)
        key_pos = lax.broadcasted_iota(jnp.int32, (positions, positions), 1)
        differ = query_pos ^ key_pos
        causal = key_pos <= query_pos
        matching = causal & ((differ & (cols - 1)) == 0)
        store_bias(0, causal)
        store_bias(1, causal & (differ < ROWBLK))
        store_bias(2, matching)
        store_bias(3, matching & (differ < COLBLK * cols))

    for copy in others_in:
        copy.wait()

    def head_bias(head):
        if head < half:
            bit = row_mask_ref[0, 1, 0, head]
            return jnp.where(bit == 1, bias[0], bias[1])
        column = lax.rem(lax.broadcasted_iota(jnp.int32, (1, positions), 1), cols)
        bits = jnp.zeros((1, positions), jnp.int32)
        for index in range(cols):
            bits = jnp.where(column == index, column_mask_ref[head - half, 1, 0, index], bits)
        return jnp.where(bits == 1, bias[2], bias[3])

    def softmax(head, query, key):
        scores = dot_nt(query, key) * (1.0 / math.sqrt(HEAD_DIM)) + head_bias(head)
        weights = jnp.exp(scores - jnp.max(scores, axis=-1, keepdims=True))
        return weights * (1.0 / jnp.sum(weights, axis=-1, keepdims=True))

    def pair_of(pair):
        return pl.ds(pair * 2 * HEAD_DIM, 2 * HEAD_DIM)

    def merge(halves):
        return jnp.where(first_lanes, halves[0], halves[1]).astype(BF16)

    def forward(base, query, key, value, slot):
        outs = []
        for side in range(2):
            weights = softmax(base + side, query * keep[side], key)
            probs[slot + side] = weights
            outs.append(dot_nn(weights.astype(BF16), value))
        return merge(outs)

    def value_grad(grad, slot):
        sides = [dot_tn(probs[slot + side].astype(BF16), grad) for side in range(2)]
        return merge(sides)

    def query_key_grads(query, key, value, grad, slot):
        grads = ([], [])
        for side in range(2):
            weights = probs[slot + side]
            grad_probs = dot_nt(grad * keep[side], value)
            grad_scores = weights * (
                grad_probs - jnp.sum(weights * grad_probs, axis=-1, keepdims=True)
            )
            grad_scores = (grad_scores * (1.0 / math.sqrt(HEAD_DIM))).astype(BF16)
            grads[0].append(dot_nn(grad_scores, key))
            grads[1].append(dot_tn(grad_scores, query))
        return [merge(grad_pair) for grad_pair in grads]

    def rs_copy(which, hop):
        piece, order = which // 2, which % 2
        if hop == 0:
            src, dst, peer = part.at[which, :, :, :, 1 - core], part_recv1.at[which], core_peer
        elif hop == 1 and order == 0:
            src, dst, peer = acc1.at[which, other], recv_x_first.at[piece], x_peer
        elif hop == 1:
            src, dst, peer = acc1.at[which, :, :, 1 - y], recv_y_first.at[piece], y_peer
        elif hop == 2 and order == 0:
            src, dst, peer = acc_x_first.at[piece, :, 1 - y], part_recv3.at[which], y_peer
        elif hop == 2:
            src, dst, peer = acc_y_first.at[piece, other], part_recv3.at[which], x_peer
        else:
            z_there = lax.rem(z + hop - 2, z_count)
            src, dst = acc3.at[which, z_there], part_recv4.at[which, hop - 3]
            peer = (dp, z_there * 4 + y * 2 + core)
        return pltpu.make_async_remote_copy(
            src_ref=src,
            dst_ref=dst,
            send_sem=r_send_sem.at[which, hop],
            recv_sem=r_recv_sem.at[which, hop],
            device_id=peer,
            device_id_type=MESH,
        )

    def rs_start(piece, full):
        lanes = split // 2
        for order in range(2):
            half_piece = full[:, order * lanes : (order + 1) * lanes].astype(BF16)
            part[2 * piece + order] = half_piece.reshape(part.shape[1:])
            rs_copy(2 * piece + order, 0).start()

    def rs_next(piece, hop):
        for order in range(2):
            which = 2 * piece + order
            rs_copy(which, hop).wait_recv()
            if hop == 0:
                acc1[which] = (
                    part[which, :, :, :, core].astype(F32) + part_recv1[which].astype(F32)
                ).astype(BF16)
            elif hop == 1 and order == 0:
                acc_x_first[piece] = (
                    acc1[which, dp].astype(F32) + recv_x_first[piece].astype(F32)
                ).astype(BF16)
            elif hop == 1:
                acc_y_first[piece] = (
                    acc1[which, :, :, y].astype(F32) + recv_y_first[piece].astype(F32)
                ).astype(BF16)
            elif order == 0:
                acc3[which] = (
                    acc_x_first[piece, :, y].astype(F32) + part_recv3[which].astype(F32)
                ).astype(BF16)
            else:
                acc3[which] = (
                    acc_y_first[piece, dp].astype(F32) + part_recv3[which].astype(F32)
                ).astype(BF16)
            if hop < 2:
                rs_copy(which, hop + 1).start()
            else:
                for step in range(1, z_count):
                    rs_copy(which, 2 + step).start()

    def rs_end(piece, out, first_lane):
        for order in range(2):
            which = 2 * piece + order
            total = acc3[which, z].astype(F32)
            for step in range(1, z_count):
                rs_copy(which, 2 + step).wait_recv()
                total = total + part_recv4[which, step - 1].astype(F32)
            out[:, pl.ds(first_lane + order * (split // 2), split // 2)] = total

    def project_columns(index):
        weights_here(index)
        qkv_send[index] = dot_nn(tokens_ref[...], w_full[index, :, split:]).astype(BF16)
        exchange(one(qkv_send, index), one(qkv_recv, index), index)

    pass_on(0)
    pass_on(1)
    pass_core(0)
    pass_on(2)
    project_columns(0)
    pass_core(1)
    pass_on(3)
    project_columns(1)
    pass_core(2)
    pass_on(4)
    project_columns(2)
    pass_core(3)
    pass_core(4)
    weights_here(3)
    weights_here(4)
    g_send[0] = dot_nt(cot_ref[...], wo_full[split:, :]).astype(BF16)
    exchange(g_send, g_recv, 3)
    build_bias()
    g_rows[...] = dot_nt(cot_ref[...], wo_full[:split, :]).astype(BF16)
    tokens_t[...] = tokens_ref[...].T
    cot_t[...] = cot_ref[...].T
    pass_on(5)

    for index in range(3):
        arrived(one(qkv_send, index), one(qkv_recv, index), index)
    for pair in range(split // (2 * HEAD_DIM)):
        query, key, value = (qkv_recv[index, :, pair_of(pair)] for index in range(3))
        out_send[0, :, pair_of(pair)] = forward(half + 2 * pair, query, key, value, 2 * pair)
    exchange(out_send, out_recv, 4)
    pass_core(5)

    arrived(g_send, g_recv, 3)
    pairs = range(split // (2 * HEAD_DIM))
    for pair in pairs:
        grad_send[2, :, pair_of(pair)] = value_grad(g_recv[0, :, pair_of(pair)], 2 * pair)
    exchange(one(grad_send, 2), one(grad_recv, 2), 5)
    for pair in pairs:
        query, key, value = (qkv_recv[index, :, pair_of(pair)] for index in range(3))
        grads = query_key_grads(query, key, value, g_recv[0, :, pair_of(pair)], 2 * pair)
        for index in range(2):
            grad_send[index, :, pair_of(pair)] = grads[index]
    exchange(grad_send.at[pl.ds(0, 2)], grad_recv.at[pl.ds(0, 2)], 6)

    weights_here(5)
    for index in range(3):
        row_qkv[index] = dot_nn(tokens_ref[...], w_full[index, :, :split]).astype(BF16)
    for pair in pairs:
        query, key, value = (row_qkv[index, :, pair_of(pair)] for index in range(3))
        slot = half + 2 * pair
        attended[:, pair_of(pair)] = forward(2 * pair, query, key, value, slot)
        row_grads[2, :, pair_of(pair)] = value_grad(g_rows[:, pair_of(pair)], slot)
    rs_start(0, dot_nn(cot_t[...], attended[:, :split]))
    rs_start(1, dot_nn(tokens_t[...], row_grads[2]))
    arrived(out_send, out_recv, 4)
    rs_start(2, dot_nn(cot_t[...], out_recv[0]))
    rs_next(0, 0)
    arrived(one(grad_send, 2), one(grad_recv, 2), 5)
    rs_start(3, dot_nn(tokens_t[...], grad_recv[2]))
    rs_next(1, 0)

    def row_query_key(pair):
        query, key, value = (row_qkv[index, :, pair_of(pair)] for index in range(3))
        grads = query_key_grads(query, key, value, g_rows[:, pair_of(pair)], half + 2 * pair)
        for index in range(2):
            row_grads[index, :, pair_of(pair)] = grads[index]

    for pair in pairs:
        row_query_key(pair)
        if pair == 0:
            rs_next(2, 0)
            rs_next(3, 0)
    rs_next(0, 1)
    rs_next(1, 1)
    attended[:, pl.ds(split, split)] = out_recv[0]
    mixed_ref[...] = dot_nn(attended[...], wo_full[...]).astype(BF16)
    outs[0].start()
    rs_next(2, 1)
    gtok_part[...] = (
        dot_nt(row_grads[0], w_full[0, :, :split])
        + dot_nt(row_grads[1], w_full[1, :, :split])
        + dot_nt(row_grads[2], w_full[2, :, :split])
    )
    rs_next(3, 1)
    rs_next(0, 2)
    rs_next(1, 2)
    arrived(grad_send.at[pl.ds(0, 2)], grad_recv.at[pl.ds(0, 2)], 6)
    gtok_ref[...] = (
        gtok_part[...]
        + dot_nt(grad_recv[0], w_full[0, :, split:])
        + dot_nt(grad_recv[1], w_full[1, :, split:])
        + dot_nt(grad_recv[2], w_full[2, :, split:])
    ).astype(BF16)
    outs[1].start()
    rs_next(2, 2)
    rs_next(3, 2)
    for group in range(6):
        for hop in range(4):
            weight_copy(group, hop).wait_send()
    for index in range(3):
        sent(one(qkv_send, index), one(qkv_recv, index), index)
    sent(g_send, g_recv, 3)
    sent(out_send, out_recv, 4)
    sent(one(grad_send, 2), one(grad_recv, 2), 5)
    sent(grad_send.at[pl.ds(0, 2)], grad_recv.at[pl.ds(0, 2)], 6)
    rs_end(0, gout_ref, 0)
    rs_end(2, gout_ref, split)
    outs[3].start()
    rs_end(1, gval_ref, 0)
    rs_end(3, gval_ref, split)
    outs[2].start()
    for which in range(8):
        for hop in range(2 + z_count):
            rs_copy(which, hop).wait_send()
    for copy in outs:
        copy.wait()


def hand_out_kernel(*refs):
    count = (len(refs) - 2) // 3
    ins, outs, held = refs[:count], refs[count : 2 * count], refs[2 * count : 3 * count]
    in_sems, out_sems = refs[-2:]
    fetches = [
        pltpu.make_async_copy(ins[index], held[index], in_sems.at[index]) for index in range(count)
    ]
    stores = [
        pltpu.make_async_copy(held[index], outs[index], out_sems.at[index])
        for index in range(count)
    ]
    for copy in fetches:
        copy.start()
    for index in range(count):
        fetches[index].wait()
        stores[index].start()
    for copy in stores:
        copy.wait()


def hand_out(*arrays):
    count = len(arrays)
    return pl.pallas_call(
        hand_out_kernel,
        out_shape=[jax.ShapeDtypeStruct(item.shape, item.dtype) for item in arrays],
        in_specs=[pl.BlockSpec(memory_space=pltpu.HBM)] * count,
        out_specs=[pl.BlockSpec(memory_space=pltpu.HBM)] * count,
        scratch_shapes=[pltpu.VMEM(item.shape, item.dtype) for item in arrays]
        + [pltpu.SemaphoreType.DMA((count,)), pltpu.SemaphoreType.DMA((count,))],
        compiler_params=pltpu.CompilerParams(vmem_limit_bytes=64 * 1024 * 1024 - 65536),
    )(*arrays)


def fused_fits(dp_count, seq_count, tokens, row_mask, column_mask, w_query, w_out):
    positions = tokens.shape[1] * tokens.shape[2]
    return (
        tokens.shape[0] == 1
        and tokens.shape[1] == 1
        and dp_count == 2
        and seq_count % 4 == 0
        and positions % (16 * seq_count) == 0
        and w_query.shape[0] % 64 == 0
        and w_query.shape[1] % 512 == 0
        and w_out.shape[1] % 256 == 0
        and positions & (positions - 1) == 0
        and seq_count & (seq_count - 1) == 0
        and w_out.shape[0] % 64 == 0
        and tokens.shape[3] % (16 * dp_count * seq_count) == 0
        and row_mask.shape[2] == 2
        and column_mask.shape[2] == 2
    )


def fused_body(tokens, cotangent, row_mask, column_mask, w_query, w_key, w_value, w_out):
    dp_count, seq_count = lax.axis_size("dp"), lax.axis_size("seq")
    if not fused_fits(dp_count, seq_count, tokens, row_mask, column_mask, w_query, w_out):
        return body(
            tokens, cotangent, row_mask, column_mask, w_query, w_key, w_value, w_out
        )
    positions, width = tokens.shape[1] * tokens.shape[2], tokens.shape[3]
    heads_width = w_query.shape[1]
    split = heads_width // 2
    rows = width // (dp_count * seq_count)
    z_count = seq_count // 4
    stored_row_mask = jnp.transpose(row_mask, (1, 2, 3, 0))
    stored_column_mask = jnp.transpose(column_mask, (0, 2, 3, 1))
    lead = (8, dp_count, z_count, 2)
    lanes = split // 2
    call = pl.pallas_call(
        lambda *refs: fused_kernel(dp_count, seq_count, *refs),
        out_shape=(
            jax.ShapeDtypeStruct((positions, width), BF16),
            jax.ShapeDtypeStruct((positions, width), BF16),
            jax.ShapeDtypeStruct((rows, heads_width), F32),
            jax.ShapeDtypeStruct((rows, heads_width), F32),
        ),
        in_specs=[pl.BlockSpec(memory_space=pltpu.HBM)] * 8,
        out_specs=[pl.BlockSpec(memory_space=pltpu.HBM)] * 4,
        scratch_shapes=[
            pltpu.VMEM((positions, width), BF16),
            pltpu.VMEM((positions, width), BF16),
            pltpu.VMEM((width, positions), BF16),
            pltpu.VMEM((width, positions), BF16),
            pltpu.SMEM(stored_row_mask.shape, jnp.int32),
            pltpu.SMEM(stored_column_mask.shape, jnp.int32),
            pltpu.VMEM((4, positions, positions), F32),
            pltpu.VMEM((positions, width), BF16),
            pltpu.VMEM((positions, width), BF16),
            pltpu.VMEM((rows, heads_width), F32),
            pltpu.VMEM((rows, heads_width), F32),
            pltpu.VMEM((positions, width), F32),
            pltpu.VMEM((3, width, heads_width), BF16),
            pltpu.VMEM((heads_width, width), BF16),
            pltpu.VMEM((3, positions, split), BF16),
            pltpu.VMEM((3, positions, split), BF16),
            pltpu.VMEM((positions, split), BF16),
            pltpu.VMEM((1, positions, split), BF16),
            pltpu.VMEM((1, positions, split), BF16),
            pltpu.VMEM((1, positions, split), BF16),
            pltpu.VMEM((1, positions, split), BF16),
            pltpu.VMEM((3, positions, split), BF16),
            pltpu.VMEM((3, positions, split), BF16),
            pltpu.VMEM((3, positions, split), BF16),
            pltpu.VMEM((3, positions, split), BF16),
            pltpu.VMEM((heads_width // HEAD_DIM, positions, positions), F32),
            pltpu.VMEM((positions, heads_width), BF16),
            pltpu.VMEM(lead + (2, rows, lanes), BF16),
            pltpu.VMEM(lead + (rows, lanes), BF16),
            pltpu.VMEM(lead + (rows, lanes), BF16),
            pltpu.VMEM((4, z_count, 2, rows, lanes), BF16),
            pltpu.VMEM((4, 2, z_count, rows, lanes), BF16),
            pltpu.VMEM((4, z_count, 2, rows, lanes), BF16),
            pltpu.VMEM((4, 2, z_count, rows, lanes), BF16),
            pltpu.VMEM((8, z_count, rows, lanes), BF16),
            pltpu.VMEM((8, z_count, rows, lanes), BF16),
            pltpu.VMEM((8, z_count - 1, rows, lanes), BF16),
            pltpu.SemaphoreType.DMA((6, 4)),
            pltpu.SemaphoreType.DMA((6, 4)),
            pltpu.SemaphoreType.DMA((7,)),
            pltpu.SemaphoreType.DMA((7,)),
            pltpu.SemaphoreType.DMA((8, 2 + z_count)),
            pltpu.SemaphoreType.DMA((8, 2 + z_count)),
            pltpu.SemaphoreType.DMA((12,)),
        ],
        compiler_params=pltpu.CompilerParams(
            collective_id=0, has_side_effects=True, vmem_limit_bytes=64 * 1024 * 1024 - 65536
        ),
        cost_estimate=pl.CostEstimate(
            flops=3_400_000_000, bytes_accessed=8_000_000, transcendentals=524288
        ),
    )
    mixed, grad_tokens, grad_value, grad_output = call(
        tokens.reshape(positions, width),
        cotangent.reshape(positions, width),
        stored_row_mask,
        stored_column_mask,
        w_query,
        w_key,
        w_value,
        w_out,
    )
    mixed, grad_tokens, grad_value, grad_output = hand_out(
        mixed, grad_tokens, grad_value, grad_output
    )
    return (
        mixed.reshape(tokens.shape),
        grad_tokens.reshape(tokens.shape),
        grad_value,
        jnp.transpose(grad_output),
    )


def solution(mesh):
    return jax.shard_map(
        fused_body,
        mesh=mesh,
        in_specs=(
            P("dp", "seq", None, None),
            P("dp", "seq", None, None),
            P(None, "seq", None, None),
            P(None, "seq", None, None),
            P("dp", None),
            P("dp", None),
            P("dp", None),
            P("dp", None),
        ),
        out_specs=(
            P("dp", "seq", None, None),
            P("dp", "seq", None, None),
            P(("dp", "seq"), None),
            P(None, ("dp", "seq")),
        ),
        check_vma=False,
    )
```

```python
import math

import jax
import jax.numpy as jnp
from jax import lax
from jax.experimental import pallas as pl
from jax.experimental.pallas import tpu as pltpu
from jax.sharding import PartitionSpec as P

HEAD_DIM = 64
ROWBLK = 128
COLBLK = 8


row_forms = ("blhe,bmhe->bhlm", "bhlm,bmhe->blhe")
column_forms = ("lbhe,mbhe->bhlm", "bhlm,mbhe->lbhe")
contract_last = (((1,), (1,)), ((), ()))
contract_first = (((0,), (0,)), ((), ()))


def allowed_cells(mask_blocks, block_size):
    expanded = jnp.repeat(jnp.repeat(mask_blocks, block_size, axis=-2), block_size, axis=-1)
    length = expanded.shape[-1]
    causal = jnp.arange(length)[:, None] >= jnp.arange(length)[None, :]
    return (expanded == 1) & causal


def attend(queries, key_part, value_part, allowed, forms):
    scale_factor = 1.0 / math.sqrt(queries.shape[-1])
    scores = (
        jnp.einsum(forms[0], queries.astype(jnp.float32), key_part.astype(jnp.float32))
        * scale_factor
    )
    scores = jnp.where(allowed, scores, -1e30)
    highest = lax.stop_gradient(jnp.max(scores, axis=-1, keepdims=True))
    weights = jnp.exp(scores - highest)
    weights = weights / jnp.sum(weights, axis=-1, keepdims=True)
    rounded = lax.optimization_barrier(weights.astype(jnp.bfloat16)).astype(jnp.float32)
    result = jnp.einsum(forms[1], rounded, value_part.astype(jnp.float32))
    return result.astype(jnp.bfloat16)


def body(tokens, cotangent, row_mask, column_mask, w_query, w_key, w_value, w_out):
    rows_here = tokens.shape[1]
    grid_cols = tokens.shape[2]
    width = tokens.shape[3]
    heads_width = w_query.shape[1]
    half = heads_width // HEAD_DIM // 2
    split = half * HEAD_DIM
    flat = tokens.reshape(-1, width)
    cot_flat = cotangent.reshape(-1, width)
    token_count = flat.shape[0]
    seq_count = lax.axis_size("seq")
    grid_rows = rows_here * seq_count
    cols_here = grid_cols // seq_count
    full_query, full_key, full_value, full_out = (
        lax.all_gather(w_query, "dp", axis=0, tiled=True),
        lax.all_gather(w_key, "dp", axis=0, tiled=True),
        lax.all_gather(w_value, "dp", axis=0, tiled=True),
        lax.all_gather(w_out, "dp", axis=0, tiled=True),
    )
    proj_query = jnp.dot(flat, full_query, preferred_element_type=jnp.float32)
    proj_key = jnp.dot(flat, full_key, preferred_element_type=jnp.float32)
    proj_value = jnp.dot(flat, full_value, preferred_element_type=jnp.float32)
    query_flat = proj_query.astype(jnp.bfloat16)
    key_flat = proj_key.astype(jnp.bfloat16)
    value_flat = proj_value.astype(jnp.bfloat16)
    row_allowed = allowed_cells(jnp.transpose(row_mask, (1, 0, 2, 3)), ROWBLK)
    column_allowed = allowed_cells(jnp.transpose(column_mask, (1, 0, 2, 3)), COLBLK)

    def row_core(first, second, third):
        return attend(first, second, third, row_allowed, row_forms)

    def column_core(first, second, third):
        return attend(first, second, third, column_allowed, column_forms)

    def row_heads(matrix):
        return matrix[:, :split].reshape(rows_here, grid_cols, half, HEAD_DIM)

    def column_heads(matrix):
        return matrix[:, split:].reshape(rows_here, grid_cols, split)

    def as_columns(block):
        return block.reshape(grid_rows, cols_here, half, HEAD_DIM)

    def joined(row_part, col_part):
        return jnp.concatenate(
            [row_part.reshape(token_count, split), col_part.reshape(token_count, split)], axis=1
        )

    col_query, col_key, col_value = (
        lax.all_to_all(column_heads(query_flat), "seq", split_axis=1, concat_axis=0, tiled=True),
        lax.all_to_all(column_heads(key_flat), "seq", split_axis=1, concat_axis=0, tiled=True),
        lax.all_to_all(column_heads(value_flat), "seq", split_axis=1, concat_axis=0, tiled=True),
    )
    row_out, row_back = jax.vjp(
        row_core, row_heads(query_flat), row_heads(key_flat), row_heads(value_flat)
    )
    column_out, column_back = jax.vjp(
        column_core, as_columns(col_query), as_columns(col_key), as_columns(col_value)
    )
    returned = lax.all_to_all(
        column_out.reshape(grid_rows, cols_here, split),
        "seq",
        split_axis=0,
        concat_axis=1,
        tiled=True,
    )
    attended = joined(row_out, returned)
    mixed = jnp.dot(attended, full_out, preferred_element_type=jnp.float32)
    grad_heads = lax.dot_general(
        cot_flat, full_out, contract_last, preferred_element_type=jnp.float32
    )
    mixed = mixed.astype(jnp.bfloat16).reshape(tokens.shape)
    grad_heads = grad_heads.astype(jnp.bfloat16)
    row_grads = row_back(grad_heads[:, :split].reshape(rows_here, grid_cols, half, HEAD_DIM))
    grad_columns = lax.all_to_all(
        grad_heads[:, split:].reshape(rows_here, grid_cols, split),
        "seq",
        split_axis=1,
        concat_axis=0,
        tiled=True,
    )
    col_grads = column_back(as_columns(grad_columns))
    back_grads = (
        lax.all_to_all(
            col_grads[0].reshape(grid_rows, cols_here, split),
            "seq",
            split_axis=0,
            concat_axis=1,
            tiled=True,
        ),
        lax.all_to_all(
            col_grads[1].reshape(grid_rows, cols_here, split),
            "seq",
            split_axis=0,
            concat_axis=1,
            tiled=True,
        ),
        lax.all_to_all(
            col_grads[2].reshape(grid_rows, cols_here, split),
            "seq",
            split_axis=0,
            concat_axis=1,
            tiled=True,
        ),
    )
    grad_query = joined(row_grads[0], back_grads[0])
    grad_key = joined(row_grads[1], back_grads[1])
    grad_val = joined(row_grads[2], back_grads[2])
    grad_tokens = (
        lax.dot_general(grad_query, full_query, contract_last, preferred_element_type=jnp.float32)
        + lax.dot_general(grad_key, full_key, contract_last, preferred_element_type=jnp.float32)
        + lax.dot_general(grad_val, full_value, contract_last, preferred_element_type=jnp.float32)
    )
    grad_tokens = grad_tokens.astype(jnp.bfloat16).reshape(tokens.shape)
    summed = lax.psum_scatter(
        jnp.concatenate(
            [
                lax.dot_general(flat, grad_val, contract_first, preferred_element_type=jnp.float32),
                lax.dot_general(
                    cot_flat, attended, contract_first, preferred_element_type=jnp.float32
                ),
            ],
            axis=1,
        ),
        ("dp", "seq"),
        scatter_dimension=0,
        tiled=True,
    )
    grad_value = summed[:, :heads_width]
    grad_output = jnp.transpose(summed[:, heads_width:])
    return (mixed, grad_tokens, grad_value, grad_output)


MESH = pl.DeviceIdType.MESH
F32 = jnp.float32
BF16 = jnp.bfloat16


def dot_nn(a, b):
    return jnp.dot(a, b, preferred_element_type=F32)


def dot_nt(a, b):
    return lax.dot_general(a, b, contract_last, preferred_element_type=F32)


def fused_kernel(
    dp_count,
    seq_count,
    tokens_hbm,
    cot_hbm,
    row_mask_hbm,
    column_mask_hbm,
    wq_hbm,
    wk_hbm,
    wv_hbm,
    wo_hbm,
    mixed_hbm,
    gtok_hbm,
    gval_hbm,
    gout_hbm,
    tokens_ref,
    cot_ref,
    tokens_t,
    cot_t,
    row_mask_ref,
    column_mask_ref,
    bias,
    unit,
    mixed_ref,
    gtok_ref,
    gval_ref,
    gout_ref,
    gtok_part,
    w_full,
    wo_full,
    qkv_send,
    qkv_recv,
    g_rows,
    g_send,
    g_recv,
    out_send,
    out_recv,
    grad_send,
    grad_recv,
    row_qkv,
    row_grads,
    probs,
    attended,
    part,
    part_recv1,
    acc1,
    recv_x_first,
    recv_y_first,
    acc_x_first,
    acc_y_first,
    part_recv3,
    acc3,
    part_recv4,
    w_send_sem,
    w_recv_sem,
    a_send_sem,
    a_recv_sem,
    r_send_sem,
    r_recv_sem,
    local_sem,
):
    dp = lax.axis_index("dp")
    seq = lax.axis_index("seq")
    core = lax.rem(seq, 2)
    y = lax.rem(seq // 2, 2)
    z = seq // 4
    z_count = seq_count // 4
    positions = tokens_ref.shape[0]
    cols = positions // seq_count
    shard = wq_hbm.shape[0]
    out_shard = wo_hbm.shape[0]
    split = qkv_send.shape[2]
    half = split // HEAD_DIM
    other = 1 - dp
    x_peer = (other, seq)
    core_peer = (dp, seq + 1 - 2 * core)
    y_peer = (dp, seq + 2 - 4 * y)

    own_rows = pl.ds(pl.multiple_of(dp * shard, shard), shard)
    own_out = pl.ds(pl.multiple_of(dp * out_shard, out_shard), out_shard)
    weights_in = [
        pltpu.make_async_copy(wq_hbm, w_full.at[0, own_rows, :], local_sem.at[0]),
        pltpu.make_async_copy(wk_hbm, w_full.at[1, own_rows, :], local_sem.at[1]),
        pltpu.make_async_copy(wv_hbm, w_full.at[2, own_rows, :], local_sem.at[2]),
        pltpu.make_async_copy(wo_hbm, wo_full.at[own_out, :], local_sem.at[3]),
    ]
    others_in = [
        pltpu.make_async_copy(tokens_hbm, tokens_ref, local_sem.at[4]),
        pltpu.make_async_copy(cot_hbm, cot_ref, local_sem.at[5]),
        pltpu.make_async_copy(row_mask_hbm, row_mask_ref, local_sem.at[6]),
        pltpu.make_async_copy(column_mask_hbm, column_mask_ref, local_sem.at[7]),
    ]
    outs = [
        pltpu.make_async_copy(mixed_ref, mixed_hbm, local_sem.at[8]),
        pltpu.make_async_copy(gtok_ref, gtok_hbm, local_sem.at[9]),
        pltpu.make_async_copy(gval_ref, gval_hbm, local_sem.at[10]),
        pltpu.make_async_copy(gout_ref, gout_hbm, local_sem.at[11]),
    ]
    for copy in weights_in + others_in:
        copy.start()

    barrier = pltpu.get_barrier_semaphore()
    pl.semaphore_signal(barrier, inc=1, device_id=x_peer, device_id_type=MESH)

    @pl.loop(1, seq_count, unroll=True)
    def _(step):
        pl.semaphore_signal(
            barrier,
            inc=1,
            device_id=(dp, lax.rem(seq + step, seq_count)),
            device_id_type=MESH,
        )

    def store_bias(index, seen):
        bias[index] = jnp.where(seen, 0.0, -1e30)

    query_pos = lax.broadcasted_iota(jnp.int32, (positions, positions), 0)
    key_pos = lax.broadcasted_iota(jnp.int32, (positions, positions), 1)
    differ = query_pos ^ key_pos
    causal = key_pos <= query_pos
    matching = causal & ((differ & (cols - 1)) == 0)
    store_bias(0, causal)
    store_bias(1, causal & (differ < ROWBLK))
    store_bias(2, matching)
    store_bias(3, matching & (differ < COLBLK * cols))
    unit[...] = jnp.where(differ == 0, 1.0, 0.0).astype(BF16)

    for copy in weights_in:
        copy.wait()
    pl.semaphore_wait(barrier, seq_count)

    def region(group, owner, qy, qc):
        if group in (3, 4):
            quarter = out_shard // 4
            start = pl.multiple_of(owner * out_shard + (qy * 2 + qc) * quarter, quarter)
            width = wo_full.shape[1] // 2
            return wo_full.at[pl.ds(start, quarter), pl.ds((group - 3) * width, width)]
        quarter = shard // 4
        start = pl.multiple_of(owner * shard + (qy * 2 + qc) * quarter, quarter)
        if group == 5:
            return w_full.at[:, pl.ds(start, quarter), pl.ds(0, split)]
        return w_full.at[group, pl.ds(start, quarter), pl.ds(split, split)]

    def weight_copy(group, hop):
        if hop == 0:
            ref, peer = region(group, dp, y, core), x_peer
        elif hop == 1:
            ref, peer = region(group, other, y, core), y_peer
        elif hop == 2:
            ref, peer = region(group, other, y, core), core_peer
        else:
            ref, peer = region(group, other, 1 - y, core), core_peer
        return pltpu.make_async_remote_copy(
            src_ref=ref,
            dst_ref=ref,
            send_sem=w_send_sem.at[group, hop],
            recv_sem=w_recv_sem.at[group, hop],
            device_id=peer,
            device_id_type=MESH,
        )

    def pass_on(group):
        weight_copy(group, 0).wait_recv()
        if group < 3:
            weight_copy(group + 2, 0).start()
        elif group == 4:
            weight_copy(5, 0).start()
        weight_copy(group, 1).start()
        weight_copy(group, 2).start()

    def pass_core(group):
        weight_copy(group, 1).wait_recv()
        weight_copy(group, 3).start()

    def weights_here(group):
        weight_copy(group, 2).wait_recv()
        weight_copy(group, 3).wait_recv()

    def column_copy(src, dst, phase, step):
        target = lax.rem(seq + step, seq_count)
        there = pl.ds(pl.multiple_of(target * cols, cols), cols)
        here = pl.ds(pl.multiple_of(seq * cols, cols), cols)
        return pltpu.make_async_remote_copy(
            src_ref=src.at[:, there, :],
            dst_ref=dst.at[:, here, :],
            send_sem=a_send_sem.at[phase],
            recv_sem=a_recv_sem.at[phase],
            device_id=(dp, target),
            device_id_type=MESH,
        )

    def one(ref, index):
        return ref.at[pl.ds(index, 1)]

    def exchange(src, dst, phase):
        @pl.loop(1, seq_count, unroll=True)
        def _(step):
            column_copy(src, dst, phase, step).start()

        here = pl.ds(pl.multiple_of(seq * cols, cols), cols)
        dst[:, here, :] = src[:, here, :]

    def whole_exchange(src, dst, phase):
        many = pl.ds(0, positions - cols)
        return pltpu.make_async_remote_copy(
            src_ref=src.at[:, many, :],
            dst_ref=dst.at[:, many, :],
            send_sem=a_send_sem.at[phase],
            recv_sem=a_recv_sem.at[phase],
            device_id=core_peer,
            device_id_type=MESH,
        )

    def arrived(src, dst, phase):
        whole_exchange(src, dst, phase).wait_recv()

    def sent(src, dst, phase):
        whole_exchange(src, dst, phase).wait_send()

    weight_copy(0, 0).start()
    weight_copy(1, 0).start()

    lane = lax.broadcasted_iota(jnp.int32, (1, 2 * HEAD_DIM), 1)
    first_lanes = lane < HEAD_DIM
    keep = (first_lanes.astype(F32).astype(BF16), (lane >= HEAD_DIM).astype(F32).astype(BF16))

    for copy in others_in:
        copy.wait()
    for first in range(0, tokens_ref.shape[1], positions):
        block = slice(first, first + positions)
        tokens_t[block, :] = dot_nt(unit[...], tokens_ref[:, block]).astype(BF16)
        cot_t[block, :] = dot_nt(unit[...], cot_ref[:, block]).astype(BF16)

    def head_bias(head):
        if head < half:
            bit = row_mask_ref[0, 1, 0, head]
            return jnp.where(bit == 1, bias[0], bias[1])
        column = lax.rem(lax.broadcasted_iota(jnp.int32, (1, positions), 1), cols)
        bits = jnp.zeros((1, positions), jnp.int32)
        for index in range(cols):
            bits = jnp.where(column == index, column_mask_ref[head - half, 1, 0, index], bits)
        return jnp.where(bits == 1, bias[2], bias[3])

    def softmax(head, query, key):
        scores = dot_nt(query, key) * (1.0 / math.sqrt(HEAD_DIM)) + head_bias(head)
        weights = jnp.exp(scores - jnp.max(scores, axis=-1, keepdims=True))
        return weights * (1.0 / jnp.sum(weights, axis=-1, keepdims=True))

    def pair_of(pair):
        return pl.ds(pair * 2 * HEAD_DIM, 2 * HEAD_DIM)

    def merge(halves):
        return jnp.where(first_lanes, halves[0], halves[1]).astype(BF16)

    def forward(base, query, key, value, slot):
        outs = []
        for side in range(2):
            weights = softmax(base + side, query * keep[side], key)
            probs[slot + side] = weights
            outs.append(dot_nn(weights.astype(BF16), value))
        return merge(outs)

    def turned(square):
        return dot_nt(unit[...], square).astype(BF16)

    def value_grad(grad, slot):
        sides = [dot_nn(turned(probs[slot + side].astype(BF16)), grad) for side in range(2)]
        return merge(sides)

    def query_key_grads(query, key, value, grad, slot):
        grads = ([], [])
        for side in range(2):
            weights = probs[slot + side]
            grad_probs = dot_nt(grad * keep[side], value)
            grad_scores = weights * (
                grad_probs - jnp.sum(weights * grad_probs, axis=-1, keepdims=True)
            )
            grad_scores = (grad_scores * (1.0 / math.sqrt(HEAD_DIM))).astype(BF16)
            grads[0].append(dot_nn(grad_scores, key))
            grads[1].append(dot_nn(turned(grad_scores), query))
        return [merge(grad_pair) for grad_pair in grads]

    def rs_copy(which, hop):
        piece, order = which // 2, which % 2
        if hop == 0:
            src, dst, peer = part.at[which, :, :, :, 1 - core], part_recv1.at[which], core_peer
        elif hop == 1 and order == 0:
            src, dst, peer = acc1.at[which, other], recv_x_first.at[piece], x_peer
        elif hop == 1:
            src, dst, peer = acc1.at[which, :, :, 1 - y], recv_y_first.at[piece], y_peer
        elif hop == 2 and order == 0:
            src, dst, peer = acc_x_first.at[piece, :, 1 - y], part_recv3.at[which], y_peer
        elif hop == 2:
            src, dst, peer = acc_y_first.at[piece, other], part_recv3.at[which], x_peer
        else:
            z_there = lax.rem(z + hop - 2, z_count)
            src, dst = acc3.at[which, z_there], part_recv4.at[which, hop - 3]
            peer = (dp, z_there * 4 + y * 2 + core)
        return pltpu.make_async_remote_copy(
            src_ref=src,
            dst_ref=dst,
            send_sem=r_send_sem.at[which, hop],
            recv_sem=r_recv_sem.at[which, hop],
            device_id=peer,
            device_id_type=MESH,
        )

    def rs_start(piece, full):
        lanes = split // 2
        for order in range(2):
            half_piece = full[:, order * lanes : (order + 1) * lanes].astype(BF16)
            part[2 * piece + order] = half_piece.reshape(part.shape[1:])
            rs_copy(2 * piece + order, 0).start()

    def rs_next(piece, hop):
        for order in range(2):
            which = 2 * piece + order
            rs_copy(which, hop).wait_recv()
            if hop == 0:
                acc1[which] = (
                    part[which, :, :, :, core].astype(F32) + part_recv1[which].astype(F32)
                ).astype(BF16)
            elif hop == 1 and order == 0:
                acc_x_first[piece] = (
                    acc1[which, dp].astype(F32) + recv_x_first[piece].astype(F32)
                ).astype(BF16)
            elif hop == 1:
                acc_y_first[piece] = (
                    acc1[which, :, :, y].astype(F32) + recv_y_first[piece].astype(F32)
                ).astype(BF16)
            elif order == 0:
                acc3[which] = (
                    acc_x_first[piece, :, y].astype(F32) + part_recv3[which].astype(F32)
                ).astype(BF16)
            else:
                acc3[which] = (
                    acc_y_first[piece, dp].astype(F32) + part_recv3[which].astype(F32)
                ).astype(BF16)
            if hop < 2:
                rs_copy(which, hop + 1).start()
            else:
                for step in range(1, z_count):
                    rs_copy(which, 2 + step).start()

    def rs_end(piece, out, first_lane):
        for order in range(2):
            which = 2 * piece + order
            total = acc3[which, z].astype(F32)
            for step in range(1, z_count):
                rs_copy(which, 2 + step).wait_recv()
                total = total + part_recv4[which, step - 1].astype(F32)
            out[:, pl.ds(first_lane + order * (split // 2), split // 2)] = total

    def project_columns(index):
        weights_here(index)
        qkv_send[index] = dot_nn(tokens_ref[...], w_full[index, :, split:]).astype(BF16)
        exchange(one(qkv_send, index), one(qkv_recv, index), index)

    pass_on(0)
    pass_on(1)
    pass_core(0)
    pass_on(2)
    project_columns(0)
    pass_core(1)
    pass_on(3)
    project_columns(1)
    pass_core(2)
    pass_on(4)
    project_columns(2)
    pass_core(3)
    pass_core(4)
    weights_here(3)
    weights_here(4)
    g_send[0] = dot_nt(cot_ref[...], wo_full[split:, :]).astype(BF16)
    exchange(g_send, g_recv, 3)
    g_rows[...] = dot_nt(cot_ref[...], wo_full[:split, :]).astype(BF16)
    pass_on(5)

    for index in range(3):
        arrived(one(qkv_send, index), one(qkv_recv, index), index)
    for pair in range(split // (2 * HEAD_DIM)):
        query, key, value = (qkv_recv[index, :, pair_of(pair)] for index in range(3))
        out_send[0, :, pair_of(pair)] = forward(half + 2 * pair, query, key, value, 2 * pair)
    exchange(out_send, out_recv, 4)
    pass_core(5)

    arrived(g_send, g_recv, 3)
    pairs = range(split // (2 * HEAD_DIM))
    for pair in pairs:
        grad_send[2, :, pair_of(pair)] = value_grad(g_recv[0, :, pair_of(pair)], 2 * pair)
    exchange(one(grad_send, 2), one(grad_recv, 2), 5)
    for pair in pairs:
        query, key, value = (qkv_recv[index, :, pair_of(pair)] for index in range(3))
        grads = query_key_grads(query, key, value, g_recv[0, :, pair_of(pair)], 2 * pair)
        for index in range(2):
            grad_send[index, :, pair_of(pair)] = grads[index]
    exchange(grad_send.at[pl.ds(0, 2)], grad_recv.at[pl.ds(0, 2)], 6)

    weights_here(5)
    for index in range(3):
        row_qkv[index] = dot_nn(tokens_ref[...], w_full[index, :, :split]).astype(BF16)
    for pair in pairs:
        query, key, value = (row_qkv[index, :, pair_of(pair)] for index in range(3))
        slot = half + 2 * pair
        attended[:, pair_of(pair)] = forward(2 * pair, query, key, value, slot)
        row_grads[2, :, pair_of(pair)] = value_grad(g_rows[:, pair_of(pair)], slot)
    rs_start(0, dot_nn(cot_t[...], attended[:, :split]))
    rs_start(1, dot_nn(tokens_t[...], row_grads[2]))
    arrived(out_send, out_recv, 4)
    rs_start(2, dot_nn(cot_t[...], out_recv[0]))
    rs_next(0, 0)
    arrived(one(grad_send, 2), one(grad_recv, 2), 5)
    rs_start(3, dot_nn(tokens_t[...], grad_recv[2]))
    rs_next(1, 0)

    def row_query_key(pair):
        query, key, value = (row_qkv[index, :, pair_of(pair)] for index in range(3))
        grads = query_key_grads(query, key, value, g_rows[:, pair_of(pair)], half + 2 * pair)
        for index in range(2):
            row_grads[index, :, pair_of(pair)] = grads[index]

    for pair in pairs:
        row_query_key(pair)
        if pair == 0:
            rs_next(2, 0)
            rs_next(3, 0)
    rs_next(0, 1)
    rs_next(1, 1)
    attended[:, pl.ds(split, split)] = out_recv[0]
    mixed_ref[...] = dot_nn(attended[...], wo_full[...]).astype(BF16)
    outs[0].start()
    rs_next(2, 1)
    gtok_part[...] = (
        dot_nt(row_grads[0], w_full[0, :, :split])
        + dot_nt(row_grads[1], w_full[1, :, :split])
        + dot_nt(row_grads[2], w_full[2, :, :split])
    )
    rs_next(3, 1)
    rs_next(0, 2)
    rs_next(1, 2)
    arrived(grad_send.at[pl.ds(0, 2)], grad_recv.at[pl.ds(0, 2)], 6)
    gtok_ref[...] = (
        gtok_part[...]
        + dot_nt(grad_recv[0], w_full[0, :, split:])
        + dot_nt(grad_recv[1], w_full[1, :, split:])
        + dot_nt(grad_recv[2], w_full[2, :, split:])
    ).astype(BF16)
    outs[1].start()
    rs_next(2, 2)
    rs_next(3, 2)
    for group in range(6):
        for hop in range(4):
            weight_copy(group, hop).wait_send()
    for index in range(3):
        sent(one(qkv_send, index), one(qkv_recv, index), index)
    sent(g_send, g_recv, 3)
    sent(out_send, out_recv, 4)
    sent(one(grad_send, 2), one(grad_recv, 2), 5)
    sent(grad_send.at[pl.ds(0, 2)], grad_recv.at[pl.ds(0, 2)], 6)
    rs_end(0, gout_ref, 0)
    rs_end(2, gout_ref, split)
    outs[3].start()
    rs_end(1, gval_ref, 0)
    rs_end(3, gval_ref, split)
    outs[2].start()
    for which in range(8):
        for hop in range(2 + z_count):
            rs_copy(which, hop).wait_send()
    for copy in outs:
        copy.wait()


def hand_out_kernel(*refs):
    count = (len(refs) - 2) // 3
    ins, outs, held = refs[:count], refs[count : 2 * count], refs[2 * count : 3 * count]
    in_sems, out_sems = refs[-2:]
    fetches = [
        pltpu.make_async_copy(ins[index], held[index], in_sems.at[index]) for index in range(count)
    ]
    stores = [
        pltpu.make_async_copy(held[index], outs[index], out_sems.at[index])
        for index in range(count)
    ]
    for copy in fetches:
        copy.start()
    for index in range(count):
        fetches[index].wait()
        stores[index].start()
    for copy in stores:
        copy.wait()


def hand_out(*arrays):
    count = len(arrays)
    return pl.pallas_call(
        hand_out_kernel,
        out_shape=[jax.ShapeDtypeStruct(item.shape, item.dtype) for item in arrays],
        in_specs=[pl.BlockSpec(memory_space=pltpu.HBM)] * count,
        out_specs=[pl.BlockSpec(memory_space=pltpu.HBM)] * count,
        scratch_shapes=[pltpu.VMEM(item.shape, item.dtype) for item in arrays]
        + [pltpu.SemaphoreType.DMA((count,)), pltpu.SemaphoreType.DMA((count,))],
        compiler_params=pltpu.CompilerParams(vmem_limit_bytes=64 * 1024 * 1024 - 65536),
    )(*arrays)


def fused_fits(dp_count, seq_count, tokens, row_mask, column_mask, w_query, w_out):
    positions = tokens.shape[1] * tokens.shape[2]
    return (
        tokens.shape[0] == 1
        and tokens.shape[1] == 1
        and dp_count == 2
        and seq_count % 4 == 0
        and positions % (16 * seq_count) == 0
        and w_query.shape[0] % 64 == 0
        and w_query.shape[1] % 512 == 0
        and w_out.shape[1] % 256 == 0
        and tokens.shape[3] % positions == 0
        and positions % 128 == 0
        and positions & (positions - 1) == 0
        and seq_count & (seq_count - 1) == 0
        and w_out.shape[0] % 64 == 0
        and tokens.shape[3] % (16 * dp_count * seq_count) == 0
        and row_mask.shape[2] == 2
        and column_mask.shape[2] == 2
    )


def fused_body(tokens, cotangent, row_mask, column_mask, w_query, w_key, w_value, w_out):
    dp_count, seq_count = lax.axis_size("dp"), lax.axis_size("seq")
    if not fused_fits(dp_count, seq_count, tokens, row_mask, column_mask, w_query, w_out):
        return body(
            tokens, cotangent, row_mask, column_mask, w_query, w_key, w_value, w_out
        )
    positions, width = tokens.shape[1] * tokens.shape[2], tokens.shape[3]
    heads_width = w_query.shape[1]
    split = heads_width // 2
    rows = width // (dp_count * seq_count)
    z_count = seq_count // 4
    stored_row_mask = jnp.transpose(row_mask, (1, 2, 3, 0))
    stored_column_mask = jnp.transpose(column_mask, (0, 2, 3, 1))
    lead = (8, dp_count, z_count, 2)
    lanes = split // 2
    call = pl.pallas_call(
        lambda *refs: fused_kernel(dp_count, seq_count, *refs),
        out_shape=(
            jax.ShapeDtypeStruct((positions, width), BF16),
            jax.ShapeDtypeStruct((positions, width), BF16),
            jax.ShapeDtypeStruct((rows, heads_width), F32),
            jax.ShapeDtypeStruct((rows, heads_width), F32),
        ),
        in_specs=[pl.BlockSpec(memory_space=pltpu.HBM)] * 8,
        out_specs=[pl.BlockSpec(memory_space=pltpu.HBM)] * 4,
        scratch_shapes=[
            pltpu.VMEM((positions, width), BF16),
            pltpu.VMEM((positions, width), BF16),
            pltpu.VMEM((width, positions), BF16),
            pltpu.VMEM((width, positions), BF16),
            pltpu.SMEM(stored_row_mask.shape, jnp.int32),
            pltpu.SMEM(stored_column_mask.shape, jnp.int32),
            pltpu.VMEM((4, positions, positions), F32),
            pltpu.VMEM((positions, positions), BF16),
            pltpu.VMEM((positions, width), BF16),
            pltpu.VMEM((positions, width), BF16),
            pltpu.VMEM((rows, heads_width), F32),
            pltpu.VMEM((rows, heads_width), F32),
            pltpu.VMEM((positions, width), F32),
            pltpu.VMEM((3, width, heads_width), BF16),
            pltpu.VMEM((heads_width, width), BF16),
            pltpu.VMEM((3, positions, split), BF16),
            pltpu.VMEM((3, positions, split), BF16),
            pltpu.VMEM((positions, split), BF16),
            pltpu.VMEM((1, positions, split), BF16),
            pltpu.VMEM((1, positions, split), BF16),
            pltpu.VMEM((1, positions, split), BF16),
            pltpu.VMEM((1, positions, split), BF16),
            pltpu.VMEM((3, positions, split), BF16),
            pltpu.VMEM((3, positions, split), BF16),
            pltpu.VMEM((3, positions, split), BF16),
            pltpu.VMEM((3, positions, split), BF16),
            pltpu.VMEM((heads_width // HEAD_DIM, positions, positions), F32),
            pltpu.VMEM((positions, heads_width), BF16),
            pltpu.VMEM(lead + (2, rows, lanes), BF16),
            pltpu.VMEM(lead + (rows, lanes), BF16),
            pltpu.VMEM(lead + (rows, lanes), BF16),
            pltpu.VMEM((4, z_count, 2, rows, lanes), BF16),
            pltpu.VMEM((4, 2, z_count, rows, lanes), BF16),
            pltpu.VMEM((4, z_count, 2, rows, lanes), BF16),
            pltpu.VMEM((4, 2, z_count, rows, lanes), BF16),
            pltpu.VMEM((8, z_count, rows, lanes), BF16),
            pltpu.VMEM((8, z_count, rows, lanes), BF16),
            pltpu.VMEM((8, z_count - 1, rows, lanes), BF16),
            pltpu.SemaphoreType.DMA((6, 4)),
            pltpu.SemaphoreType.DMA((6, 4)),
            pltpu.SemaphoreType.DMA((7,)),
            pltpu.SemaphoreType.DMA((7,)),
            pltpu.SemaphoreType.DMA((8, 2 + z_count)),
            pltpu.SemaphoreType.DMA((8, 2 + z_count)),
            pltpu.SemaphoreType.DMA((12,)),
        ],
        compiler_params=pltpu.CompilerParams(
            collective_id=0, has_side_effects=True, vmem_limit_bytes=64 * 1024 * 1024 - 65536
        ),
        cost_estimate=pl.CostEstimate(
            flops=3_400_000_000, bytes_accessed=8_000_000, transcendentals=524288
        ),
    )
    mixed, grad_tokens, grad_value, grad_output = call(
        tokens.reshape(positions, width),
        cotangent.reshape(positions, width),
        stored_row_mask,
        stored_column_mask,
        w_query,
        w_key,
        w_value,
        w_out,
    )
    mixed, grad_tokens, grad_value, grad_output = hand_out(
        mixed, grad_tokens, grad_value, grad_output
    )
    return (
        mixed.reshape(tokens.shape),
        grad_tokens.reshape(tokens.shape),
        grad_value,
        jnp.transpose(grad_output),
    )


def solution(mesh):
    return jax.shard_map(
        fused_body,
        mesh=mesh,
        in_specs=(
            P("dp", "seq", None, None),
            P("dp", "seq", None, None),
            P(None, "seq", None, None),
            P(None, "seq", None, None),
            P("dp", None),
            P("dp", None),
            P("dp", None),
            P("dp", None),
        ),
        out_specs=(
            P("dp", "seq", None, None),
            P("dp", "seq", None, None),
            P(("dp", "seq"), None),
            P(None, ("dp", "seq")),
        ),
        check_vma=False,
    )
```

```python
import math

import jax
import jax.numpy as jnp
from jax import lax
from jax.experimental import pallas as pl
from jax.experimental.pallas import tpu as pltpu
from jax.sharding import PartitionSpec as P

HEAD_DIM = 64
ROWBLK = 128
COLBLK = 8


row_forms = ("blhe,bmhe->bhlm", "bhlm,bmhe->blhe")
column_forms = ("lbhe,mbhe->bhlm", "bhlm,mbhe->lbhe")
contract_last = (((1,), (1,)), ((), ()))
contract_first = (((0,), (0,)), ((), ()))


def allowed_cells(mask_blocks, block_size):
    expanded = jnp.repeat(jnp.repeat(mask_blocks, block_size, axis=-2), block_size, axis=-1)
    length = expanded.shape[-1]
    causal = jnp.arange(length)[:, None] >= jnp.arange(length)[None, :]
    return (expanded == 1) & causal


def attend(queries, key_part, value_part, allowed, forms):
    scale_factor = 1.0 / math.sqrt(queries.shape[-1])
    scores = (
        jnp.einsum(forms[0], queries.astype(jnp.float32), key_part.astype(jnp.float32))
        * scale_factor
    )
    scores = jnp.where(allowed, scores, -1e30)
    highest = lax.stop_gradient(jnp.max(scores, axis=-1, keepdims=True))
    weights = jnp.exp(scores - highest)
    weights = weights / jnp.sum(weights, axis=-1, keepdims=True)
    rounded = lax.optimization_barrier(weights.astype(jnp.bfloat16)).astype(jnp.float32)
    result = jnp.einsum(forms[1], rounded, value_part.astype(jnp.float32))
    return result.astype(jnp.bfloat16)


def body(tokens, cotangent, row_mask, column_mask, w_query, w_key, w_value, w_out):
    rows_here = tokens.shape[1]
    grid_cols = tokens.shape[2]
    width = tokens.shape[3]
    heads_width = w_query.shape[1]
    half = heads_width // HEAD_DIM // 2
    split = half * HEAD_DIM
    flat = tokens.reshape(-1, width)
    cot_flat = cotangent.reshape(-1, width)
    token_count = flat.shape[0]
    seq_count = lax.axis_size("seq")
    grid_rows = rows_here * seq_count
    cols_here = grid_cols // seq_count
    full_query, full_key, full_value, full_out = (
        lax.all_gather(w_query, "dp", axis=0, tiled=True),
        lax.all_gather(w_key, "dp", axis=0, tiled=True),
        lax.all_gather(w_value, "dp", axis=0, tiled=True),
        lax.all_gather(w_out, "dp", axis=0, tiled=True),
    )
    proj_query = jnp.dot(flat, full_query, preferred_element_type=jnp.float32)
    proj_key = jnp.dot(flat, full_key, preferred_element_type=jnp.float32)
    proj_value = jnp.dot(flat, full_value, preferred_element_type=jnp.float32)
    query_flat = proj_query.astype(jnp.bfloat16)
    key_flat = proj_key.astype(jnp.bfloat16)
    value_flat = proj_value.astype(jnp.bfloat16)
    row_allowed = allowed_cells(jnp.transpose(row_mask, (1, 0, 2, 3)), ROWBLK)
    column_allowed = allowed_cells(jnp.transpose(column_mask, (1, 0, 2, 3)), COLBLK)

    def row_core(first, second, third):
        return attend(first, second, third, row_allowed, row_forms)

    def column_core(first, second, third):
        return attend(first, second, third, column_allowed, column_forms)

    def row_heads(matrix):
        return matrix[:, :split].reshape(rows_here, grid_cols, half, HEAD_DIM)

    def column_heads(matrix):
        return matrix[:, split:].reshape(rows_here, grid_cols, split)

    def as_columns(block):
        return block.reshape(grid_rows, cols_here, half, HEAD_DIM)

    def joined(row_part, col_part):
        return jnp.concatenate(
            [row_part.reshape(token_count, split), col_part.reshape(token_count, split)], axis=1
        )

    col_query, col_key, col_value = (
        lax.all_to_all(column_heads(query_flat), "seq", split_axis=1, concat_axis=0, tiled=True),
        lax.all_to_all(column_heads(key_flat), "seq", split_axis=1, concat_axis=0, tiled=True),
        lax.all_to_all(column_heads(value_flat), "seq", split_axis=1, concat_axis=0, tiled=True),
    )
    row_out, row_back = jax.vjp(
        row_core, row_heads(query_flat), row_heads(key_flat), row_heads(value_flat)
    )
    column_out, column_back = jax.vjp(
        column_core, as_columns(col_query), as_columns(col_key), as_columns(col_value)
    )
    returned = lax.all_to_all(
        column_out.reshape(grid_rows, cols_here, split),
        "seq",
        split_axis=0,
        concat_axis=1,
        tiled=True,
    )
    attended = joined(row_out, returned)
    mixed = jnp.dot(attended, full_out, preferred_element_type=jnp.float32)
    grad_heads = lax.dot_general(
        cot_flat, full_out, contract_last, preferred_element_type=jnp.float32
    )
    mixed = mixed.astype(jnp.bfloat16).reshape(tokens.shape)
    grad_heads = grad_heads.astype(jnp.bfloat16)
    row_grads = row_back(grad_heads[:, :split].reshape(rows_here, grid_cols, half, HEAD_DIM))
    grad_columns = lax.all_to_all(
        grad_heads[:, split:].reshape(rows_here, grid_cols, split),
        "seq",
        split_axis=1,
        concat_axis=0,
        tiled=True,
    )
    col_grads = column_back(as_columns(grad_columns))
    back_grads = (
        lax.all_to_all(
            col_grads[0].reshape(grid_rows, cols_here, split),
            "seq",
            split_axis=0,
            concat_axis=1,
            tiled=True,
        ),
        lax.all_to_all(
            col_grads[1].reshape(grid_rows, cols_here, split),
            "seq",
            split_axis=0,
            concat_axis=1,
            tiled=True,
        ),
        lax.all_to_all(
            col_grads[2].reshape(grid_rows, cols_here, split),
            "seq",
            split_axis=0,
            concat_axis=1,
            tiled=True,
        ),
    )
    grad_query = joined(row_grads[0], back_grads[0])
    grad_key = joined(row_grads[1], back_grads[1])
    grad_val = joined(row_grads[2], back_grads[2])
    grad_tokens = (
        lax.dot_general(grad_query, full_query, contract_last, preferred_element_type=jnp.float32)
        + lax.dot_general(grad_key, full_key, contract_last, preferred_element_type=jnp.float32)
        + lax.dot_general(grad_val, full_value, contract_last, preferred_element_type=jnp.float32)
    )
    grad_tokens = grad_tokens.astype(jnp.bfloat16).reshape(tokens.shape)
    summed = lax.psum_scatter(
        jnp.concatenate(
            [
                lax.dot_general(flat, grad_val, contract_first, preferred_element_type=jnp.float32),
                lax.dot_general(
                    cot_flat, attended, contract_first, preferred_element_type=jnp.float32
                ),
            ],
            axis=1,
        ),
        ("dp", "seq"),
        scatter_dimension=0,
        tiled=True,
    )
    grad_value = summed[:, :heads_width]
    grad_output = jnp.transpose(summed[:, heads_width:])
    return (mixed, grad_tokens, grad_value, grad_output)


MESH = pl.DeviceIdType.MESH
F32 = jnp.float32
BF16 = jnp.bfloat16


def dot_nn(a, b):
    return jnp.dot(a, b, preferred_element_type=F32)


def dot_nt(a, b):
    return lax.dot_general(a, b, contract_last, preferred_element_type=F32)


def fused_kernel(
    dp_count,
    seq_count,
    tokens_hbm,
    cot_hbm,
    row_mask_hbm,
    column_mask_hbm,
    wq_hbm,
    wk_hbm,
    wv_hbm,
    wo_hbm,
    mixed_hbm,
    gtok_hbm,
    gval_hbm,
    gout_hbm,
    tokens_ref,
    cot_ref,
    tokens_t,
    cot_t,
    row_mask_ref,
    column_mask_ref,
    bias,
    unit,
    mixed_ref,
    gtok_ref,
    gval_ref,
    gout_ref,
    gtok_part,
    w_full,
    wo_full,
    qkv_send,
    qkv_recv,
    g_rows,
    g_send,
    g_recv,
    out_send,
    out_recv,
    grad_send,
    grad_recv,
    row_qkv,
    row_grads,
    probs,
    attended,
    part,
    part_recv1,
    acc1,
    recv_x_first,
    recv_y_first,
    acc_x_first,
    acc_y_first,
    part_recv3,
    acc3,
    part_recv4,
    w_send_sem,
    w_recv_sem,
    a_send_sem,
    a_recv_sem,
    r_send_sem,
    r_recv_sem,
    local_sem,
):
    dp = lax.axis_index("dp")
    seq = lax.axis_index("seq")
    core = lax.rem(seq, 2)
    y = lax.rem(seq // 2, 2)
    z = seq // 4
    z_count = seq_count // 4
    positions = tokens_ref.shape[0]
    cols = positions // seq_count
    shard = wq_hbm.shape[0]
    out_shard = wo_hbm.shape[0]
    split = qkv_send.shape[2]
    half = split // HEAD_DIM
    other = 1 - dp
    x_peer = (other, seq)
    core_peer = (dp, seq + 1 - 2 * core)
    y_peer = (dp, seq + 2 - 4 * y)

    own_rows = pl.ds(pl.multiple_of(dp * shard, shard), shard)
    own_out = pl.ds(pl.multiple_of(dp * out_shard, out_shard), out_shard)
    weights_in = [
        pltpu.make_async_copy(wq_hbm, w_full.at[0, own_rows, :], local_sem.at[0]),
        pltpu.make_async_copy(wk_hbm, w_full.at[1, own_rows, :], local_sem.at[1]),
        pltpu.make_async_copy(wv_hbm, w_full.at[2, own_rows, :], local_sem.at[2]),
        pltpu.make_async_copy(wo_hbm, wo_full.at[own_out, :], local_sem.at[3]),
    ]
    others_in = [
        pltpu.make_async_copy(tokens_hbm, tokens_ref, local_sem.at[4]),
        pltpu.make_async_copy(cot_hbm, cot_ref, local_sem.at[5]),
        pltpu.make_async_copy(row_mask_hbm, row_mask_ref, local_sem.at[6]),
        pltpu.make_async_copy(column_mask_hbm, column_mask_ref, local_sem.at[7]),
    ]
    outs = [
        pltpu.make_async_copy(mixed_ref, mixed_hbm, local_sem.at[8]),
        pltpu.make_async_copy(gtok_ref, gtok_hbm, local_sem.at[9]),
        pltpu.make_async_copy(gval_ref, gval_hbm, local_sem.at[10]),
        pltpu.make_async_copy(gout_ref, gout_hbm, local_sem.at[11]),
    ]
    for copy in weights_in + others_in:
        copy.start()

    barrier = pltpu.get_barrier_semaphore()
    pl.semaphore_signal(barrier, inc=1, device_id=x_peer, device_id_type=MESH)

    @pl.loop(1, seq_count, unroll=True)
    def _(step):
        pl.semaphore_signal(
            barrier,
            inc=1,
            device_id=(dp, lax.rem(seq + step, seq_count)),
            device_id_type=MESH,
        )

    def store_bias(index, seen):
        bias[index] = jnp.where(seen, 0.0, -1e30)

    query_pos = lax.broadcasted_iota(jnp.int32, (positions, positions), 0)
    key_pos = lax.broadcasted_iota(jnp.int32, (positions, positions), 1)
    differ = query_pos ^ key_pos
    causal = key_pos <= query_pos
    matching = causal & ((differ & (cols - 1)) == 0)
    store_bias(0, causal)
    store_bias(1, causal & (differ < ROWBLK))
    store_bias(2, matching)
    store_bias(3, matching & (differ < COLBLK * cols))
    unit[...] = jnp.where(differ == 0, 1.0, 0.0).astype(BF16)

    for copy in weights_in:
        copy.wait()
    pl.semaphore_wait(barrier, seq_count)

    def region(group, owner, qy, qc):
        if group == 3:
            quarter = out_shard // 4
            start = pl.multiple_of(owner * out_shard + (qy * 2 + qc) * quarter, quarter)
            return wo_full.at[pl.ds(start, quarter), :]
        quarter = shard // 4
        start = pl.multiple_of(owner * shard + (qy * 2 + qc) * quarter, quarter)
        if group == 4:
            return w_full.at[:, pl.ds(start, quarter), pl.ds(0, split)]
        return w_full.at[group, pl.ds(start, quarter), pl.ds(split, split)]

    def weight_copy(group, hop):
        if hop == 0:
            ref, peer = region(group, dp, y, core), x_peer
        elif hop == 1:
            ref, peer = region(group, other, y, core), y_peer
        elif hop == 2:
            ref, peer = region(group, other, y, core), core_peer
        else:
            ref, peer = region(group, other, 1 - y, core), core_peer
        return pltpu.make_async_remote_copy(
            src_ref=ref,
            dst_ref=ref,
            send_sem=w_send_sem.at[group, hop],
            recv_sem=w_recv_sem.at[group, hop],
            device_id=peer,
            device_id_type=MESH,
        )

    def pass_on(group):
        weight_copy(group, 0).wait_recv()
        if group + 2 < 5:
            weight_copy(group + 2, 0).start()
        weight_copy(group, 1).start()
        weight_copy(group, 2).start()

    def pass_core(group):
        weight_copy(group, 1).wait_recv()
        weight_copy(group, 3).start()

    def weights_here(group):
        weight_copy(group, 2).wait_recv()
        weight_copy(group, 3).wait_recv()

    def column_copy(src, dst, phase, step):
        target = lax.rem(seq + step, seq_count)
        there = pl.ds(pl.multiple_of(target * cols, cols), cols)
        here = pl.ds(pl.multiple_of(seq * cols, cols), cols)
        return pltpu.make_async_remote_copy(
            src_ref=src.at[:, there, :],
            dst_ref=dst.at[:, here, :],
            send_sem=a_send_sem.at[phase],
            recv_sem=a_recv_sem.at[phase],
            device_id=(dp, target),
            device_id_type=MESH,
        )

    def one(ref, index):
        return ref.at[pl.ds(index, 1)]

    def exchange(src, dst, phase):
        @pl.loop(1, seq_count, unroll=True)
        def _(step):
            column_copy(src, dst, phase, step).start()

        here = pl.ds(pl.multiple_of(seq * cols, cols), cols)
        dst[:, here, :] = src[:, here, :]

    def whole_exchange(src, dst, phase):
        many = pl.ds(0, positions - cols)
        return pltpu.make_async_remote_copy(
            src_ref=src.at[:, many, :],
            dst_ref=dst.at[:, many, :],
            send_sem=a_send_sem.at[phase],
            recv_sem=a_recv_sem.at[phase],
            device_id=core_peer,
            device_id_type=MESH,
        )

    def arrived(src, dst, phase):
        whole_exchange(src, dst, phase).wait_recv()

    def sent(src, dst, phase):
        whole_exchange(src, dst, phase).wait_send()

    weight_copy(0, 0).start()
    weight_copy(1, 0).start()

    lane = lax.broadcasted_iota(jnp.int32, (1, 2 * HEAD_DIM), 1)
    first_lanes = lane < HEAD_DIM
    keep = (first_lanes.astype(F32).astype(BF16), (lane >= HEAD_DIM).astype(F32).astype(BF16))

    for copy in others_in:
        copy.wait()
    for first in range(0, tokens_ref.shape[1], positions):
        block = slice(first, first + positions)
        tokens_t[block, :] = dot_nt(unit[...], tokens_ref[:, block]).astype(BF16)
        cot_t[block, :] = dot_nt(unit[...], cot_ref[:, block]).astype(BF16)

    def head_bias(head):
        if head < half:
            bit = row_mask_ref[0, 1, 0, head]
            return jnp.where(bit == 1, bias[0], bias[1])
        column = lax.rem(lax.broadcasted_iota(jnp.int32, (1, positions), 1), cols)
        bits = jnp.zeros((1, positions), jnp.int32)
        for index in range(cols):
            bits = jnp.where(column == index, column_mask_ref[head - half, 1, 0, index], bits)
        return jnp.where(bits == 1, bias[2], bias[3])

    def softmax(head, query, key):
        scores = dot_nt(query, key) * (1.0 / math.sqrt(HEAD_DIM)) + head_bias(head)
        weights = jnp.exp(scores - jnp.max(scores, axis=-1, keepdims=True))
        return weights * (1.0 / jnp.sum(weights, axis=-1, keepdims=True))

    def pair_of(pair):
        return pl.ds(pair * 2 * HEAD_DIM, 2 * HEAD_DIM)

    def merge(halves):
        return jnp.where(first_lanes, halves[0], halves[1]).astype(BF16)

    def forward(base, query, key, value, slot):
        outs = []
        for side in range(2):
            weights = softmax(base + side, query * keep[side], key)
            probs[slot + side] = weights
            outs.append(dot_nn(weights.astype(BF16), value))
        return merge(outs)

    def turned(square):
        return dot_nt(unit[...], square).astype(BF16)

    def value_grad(grad, slot):
        sides = [dot_nn(turned(probs[slot + side].astype(BF16)), grad) for side in range(2)]
        return merge(sides)

    def query_key_grads(query, key, value, grad, slot):
        grads = ([], [])
        for side in range(2):
            weights = probs[slot + side]
            grad_probs = dot_nt(grad * keep[side], value)
            grad_scores = weights * (
                grad_probs - jnp.sum(weights * grad_probs, axis=-1, keepdims=True)
            )
            grad_scores = (grad_scores * (1.0 / math.sqrt(HEAD_DIM))).astype(BF16)
            grads[0].append(dot_nn(grad_scores, key))
            grads[1].append(dot_nn(turned(grad_scores), query))
        return [merge(grad_pair) for grad_pair in grads]

    def rs_copy(which, hop):
        piece, order = which // 2, which % 2
        if hop == 0:
            src, dst, peer = part.at[which, :, :, :, 1 - core], part_recv1.at[which], core_peer
        elif hop == 1 and order == 0:
            src, dst, peer = acc1.at[which, other], recv_x_first.at[piece], x_peer
        elif hop == 1:
            src, dst, peer = acc1.at[which, :, :, 1 - y], recv_y_first.at[piece], y_peer
        elif hop == 2 and order == 0:
            src, dst, peer = acc_x_first.at[piece, :, 1 - y], part_recv3.at[which], y_peer
        elif hop == 2:
            src, dst, peer = acc_y_first.at[piece, other], part_recv3.at[which], x_peer
        else:
            z_there = lax.rem(z + hop - 2, z_count)
            src, dst = acc3.at[which, z_there], part_recv4.at[which, hop - 3]
            peer = (dp, z_there * 4 + y * 2 + core)
        return pltpu.make_async_remote_copy(
            src_ref=src,
            dst_ref=dst,
            send_sem=r_send_sem.at[which, hop],
            recv_sem=r_recv_sem.at[which, hop],
            device_id=peer,
            device_id_type=MESH,
        )

    def rs_start(piece, full):
        lanes = split // 2
        for order in range(2):
            half_piece = full[:, order * lanes : (order + 1) * lanes].astype(BF16)
            part[2 * piece + order] = half_piece.reshape(part.shape[1:])
            rs_copy(2 * piece + order, 0).start()

    def rs_next(piece, hop):
        for order in range(2):
            which = 2 * piece + order
            rs_copy(which, hop).wait_recv()
            if hop == 0:
                acc1[which] = (
                    part[which, :, :, :, core].astype(F32) + part_recv1[which].astype(F32)
                ).astype(BF16)
            elif hop == 1 and order == 0:
                acc_x_first[piece] = (
                    acc1[which, dp].astype(F32) + recv_x_first[piece].astype(F32)
                ).astype(BF16)
            elif hop == 1:
                acc_y_first[piece] = (
                    acc1[which, :, :, y].astype(F32) + recv_y_first[piece].astype(F32)
                ).astype(BF16)
            elif order == 0:
                acc3[which] = (
                    acc_x_first[piece, :, y].astype(F32) + part_recv3[which].astype(F32)
                ).astype(BF16)
            else:
                acc3[which] = (
                    acc_y_first[piece, dp].astype(F32) + part_recv3[which].astype(F32)
                ).astype(BF16)
            if hop < 2:
                rs_copy(which, hop + 1).start()
            else:
                for step in range(1, z_count):
                    rs_copy(which, 2 + step).start()

    def rs_end(piece, out, first_lane):
        for order in range(2):
            which = 2 * piece + order
            total = acc3[which, z].astype(F32)
            for step in range(1, z_count):
                rs_copy(which, 2 + step).wait_recv()
                total = total + part_recv4[which, step - 1].astype(F32)
            out[:, pl.ds(first_lane + order * (split // 2), split // 2)] = total

    def project_columns(index):
        weights_here(index)
        qkv_send[index] = dot_nn(tokens_ref[...], w_full[index, :, split:]).astype(BF16)
        exchange(one(qkv_send, index), one(qkv_recv, index), index)

    pass_on(0)
    pass_on(1)
    pass_core(0)
    pass_on(2)
    project_columns(0)
    pass_core(1)
    project_columns(1)
    pass_core(2)
    pass_on(3)
    project_columns(2)
    pass_core(3)
    pass_on(4)
    weights_here(3)
    g_send[0] = dot_nt(cot_ref[...], wo_full[split:, :]).astype(BF16)
    exchange(g_send, g_recv, 3)
    g_rows[...] = dot_nt(cot_ref[...], wo_full[:split, :]).astype(BF16)
    for index in range(3):
        arrived(one(qkv_send, index), one(qkv_recv, index), index)
    for pair in range(split // (2 * HEAD_DIM)):
        query, key, value = (qkv_recv[index, :, pair_of(pair)] for index in range(3))
        out_send[0, :, pair_of(pair)] = forward(half + 2 * pair, query, key, value, 2 * pair)
    exchange(out_send, out_recv, 4)
    pass_core(4)

    arrived(g_send, g_recv, 3)
    pairs = range(split // (2 * HEAD_DIM))
    for pair in pairs:
        grad_send[2, :, pair_of(pair)] = value_grad(g_recv[0, :, pair_of(pair)], 2 * pair)
    exchange(one(grad_send, 2), one(grad_recv, 2), 5)
    for pair in pairs:
        query, key, value = (qkv_recv[index, :, pair_of(pair)] for index in range(3))
        grads = query_key_grads(query, key, value, g_recv[0, :, pair_of(pair)], 2 * pair)
        for index in range(2):
            grad_send[index, :, pair_of(pair)] = grads[index]
    exchange(grad_send.at[pl.ds(0, 2)], grad_recv.at[pl.ds(0, 2)], 6)

    weights_here(4)
    for index in range(3):
        row_qkv[index] = dot_nn(tokens_ref[...], w_full[index, :, :split]).astype(BF16)
    for pair in pairs:
        query, key, value = (row_qkv[index, :, pair_of(pair)] for index in range(3))
        slot = half + 2 * pair
        attended[:, pair_of(pair)] = forward(2 * pair, query, key, value, slot)
        row_grads[2, :, pair_of(pair)] = value_grad(g_rows[:, pair_of(pair)], slot)
    rs_start(0, dot_nn(cot_t[...], attended[:, :split]))
    rs_start(1, dot_nn(tokens_t[...], row_grads[2]))
    arrived(out_send, out_recv, 4)
    rs_start(2, dot_nn(cot_t[...], out_recv[0]))
    rs_next(0, 0)
    arrived(one(grad_send, 2), one(grad_recv, 2), 5)
    rs_start(3, dot_nn(tokens_t[...], grad_recv[2]))
    rs_next(1, 0)

    def row_query_key(pair):
        query, key, value = (row_qkv[index, :, pair_of(pair)] for index in range(3))
        grads = query_key_grads(query, key, value, g_rows[:, pair_of(pair)], half + 2 * pair)
        for index in range(2):
            row_grads[index, :, pair_of(pair)] = grads[index]

    for pair in pairs:
        row_query_key(pair)
        if pair == 0:
            rs_next(2, 0)
            rs_next(3, 0)
    rs_next(0, 1)
    rs_next(1, 1)
    attended[:, pl.ds(split, split)] = out_recv[0]
    mixed_ref[...] = dot_nn(attended[...], wo_full[...]).astype(BF16)
    outs[0].start()
    rs_next(2, 1)
    gtok_part[...] = (
        dot_nt(row_grads[0], w_full[0, :, :split])
        + dot_nt(row_grads[1], w_full[1, :, :split])
        + dot_nt(row_grads[2], w_full[2, :, :split])
    )
    rs_next(3, 1)
    rs_next(0, 2)
    rs_next(1, 2)
    arrived(grad_send.at[pl.ds(0, 2)], grad_recv.at[pl.ds(0, 2)], 6)
    gtok_ref[...] = (
        gtok_part[...]
        + dot_nt(grad_recv[0], w_full[0, :, split:])
        + dot_nt(grad_recv[1], w_full[1, :, split:])
        + dot_nt(grad_recv[2], w_full[2, :, split:])
    ).astype(BF16)
    outs[1].start()
    rs_next(2, 2)
    rs_next(3, 2)
    for group in range(5):
        for hop in range(4):
            weight_copy(group, hop).wait_send()
    for index in range(3):
        sent(one(qkv_send, index), one(qkv_recv, index), index)
    sent(g_send, g_recv, 3)
    sent(out_send, out_recv, 4)
    sent(one(grad_send, 2), one(grad_recv, 2), 5)
    sent(grad_send.at[pl.ds(0, 2)], grad_recv.at[pl.ds(0, 2)], 6)
    rs_end(0, gout_ref, 0)
    rs_end(2, gout_ref, split)
    outs[3].start()
    rs_end(1, gval_ref, 0)
    rs_end(3, gval_ref, split)
    outs[2].start()
    for which in range(8):
        for hop in range(2 + z_count):
            rs_copy(which, hop).wait_send()
    for copy in outs:
        copy.wait()


def hand_out_kernel(*refs):
    count = (len(refs) - 2) // 3
    ins, outs, held = refs[:count], refs[count : 2 * count], refs[2 * count : 3 * count]
    in_sems, out_sems = refs[-2:]
    fetches = [
        pltpu.make_async_copy(ins[index], held[index], in_sems.at[index]) for index in range(count)
    ]
    stores = [
        pltpu.make_async_copy(held[index], outs[index], out_sems.at[index])
        for index in range(count)
    ]
    for copy in fetches:
        copy.start()
    for index in range(count):
        fetches[index].wait()
        stores[index].start()
    for copy in stores:
        copy.wait()


def hand_out(*arrays):
    count = len(arrays)
    return pl.pallas_call(
        hand_out_kernel,
        out_shape=[jax.ShapeDtypeStruct(item.shape, item.dtype) for item in arrays],
        in_specs=[pl.BlockSpec(memory_space=pltpu.HBM)] * count,
        out_specs=[pl.BlockSpec(memory_space=pltpu.HBM)] * count,
        scratch_shapes=[pltpu.VMEM(item.shape, item.dtype) for item in arrays]
        + [pltpu.SemaphoreType.DMA((count,)), pltpu.SemaphoreType.DMA((count,))],
        compiler_params=pltpu.CompilerParams(vmem_limit_bytes=64 * 1024 * 1024 - 65536),
    )(*arrays)


def fused_fits(dp_count, seq_count, tokens, row_mask, column_mask, w_query, w_out):
    positions = tokens.shape[1] * tokens.shape[2]
    return (
        tokens.shape[0] == 1
        and tokens.shape[1] == 1
        and dp_count == 2
        and seq_count % 4 == 0
        and positions % (16 * seq_count) == 0
        and w_query.shape[0] % 64 == 0
        and w_query.shape[1] % 512 == 0
        and w_out.shape[1] % 256 == 0
        and tokens.shape[3] % positions == 0
        and positions % 128 == 0
        and positions & (positions - 1) == 0
        and seq_count & (seq_count - 1) == 0
        and w_out.shape[0] % 64 == 0
        and tokens.shape[3] % (16 * dp_count * seq_count) == 0
        and row_mask.shape[2] == 2
        and column_mask.shape[2] == 2
    )


def fused_body(tokens, cotangent, row_mask, column_mask, w_query, w_key, w_value, w_out):
    dp_count, seq_count = lax.axis_size("dp"), lax.axis_size("seq")
    if not fused_fits(dp_count, seq_count, tokens, row_mask, column_mask, w_query, w_out):
        return body(
            tokens, cotangent, row_mask, column_mask, w_query, w_key, w_value, w_out
        )
    positions, width = tokens.shape[1] * tokens.shape[2], tokens.shape[3]
    heads_width = w_query.shape[1]
    split = heads_width // 2
    rows = width // (dp_count * seq_count)
    z_count = seq_count // 4
    stored_row_mask = jnp.transpose(row_mask, (1, 2, 3, 0))
    stored_column_mask = jnp.transpose(column_mask, (0, 2, 3, 1))
    lead = (8, dp_count, z_count, 2)
    lanes = split // 2
    call = pl.pallas_call(
        lambda *refs: fused_kernel(dp_count, seq_count, *refs),
        out_shape=(
            jax.ShapeDtypeStruct((positions, width), BF16),
            jax.ShapeDtypeStruct((positions, width), BF16),
            jax.ShapeDtypeStruct((rows, heads_width), F32),
            jax.ShapeDtypeStruct((rows, heads_width), F32),
        ),
        in_specs=[pl.BlockSpec(memory_space=pltpu.HBM)] * 8,
        out_specs=[pl.BlockSpec(memory_space=pltpu.HBM)] * 4,
        scratch_shapes=[
            pltpu.VMEM((positions, width), BF16),
            pltpu.VMEM((positions, width), BF16),
            pltpu.VMEM((width, positions), BF16),
            pltpu.VMEM((width, positions), BF16),
            pltpu.SMEM(stored_row_mask.shape, jnp.int32),
            pltpu.SMEM(stored_column_mask.shape, jnp.int32),
            pltpu.VMEM((4, positions, positions), F32),
            pltpu.VMEM((positions, positions), BF16),
            pltpu.VMEM((positions, width), BF16),
            pltpu.VMEM((positions, width), BF16),
            pltpu.VMEM((rows, heads_width), F32),
            pltpu.VMEM((rows, heads_width), F32),
            pltpu.VMEM((positions, width), F32),
            pltpu.VMEM((3, width, heads_width), BF16),
            pltpu.VMEM((heads_width, width), BF16),
            pltpu.VMEM((3, positions, split), BF16),
            pltpu.VMEM((3, positions, split), BF16),
            pltpu.VMEM((positions, split), BF16),
            pltpu.VMEM((1, positions, split), BF16),
            pltpu.VMEM((1, positions, split), BF16),
            pltpu.VMEM((1, positions, split), BF16),
            pltpu.VMEM((1, positions, split), BF16),
            pltpu.VMEM((3, positions, split), BF16),
            pltpu.VMEM((3, positions, split), BF16),
            pltpu.VMEM((3, positions, split), BF16),
            pltpu.VMEM((3, positions, split), BF16),
            pltpu.VMEM((heads_width // HEAD_DIM, positions, positions), F32),
            pltpu.VMEM((positions, heads_width), BF16),
            pltpu.VMEM(lead + (2, rows, lanes), BF16),
            pltpu.VMEM(lead + (rows, lanes), BF16),
            pltpu.VMEM(lead + (rows, lanes), BF16),
            pltpu.VMEM((4, z_count, 2, rows, lanes), BF16),
            pltpu.VMEM((4, 2, z_count, rows, lanes), BF16),
            pltpu.VMEM((4, z_count, 2, rows, lanes), BF16),
            pltpu.VMEM((4, 2, z_count, rows, lanes), BF16),
            pltpu.VMEM((8, z_count, rows, lanes), BF16),
            pltpu.VMEM((8, z_count, rows, lanes), BF16),
            pltpu.VMEM((8, z_count - 1, rows, lanes), BF16),
            pltpu.SemaphoreType.DMA((5, 4)),
            pltpu.SemaphoreType.DMA((5, 4)),
            pltpu.SemaphoreType.DMA((7,)),
            pltpu.SemaphoreType.DMA((7,)),
            pltpu.SemaphoreType.DMA((8, 2 + z_count)),
            pltpu.SemaphoreType.DMA((8, 2 + z_count)),
            pltpu.SemaphoreType.DMA((12,)),
        ],
        compiler_params=pltpu.CompilerParams(
            collective_id=0, has_side_effects=True, vmem_limit_bytes=64 * 1024 * 1024 - 65536
        ),
        cost_estimate=pl.CostEstimate(
            flops=3_400_000_000, bytes_accessed=8_000_000, transcendentals=524288
        ),
    )
    mixed, grad_tokens, grad_value, grad_output = call(
        tokens.reshape(positions, width),
        cotangent.reshape(positions, width),
        stored_row_mask,
        stored_column_mask,
        w_query,
        w_key,
        w_value,
        w_out,
    )
    mixed, grad_tokens, grad_value, grad_output = hand_out(
        mixed, grad_tokens, grad_value, grad_output
    )
    return (
        mixed.reshape(tokens.shape),
        grad_tokens.reshape(tokens.shape),
        grad_value,
        jnp.transpose(grad_output),
    )


def solution(mesh):
    return jax.shard_map(
        fused_body,
        mesh=mesh,
        in_specs=(
            P("dp", "seq", None, None),
            P("dp", "seq", None, None),
            P(None, "seq", None, None),
            P(None, "seq", None, None),
            P("dp", None),
            P("dp", None),
            P("dp", None),
            P("dp", None),
        ),
        out_specs=(
            P("dp", "seq", None, None),
            P("dp", "seq", None, None),
            P(("dp", "seq"), None),
            P(None, ("dp", "seq")),
        ),
        check_vma=False,
    )
```
